32 devices in a mesh: section: 4 (over x, core), seq: 4 (over z), shard: 2 (over y).
Axes of the slice: x: 2, y: 2, z: 4, core: 2. Of those that a mesh axis runs over, the one named last changes fastest.
Arguments:
- frames: bfloat16 [2, 1536, 768], P(None, ('seq', 'shard')), may hold values from -6 to 6
- out_grad: bfloat16 [2, 1536, 768], P(None, ('seq', 'shard')), may hold values from -6 to 6
- norm_gain: bfloat16 [4, 2, 768], P('section', None, 'shard'), may hold values from 0.5 to 1.5
- norm_bias: bfloat16 [4, 2, 768], P('section', None, 'shard'), may hold values from -3 to 3
- w_qkv: bfloat16 [4, 768, 2304], P('section', 'shard'), may hold values from -0.20412415 to 0.20412415, as said below
- w_out: bfloat16 [4, 768, 768], P('section', 'shard'), may hold values from -0.4375 to 0.4375
- w_up: bfloat16 [4, 768, 3072], P('section', 'shard'), may hold values from -0.21875 to 0.21875
- w_down: bfloat16 [4, 3072, 768], P('section', 'shard'), may hold values from -0.109375 to 0.109375
- proj_bias: bfloat16 [4, 4, 768], P('section', None, 'shard'), may hold values from -1.5 to 1.5, as said below
- up_bias: bfloat16 [4, 3072], P('section', 'shard'), may hold values from -3 to 3
Outputs:
- hidden_states: bfloat16 [4, 2, 1536, 768], P('section', None, ('seq', 'shard'))
- input_grads: bfloat16 [4, 2, 1536, 768], P('section', None, ('seq', 'shard'))
- grad_norm_gain: float32 [4, 2, 768], P('section', None, 'shard')
- grad_norm_bias: float32 [4, 2, 768], P('section', None, 'shard')
- grad_qkv: float32 [4, 768, 2304], P('section', 'shard')
- grad_out: float32 [4, 768, 768], P('section', 'shard')
- grad_up: float32 [4, 768, 3072], P('section', 'shard')
- grad_down: float32 [4, 3072, 768], P('section', 'shard')
- grad_proj_bias: float32 [4, 4, 768], P('section', None, 'shard')
- grad_up_bias: float32 [4, 3072], P('section', 'shard')
The draws below stay inside these ranges and needn't reach their ends.
Inputs may be any that keep to these rules, and one draw needn't show every extreme that they name: `w_qkv`: independent entries of mean 0. `proj_bias`: independent entries of mean 0.
All inputs are finite; a program needn't handle non-finite values.
Results may differ from the reference program's by a relative error of at most 0.02.
Values may be sent and summed in bfloat16 or wider, within the bound.
No kernel may reach another device: no remote copies, remote signals or barrier semaphores. Data moves between devices by JAX's collectives and lax.ppermute only.
A program may use at most 192 MiB of HBM per device.

```python
import math
from functools import partial
import jax
import jax.numpy as jnp
from jax import lax

D = 768
HEADS = 12
FF = 3072
HEAD = 64
LENGTH = 1536
MICRO = 2
SECTIONS = 4


def draw_w_qkv(key, part):
    key = jax.random.fold_in(key, 11)
    values = jnp.clip(jax.random.normal(key, (SECTIONS, D, 3 * D), jnp.float32), -4.0, 4.0)
    return (values * (2.0 / D) ** 0.5).astype(jnp.bfloat16)


def draw_proj_bias(key, part):
    key = jax.random.fold_in(key, 23)
    values = jnp.clip(jax.random.normal(key, (SECTIONS, 4, D), jnp.float32), -3.0, 3.0)
    return (values * 0.5).astype(jnp.bfloat16)


def block_levels(stream_key, dims, cuts, low, largest):
    level, own = 1.0, jax.random.fold_in(stream_key, 6)
    for axis_at, shards_of in cuts:
        draws = jnp.exp(jax.random.uniform(jax.random.fold_in(own, axis_at), (shards_of,), jnp.float32, low / len(cuts), largest / len(cuts)))
        level = level * jnp.repeat(draws, dims[axis_at] // shards_of).reshape([-1 if axis == axis_at else 1 for axis in range(len(dims))])
    return level


def normal_values(key, dims, spread, limit, split=(), dtype=jnp.bfloat16):
    values = jax.random.normal(key, dims, jnp.float32) * spread
    if len(split) > 0:
        values = block_levels(key, dims, split, -0.22, 0.18) * values
    return jnp.clip(values, min=-limit, max=limit).astype(dtype)


def setup_inputs(seed: int = 0) -> dict:
    arg_keys = jax.random.split(jax.random.key(seed), 11)
    return {
        "frames": normal_values(arg_keys[0], (MICRO, LENGTH, D), 1.0, 6.0, ((1, 8),)),
        "out_grad": normal_values(arg_keys[1], (MICRO, LENGTH, D), 1.0, 6.0, ((1, 8),)),
        "norm_gain": jnp.clip(1.0 + 0.1 * jax.random.normal(arg_keys[2], (SECTIONS, 2, D), jnp.float32), 0.5, 1.5).astype(jnp.bfloat16),
        "norm_bias": normal_values(arg_keys[3], (SECTIONS, 2, D), 0.5, 3.0, ((0, 4), (2, 2))),
        "w_qkv": draw_w_qkv(jax.random.fold_in(arg_keys[10], 71), 0),
        "w_out": normal_values(arg_keys[5], (SECTIONS, D, D), (D // 4) ** -0.5, 0.4375, ((0, 4), (1, 2))),
        "w_up": normal_values(arg_keys[6], (SECTIONS, D, FF), D ** -0.5, 0.21875, ((0, 4), (1, 2))),
        "w_down": normal_values(arg_keys[7], (SECTIONS, FF, D), FF ** -0.5, 0.109375, ((0, 4), (1, 2))),
        "proj_bias": draw_proj_bias(jax.random.fold_in(arg_keys[10], 71), 0),
        "up_bias": normal_values(arg_keys[9], (SECTIONS, FF), 0.5, 3.0, ((0, 4), (1, 2))),
    }


@jax.custom_vjp
def low(v):
    return lax.optimization_barrier(v.astype(jnp.bfloat16)).astype(jnp.float32)

@jax.custom_vjp
def low_back(v):
    return v

def low_keep(v):
    return (low(v), None)

def low_pass(kept, grad):
    return (grad,)

def back_keep(v):
    return (v, None)

def back_low(kept, grad):
    return (low(grad),)
low.defvjp(low_keep, low_pass)
low_back.defvjp(back_keep, back_low)
norm_eps = 1e-05
highest_mode = lax.Precision.HIGHEST

def layer_norm(values, gain_row, bias_row):
    center = values - lax.optimization_barrier(jnp.mean(values, axis=-1, keepdims=True))
    scaled = center * lax.rsqrt(lax.optimization_barrier(jnp.mean(center * center, axis=-1, keepdims=True)) + norm_eps)
    return scaled * gain_row + bias_row

def attend_block(query_block, key_set, value_set):
    scores = jnp.einsum('qhe,khe->hqk', query_block, key_set, precision=highest_mode) / math.sqrt(HEAD)
    scores = low_back(scores)
    top_score = lax.optimization_barrier(jnp.max(scores, axis=-1, keepdims=True))
    exponent = jnp.exp(scores - top_score)
    attn_probs = low(exponent / lax.optimization_barrier(jnp.sum(exponent, axis=-1, keepdims=True)))
    return jnp.einsum('hqk,khe->qhe', attn_probs, value_set, precision=highest_mode)

def encoder_layer(inputs, params):
    norm_gains, shifts, mix_qkv, mix_out, mix_up, mix_down, proj_bias, up_bias = params
    length = inputs.shape[0]
    normed = low(layer_norm(inputs, norm_gains[0], shifts[0]))
    qkv_bias = jnp.concatenate([proj_bias[0], jnp.zeros_like(proj_bias[0]), proj_bias[1]])
    projected = low_back(low(jnp.dot(normed, mix_qkv, precision=highest_mode) + qkv_bias))
    query_set = projected[:, :D].reshape(length, HEADS, HEAD)
    key_set = projected[:, D:2 * D].reshape(length, HEADS, HEAD)
    value_set = projected[:, 2 * D:].reshape(length, HEADS, HEAD)
    block_rows = min(512, length)
    blocks = query_set.reshape(length // block_rows, block_rows, HEADS, HEAD)
    attended = lax.map(jax.checkpoint(partial(attend_block, key_set=key_set, value_set=value_set)), blocks)
    attended = low_back(low(attended.reshape(length, D)))
    branch = low_back(jnp.dot(attended, mix_out, precision=highest_mode) + proj_bias[2])
    middle = inputs + branch
    normed_two = low(layer_norm(middle, norm_gains[1], shifts[1]))
    upper_pre = low_back(jnp.dot(normed_two, mix_up, precision=highest_mode) + up_bias)
    lifted = low(jax.nn.gelu(upper_pre, approximate=False))
    branch_two = low_back(jnp.dot(lifted, mix_down, precision=highest_mode) + proj_bias[3])
    return low(middle + branch_two)

def network(clip_frames, params, probes):
    current = clip_frames
    states = []
    for depth_index in range(SECTIONS):
        layer_params = tuple((array_item[depth_index] for array_item in params))
        current = encoder_layer(low_back(current + probes[depth_index]), layer_params)
        states.append(current)
    return (current, jnp.stack(states))

def reference(frames, out_grad, norm_gain, norm_bias, w_qkv, w_out, w_up, w_down, proj_bias, up_bias):
    params = tuple((array_item.astype(jnp.float32) for array_item in (norm_gain, norm_bias, w_qkv, w_out, w_up, w_down, proj_bias, up_bias)))

    def per_clip(totals, clip_inputs):
        clip_frames, clip_grad = clip_inputs
        probes = jnp.zeros((SECTIONS, LENGTH, D), jnp.float32)
        final_out, pull_back, states = jax.vjp(partial(network, clip_frames), params, probes, has_aux=True)
        grad_params, grad_probes = pull_back(clip_grad)
        totals = jax.tree.map(jnp.add, totals, grad_params)
        return (totals, (states.astype(jnp.bfloat16), grad_probes.astype(jnp.bfloat16)))
    zeros_init = jax.tree.map(jnp.zeros_like, params)
    totals, (states, grad_all) = lax.scan(per_clip, zeros_init, (frames.astype(jnp.float32), out_grad.astype(jnp.float32)))
    hidden_states = jnp.transpose(states, (1, 0, 2, 3))
    input_grads = jnp.transpose(grad_all, (1, 0, 2, 3))
    return (hidden_states, input_grads, totals[0], totals[1], totals[2], totals[3], totals[4], totals[5], totals[6], totals[7])
```

```python
import math

import jax
import jax.numpy as jnp
from jax import lax
from jax.experimental import pallas as pl
from jax.experimental.pallas import tpu as pltpu
from jax.sharding import Mesh
from jax.sharding import PartitionSpec as P

HEADS = 12
norm_eps = 1e-05
F32 = jnp.float32
BF16 = jnp.bfloat16
VMEM_LIMIT = 56 * 1024 * 1024
AXES = ("pair", "core", "half", "quad", "side", "rest")
HEAD_GROUPS = 4


def call(body, out_shapes, grid=None, in_specs=None, out_specs=None, scratch=(), flops=0, moved=0):
    extra = {} if grid is None else dict(grid=grid, in_specs=in_specs, out_specs=out_specs)
    return pl.pallas_call(
        body,
        out_shape=out_shapes,
        scratch_shapes=scratch,
        compiler_params=pltpu.CompilerParams(vmem_limit_bytes=VMEM_LIMIT),
        cost_estimate=pl.CostEstimate(flops=flops, bytes_accessed=moved, transcendentals=0),
        **extra,
    )


def dot(left, right):
    return jnp.dot(left, right, preferred_element_type=F32)


def dot_t(left, right):
    return lax.dot_general(left, right, (((1,), (1,)), ((), ())), preferred_element_type=F32)


def t_dot(left, right):
    return lax.dot_general(left, right, (((0,), (0,)), ((), ())), preferred_element_type=F32)


def norm_parts(values):
    center = values - jnp.mean(values, axis=-1, keepdims=True)
    inverse = lax.rsqrt(jnp.mean(center * center, axis=-1, keepdims=True) + norm_eps)
    return center * inverse, inverse


def norm_back(upstream, scaled, inverse, gain_row):
    weighted = upstream * gain_row
    return inverse * (
        weighted
        - jnp.mean(weighted, axis=-1, keepdims=True)
        - scaled * jnp.mean(weighted * scaled, axis=-1, keepdims=True)
    )


def qkv_body(x_ref, gain_ref, shift_ref, w_ref, bias_ref, out_ref, normed_ref):
    scaled, _ = norm_parts(x_ref[...].astype(F32))
    normed = (scaled * gain_ref[...] + shift_ref[...]).astype(BF16)
    normed_ref[...] = normed
    span = out_ref.shape[2] // 3
    width = x_ref.shape[1]
    for part in range(3):
        cols = slice(part * width, (part + 1) * width)
        piece = (dot(normed, w_ref[:, cols]) + bias_ref[:, cols]).astype(BF16)
        for g in range(HEAD_GROUPS):
            out_ref[g, :, part * span : (part + 1) * span] = piece[:, g * span : (g + 1) * span]


def qkv_forward(x, gain, shift, w_qkv, bias):
    rows, width = x.shape
    span = width // HEAD_GROUPS
    return call(
        qkv_body,
        (
            jax.ShapeDtypeStruct((HEAD_GROUPS, rows, 3 * span), BF16),
            jax.ShapeDtypeStruct((rows, width), BF16),
        ),
        flops=2 * rows * width * 3 * width,
        moved=2 * w_qkv.size + 10 * x.size,
    )(x, gain, shift, w_qkv, bias)


def key_chunks(own_ref, other_ref):
    place = 0
    for ref in (own_ref, other_ref):
        total = ref.shape[1]
        step = 256 if total % 256 == 0 else total
        for start in range(0, total, step):
            yield ref, start, place, step
            place += step


def attend_body(q_ref, own_ref, other_ref, out_ref, log_ref, score_ref, *, head):
    span = q_ref.shape[2] // 3
    queries = q_ref.shape[1]
    scale = 1.0 / math.sqrt(head)
    for h in range(span // head):
        q = q_ref[0, :, h * head : (h + 1) * head] * scale
        top = jnp.full((1, queries), -jnp.inf, F32)
        for ref, start, place, step in key_chunks(own_ref, other_ref):
            k = ref[0, start : start + step, span + h * head : span + (h + 1) * head]
            scores = dot_t(k, q)
            score_ref[place : place + step, :] = scores
            top = jnp.maximum(top, jnp.max(scores, axis=0, keepdims=True))
        total = jnp.zeros((1, queries), F32)
        acc = jnp.zeros((head, queries), F32)
        for ref, start, place, step in key_chunks(own_ref, other_ref):
            v = ref[0, start : start + step, 2 * span + h * head : 2 * span + (h + 1) * head]
            e = jnp.exp(score_ref[place : place + step, :] - top)
            total = total + jnp.sum(e, axis=0, keepdims=True)
            acc = acc + t_dot(v, e.astype(BF16))
        out_ref[0, :, h * head : (h + 1) * head] = jnp.transpose(acc / total).astype(BF16)
        log_ref[0, h : h + 1, :] = top + jnp.log(total)


def query_block(queries):
    return 256 if queries % 256 == 0 else queries


def attend_forward(own, other, head):
    clips, queries, wide = own.shape
    span = wide // 3
    keys = queries + other.shape[1]
    block = query_block(queries)

    def body(*refs):
        attend_body(*refs, head=head)

    return call(
        body,
        (
            jax.ShapeDtypeStruct((clips, queries, span), BF16),
            jax.ShapeDtypeStruct((clips, span // head, queries), F32),
        ),
        grid=(clips, queries // block),
        in_specs=[
            pl.BlockSpec((1, block, wide), lambda m, i: (m, i, 0)),
            pl.BlockSpec((1, queries, wide), lambda m, i: (m, 0, 0)),
            pl.BlockSpec((1, other.shape[1], wide), lambda m, i: (m, 0, 0)),
        ],
        out_specs=(
            pl.BlockSpec((1, block, span), lambda m, i: (m, i, 0)),
            pl.BlockSpec((1, span // head, block), lambda m, i: (m, 0, i)),
        ),
        scratch=[pltpu.VMEM((keys, block), F32)],
        flops=16 * clips * queries * keys * span,
        moved=4 * (own.size + other.size),
    )(own, own, other)


def attend_back_body(
    q_ref,
    own_ref,
    other_ref,
    grad_ref,
    log_ref,
    dq_ref,
    dkv_own_ref,
    dkv_other_ref,
    p_ref,
    dp_ref,
    dk_acc,
    dv_acc,
    *,
    head,
):
    span = q_ref.shape[2] // 3
    queries = q_ref.shape[1]
    heads = span // head
    scale = 1.0 / math.sqrt(head)

    @pl.when(pl.program_id(1) == 0)
    def _():
        dk_acc[...] = jnp.zeros_like(dk_acc)
        dv_acc[...] = jnp.zeros_like(dv_acc)

    for h in range(heads):
        q = q_ref[0, :, h * head : (h + 1) * head] * scale
        d_out = grad_ref[0, :, h * head : (h + 1) * head]
        log_total = log_ref[0, h : h + 1, :]
        row_term = jnp.zeros((1, queries), F32)
        for ref, start, place, step in key_chunks(own_ref, other_ref):
            k = ref[0, start : start + step, span + h * head : span + (h + 1) * head]
            v = ref[0, start : start + step, 2 * span + h * head : 2 * span + (h + 1) * head]
            probs = jnp.exp(dot_t(k, q) - log_total)
            d_probs = dot_t(v, d_out)
            p_ref[place : place + step, :] = probs
            dp_ref[place : place + step, :] = d_probs
            row_term = row_term + jnp.sum(probs * d_probs, axis=0, keepdims=True)
            dv_acc[h, place : place + step, :] += dot(probs.astype(BF16), d_out)
        dq = jnp.zeros((head, queries), F32)
        for ref, start, place, step in key_chunks(own_ref, other_ref):
            k = ref[0, start : start + step, span + h * head : span + (h + 1) * head]
            d_scores = (
                p_ref[place : place + step, :] * (dp_ref[place : place + step, :] - row_term)
            ).astype(BF16)
            dk_acc[h, place : place + step, :] += dot(d_scores, q)
            dq = dq + t_dot(k, d_scores)
        dq_ref[0, :, h * head : (h + 1) * head] = jnp.transpose(dq * scale).astype(BF16)

    @pl.when(pl.program_id(1) == pl.num_programs(1) - 1)
    def _():
        place = 0
        for ref in (dkv_own_ref, dkv_other_ref):
            rows = ref.shape[1]
            for h in range(heads):
                ref[0, :, h * head : (h + 1) * head] = dk_acc[h, place : place + rows, :].astype(
                    ref.dtype
                )
                ref[0, :, span + h * head : span + (h + 1) * head] = dv_acc[
                    h, place : place + rows, :
                ].astype(ref.dtype)
            place += rows


def attend_backward(own, other, grad, log_total, head):
    clips, queries, wide = own.shape
    span = wide // 3
    others = other.shape[1]
    keys = queries + others
    block = query_block(queries)
    heads = span // head

    def body(*refs):
        attend_back_body(*refs, head=head)

    return call(
        body,
        (
            jax.ShapeDtypeStruct((clips, queries, span), BF16),
            jax.ShapeDtypeStruct((clips, queries, 2 * span), F32),
            jax.ShapeDtypeStruct((clips, others, 2 * span), BF16),
        ),
        grid=(clips, queries // block),
        in_specs=[
            pl.BlockSpec((1, block, wide), lambda m, i: (m, i, 0)),
            pl.BlockSpec((1, queries, wide), lambda m, i: (m, 0, 0)),
            pl.BlockSpec((1, others, wide), lambda m, i: (m, 0, 0)),
            pl.BlockSpec((1, block, span), lambda m, i: (m, i, 0)),
            pl.BlockSpec((1, heads, block), lambda m, i: (m, 0, i)),
        ],
        out_specs=(
            pl.BlockSpec((1, block, span), lambda m, i: (m, i, 0)),
            pl.BlockSpec((1, queries, 2 * span), lambda m, i: (m, 0, 0)),
            pl.BlockSpec((1, others, 2 * span), lambda m, i: (m, 0, 0)),
        ),
        scratch=[
            pltpu.VMEM((keys, block), F32),
            pltpu.VMEM((keys, block), F32),
            pltpu.VMEM((heads, keys, head), F32),
            pltpu.VMEM((heads, keys, head), F32),
        ],
        flops=40 * clips * queries * keys * span,
        moved=8 * (own.size + other.size),
    )(own, own, other, grad, log_total)


def feed_body(
    x_ref,
    att_ref,
    w_out_ref,
    b_out_ref,
    gain_ref,
    shift_ref,
    w_up_ref,
    b_up_ref,
    w_down_ref,
    b_down_ref,
    y_ref,
    x1_ref,
    normed_ref,
    slope_ref,
    lifted_ref,
    acc,
):
    @pl.when(pl.program_id(0) == 0)
    def _():
        middle = x_ref[...].astype(F32) + b_out_ref[...]
        for g in range(HEAD_GROUPS):
            middle = middle + dot(att_ref[g], w_out_ref[g])
        x1_ref[...] = middle
        scaled, _ = norm_parts(middle)
        normed_ref[...] = (scaled * gain_ref[...] + shift_ref[...]).astype(BF16)
        acc[...] = middle + b_down_ref[...]

    upper = dot(normed_ref[...], w_up_ref[...]) + b_up_ref[...]
    phi = 0.5 * (1.0 + lax.erf(upper * math.sqrt(0.5)))
    density = jnp.exp(-0.5 * upper * upper) * (1.0 / math.sqrt(2.0 * math.pi))
    slope_ref[...] = phi + upper * density
    lifted = (upper * phi).astype(BF16)
    lifted_ref[...] = lifted
    acc[...] += dot(lifted, w_down_ref[...])

    @pl.when(pl.program_id(0) == pl.num_programs(0) - 1)
    def _():
        y_ref[...] = acc[...].astype(BF16)


def whole(shape):
    return pl.BlockSpec(shape, lambda i: (0,) * len(shape))


def feed_forward(x, att, w_out, b_out, gain, shift, w_up, b_up, w_down, b_down):
    rows, width = x.shape
    hidden = w_up.shape[1]
    chunk = hidden // 4
    row = whole((1, width))
    full = whole((rows, width))
    return call(
        feed_body,
        (
            jax.ShapeDtypeStruct((rows, width), BF16),
            jax.ShapeDtypeStruct((rows, width), F32),
            jax.ShapeDtypeStruct((rows, width), BF16),
            jax.ShapeDtypeStruct((rows, hidden), F32),
            jax.ShapeDtypeStruct((rows, hidden), BF16),
        ),
        grid=(hidden // chunk,),
        in_specs=[
            full,
            whole(att.shape),
            whole(w_out.shape),
            row,
            row,
            row,
            pl.BlockSpec((width, chunk), lambda i: (0, i)),
            pl.BlockSpec((1, chunk), lambda i: (0, i)),
            pl.BlockSpec((chunk, width), lambda i: (i, 0)),
            row,
        ],
        out_specs=(
            full,
            full,
            full,
            pl.BlockSpec((rows, chunk), lambda i: (0, i)),
            pl.BlockSpec((rows, chunk), lambda i: (0, i)),
        ),
        scratch=[pltpu.VMEM((rows, width), F32)],
        flops=2 * rows * width * (2 * hidden + width),
        moved=4 * w_up.size + 2 * w_out.size + 10 * rows * hidden,
    )(x, att, w_out, b_out, gain, shift, w_up, b_up, w_down, b_down)


def feed_back_body(
    g_ref,
    slope_ref,
    w_down_ref,
    w_up_ref,
    w_out_ref,
    x1_ref,
    gain_ref,
    d_upper_ref,
    dx1_ref,
    branch_ref,
    datt_ref,
    sums_ref,
    up_sum_ref,
    acc,
):
    @pl.when(pl.program_id(0) == 0)
    def _():
        acc[...] = jnp.zeros_like(acc)

    d_upper = (dot_t(g_ref[...], w_down_ref[...]) * slope_ref[...]).astype(BF16)
    d_upper_ref[...] = d_upper
    up_sum_ref[...] = jnp.sum(d_upper.astype(F32), axis=0, keepdims=True)
    acc[...] += dot_t(d_upper, w_up_ref[...])

    @pl.when(pl.program_id(0) == pl.num_programs(0) - 1)
    def _():
        d_normed = acc[...]
        upstream = g_ref[...].astype(F32)
        scaled, inverse = norm_parts(x1_ref[...])
        d_middle = upstream + norm_back(d_normed, scaled, inverse, gain_ref[...])
        dx1_ref[...] = d_middle
        branch = d_middle.astype(BF16)
        branch_ref[...] = branch
        for g in range(HEAD_GROUPS):
            datt_ref[g] = dot_t(branch, w_out_ref[g]).astype(BF16)
        sums_ref[0:1, :] = jnp.sum(d_normed * scaled, axis=0, keepdims=True)
        sums_ref[1:2, :] = jnp.sum(d_normed, axis=0, keepdims=True)
        sums_ref[2:3, :] = jnp.sum(branch.astype(F32), axis=0, keepdims=True)
        sums_ref[3:4, :] = jnp.sum(upstream, axis=0, keepdims=True)


def feed_backward(g, slope, w_down, w_up, w_out, x1, gain):
    rows, width = g.shape
    hidden = w_up.shape[1]
    chunk = hidden // 4
    full = whole((rows, width))
    return call(
        feed_back_body,
        (
            jax.ShapeDtypeStruct((rows, hidden), BF16),
            jax.ShapeDtypeStruct((rows, width), F32),
            jax.ShapeDtypeStruct((rows, width), BF16),
            jax.ShapeDtypeStruct((HEAD_GROUPS, rows, width // HEAD_GROUPS), BF16),
            jax.ShapeDtypeStruct((4, width), F32),
            jax.ShapeDtypeStruct((1, hidden), F32),
        ),
        grid=(hidden // chunk,),
        in_specs=[
            full,
            pl.BlockSpec((rows, chunk), lambda i: (0, i)),
            pl.BlockSpec((chunk, width), lambda i: (i, 0)),
            pl.BlockSpec((width, chunk), lambda i: (0, i)),
            whole(w_out.shape),
            full,
            whole((1, width)),
        ],
        out_specs=(
            pl.BlockSpec((rows, chunk), lambda i: (0, i)),
            full,
            full,
            whole((HEAD_GROUPS, rows, width // HEAD_GROUPS)),
            whole((4, width)),
            pl.BlockSpec((1, chunk), lambda i: (0, i)),
        ),
        scratch=[pltpu.VMEM((rows, width), F32)],
        flops=2 * rows * width * (2 * hidden + width),
        moved=4 * w_up.size + 2 * w_out.size + 6 * rows * hidden,
    )(g, slope, w_down, w_up, w_out, x1, gain)


def qkv_back_body(
    grads_ref, w_ref, x_ref, dx1_ref, gain_ref, dx_ref, flat_ref, sums_ref
):
    width = x_ref.shape[1]
    span = grads_ref.shape[2] // 3
    for g in range(HEAD_GROUPS):
        for part in range(3):
            flat_ref[:, part * width + g * span : part * width + (g + 1) * span] = grads_ref[
                g, :, part * span : (part + 1) * span
            ]
    d_normed = dot_t(flat_ref[...], w_ref[...])
    scaled, inverse = norm_parts(x_ref[...].astype(F32))
    dx = dx1_ref[...] + norm_back(d_normed, scaled, inverse, gain_ref[...])
    dx_ref[...] = dx.astype(BF16)
    sums_ref[0:1, :] = jnp.sum(d_normed * scaled, axis=0, keepdims=True)
    sums_ref[1:2, :] = jnp.sum(d_normed, axis=0, keepdims=True)
    sums_ref[2:3, :] = jnp.sum(flat_ref[:, :width].astype(F32), axis=0, keepdims=True)
    sums_ref[3:4, :] = jnp.sum(flat_ref[:, 2 * width :].astype(F32), axis=0, keepdims=True)


def qkv_backward(grads, w_qkv, x, dx1, gain):
    rows, width = x.shape
    return call(
        qkv_back_body,
        (
            jax.ShapeDtypeStruct((rows, width), BF16),
            jax.ShapeDtypeStruct((rows, 3 * width), BF16),
            jax.ShapeDtypeStruct((4, width), F32),
        ),
        flops=2 * rows * width * 3 * width,
        moved=2 * w_qkv.size + 20 * x.size,
    )(grads, w_qkv, x, dx1, gain)


def swap(block, axis):
    return lax.ppermute(block, axis, [(0, 1), (1, 0)])


def shift(block, distance):
    count = lax.axis_size("rest")
    return lax.ppermute(block, "rest", [(i, (i + distance) % count) for i in range(count)])


def spread(block):
    return lax.all_to_all(block, ("quad", "side"), 0, 0, tiled=True)


def to_clips(block, clips):
    groups, rows, wide = block.shape
    block = block.reshape(groups, clips, rows // clips, wide)
    return jnp.swapaxes(block, 0, 1).reshape(clips, groups * (rows // clips), wide)


def to_tokens(block):
    clips, rows, wide = block.shape
    block = block.reshape(clips, HEAD_GROUPS, rows // HEAD_GROUPS, wide)
    return jnp.swapaxes(block, 0, 1).reshape(HEAD_GROUPS, -1, wide)


def other_keys(own):
    near = [shift(own, k) for k in range(1, lax.axis_size("rest"))]
    far = swap(jnp.concatenate([own] + near, axis=1) if near else own, "core")
    return jnp.concatenate(near + [far], axis=1) if near else far


def return_keys(kept, sent):
    queries = kept.shape[1]
    count = lax.axis_size("rest")
    near = (count - 1) * queries
    back = swap(sent[:, near:], "core").astype(F32)
    total = kept + back[:, :queries]
    for k in range(1, count):
        part = sent[:, (k - 1) * queries : k * queries].astype(F32)
        part = part + back[:, k * queries : (k + 1) * queries]
        total = total + shift(part.astype(BF16), -k).astype(F32)
    return total


def pick(flag, one, two):
    return jnp.where(flag, one, two)


def gather_weight(block):
    core = lax.axis_index("core")
    quads = lax.axis_size("quad")
    part = block.shape[0] // (2 * quads)
    quad = lax.axis_index("quad")

    def cut(which):
        return lax.dynamic_slice_in_dim(block, (which * quads + quad) * part, part, 0)

    own = cut(core)
    came = swap(cut(1 - core), "core")
    first = pick(core == 0, own, came)
    second = pick(core == 0, came, own)
    return [
        lax.all_gather(item, ("side", "rest", "core", "quad"), axis=0, tiled=True)
        for item in (first, second)
    ]


def add(one, two):
    return (one.astype(F32) + two.astype(F32)).astype(one.dtype)


def reduce_rows(grad, layer):
    side = lax.axis_index("side")
    paired = lax.ppermute(grad, "core", [(1 - layer, layer)])
    half = grad.shape[0] // 2

    def cut(which):
        start = which * half
        return add(
            lax.dynamic_slice_in_dim(grad, start, half, 0),
            lax.dynamic_slice_in_dim(paired, start, half, 0),
        )

    two = 2 * layer
    came = lax.ppermute(cut(1 - side), ("core", "side"), [(two, two + 1), (two + 1, two)])
    total = add(cut(side), came)
    if lax.axis_size("rest") > 1:
        total = lax.psum_scatter(total, "rest", scatter_dimension=0, tiled=True)
    quads = lax.axis_size("quad")
    if quads != 2:
        return lax.psum(total, ("half", "quad"))
    base = 4 * layer
    line = ("core", "half", "quad")

    def hop(block, pairs):
        return lax.ppermute(block, line, [(base + a, base + b) for a, b in pairs])

    total = add(total, hop(total, [(0, 1), (3, 2)]))
    total = add(total, hop(total, [(1, 2), (2, 1)]))
    came = hop(total, [(1, 0), (2, 3)])
    inner = lax.axis_index("half") != lax.axis_index("quad")
    return pick(inner, total, came)


def swap_in(block):
    core, half = lax.axis_index("core"), lax.axis_index("half")
    micro, rows, wide = block.shape
    block = block.reshape(2, (micro // 2) * rows, wide)
    own = lax.dynamic_index_in_dim(block, half, 0, keepdims=False)
    other = lax.dynamic_index_in_dim(block, 1 - half, 0, keepdims=False)
    came = lax.ppermute(other, ("core", "half"), [(1, 2), (2, 1)])
    return pick(core == half, own, came)


def swap_out(first, second, micro):
    rows, wide = first.shape
    both = jnp.stack([first, second])
    both = lax.all_to_all(both, "core", 0, 0, tiled=True)
    both = lax.all_to_all(both, "half", 0, 0, tiled=True)
    return both.reshape(micro, 2 * rows // micro, wide)


def forward_layer(x, weights, clips, head):
    w_qkv, w_out, w_up, w_down, gains, shifts, b_qkv, b_out, b_down, b_up = weights
    width = x.shape[1]
    grouped, normed_one = qkv_forward(x, gains[0:1], shifts[0:1], w_qkv, b_qkv)
    own = to_clips(spread(grouped), clips)
    other = other_keys(own)
    att, log_total = attend_forward(own, other, head)
    att = spread(to_tokens(att))
    y, x1, normed_two, slope, lifted = feed_forward(
        x,
        att,
        w_out.reshape(HEAD_GROUPS, width // HEAD_GROUPS, width),
        b_out,
        gains[1:2],
        shifts[1:2],
        w_up,
        b_up,
        w_down,
        b_down,
    )
    return y, (x, normed_one, own, other, log_total, att, x1, normed_two, slope, lifted)


def backward_layer(kept, g, weights, clips, head, with_weights):
    x, normed_one, own, other, log_total, att, x1, normed_two, slope, lifted = kept
    w_qkv, w_out, w_up, w_down, gains, shifts, b_qkv, b_out, b_down, b_up = weights
    width = x.shape[1]
    d_upper, dx1, branch, d_att, sums_two, up_sum = feed_backward(
        g,
        slope,
        w_down,
        w_up,
        w_out.reshape(HEAD_GROUPS, width // HEAD_GROUPS, width),
        x1,
        gains[1:2],
    )
    d_heads = to_clips(spread(d_att), clips)
    dq, kept_kv, sent_kv = attend_backward(own, other, d_heads, log_total, head)
    dkv = return_keys(kept_kv, sent_kv).astype(BF16)
    d_own = jnp.concatenate([dq, dkv], axis=2)
    d_tokens = spread(to_tokens(d_own))
    dx, flat, sums_one = qkv_backward(d_tokens, w_qkv, x, dx1, gains[0:1])
    if not with_weights:
        return dx, None
    grad_down = t_dot(lifted, g).astype(BF16)
    grad_up = t_dot(normed_two, d_upper).astype(BF16)
    grad_out = jnp.einsum("gtf,td->gfd", att, branch, preferred_element_type=F32)
    grad_out = grad_out.astype(BF16).reshape(width, width)
    grad_qkv = t_dot(normed_one, flat).astype(BF16)
    return dx, (grad_qkv, grad_out, grad_up, grad_down, sums_one, sums_two, up_sum)


def pack_small(sums_one, sums_two, up_sum, shards):
    rows = jnp.concatenate(
        [
            sums_one[0:1],
            sums_two[0:1],
            sums_one[1:2],
            sums_two[1:2],
            sums_one[2:4],
            sums_two[2:4],
        ]
    )
    rows = jnp.swapaxes(rows.reshape(8, shards, -1), 0, 1).reshape(shards, -1)
    packed = jnp.concatenate([rows, up_sum.reshape(shards, -1)], axis=1)
    return packed.reshape(-1, 128)


def per_device(
    frames, out_grad, norm_gain, norm_bias, w_qkv, w_out, w_up, w_down, proj_bias, up_bias
):
    pairs = lax.axis_size("pair")
    pair = lax.axis_index("pair")
    core = lax.axis_index("core")
    shards = lax.axis_size("side") * lax.axis_size("rest")
    micro, _, width = frames.shape
    clips = micro // 2
    head = width // HEADS
    part = width // shards

    small = jnp.concatenate(
        [norm_gain.reshape(-1), norm_bias.reshape(-1), proj_bias.reshape(-1), up_bias.reshape(-1)]
    )
    small = lax.all_gather(small, ("core", "side", "rest"), axis=0, tiled=False)
    small = small.reshape(2, shards, -1).astype(F32)
    rows = jnp.swapaxes(small[:, :, : 8 * part].reshape(2, shards, 8, part), 1, 2)
    rows = rows.reshape(2, 8, width)
    ups = small[:, :, 8 * part :].reshape(2, 1, -1)
    x_start = swap_in(frames)
    matrices = [gather_weight(item[0]) for item in (w_qkv, w_out, w_up, w_down)]
    layers = []
    for layer in range(2):
        r = rows[layer]
        b_qkv = jnp.concatenate([r[4:5], jnp.zeros_like(r[4:5]), r[5:6]], axis=1)
        layers.append(
            tuple(m[layer] for m in matrices)
            + (r[0:2], r[2:4], b_qkv, r[6:7], r[7:8], ups[layer])
        )

    x = x_start
    for phase in range(pairs):
        if phase > 0:
            came = lax.ppermute(second, "pair", [(i, i + 1) for i in range(pairs - 1)])
            x = pick(pair == 0, x_start, came)
        first, kept_first = forward_layer(x, layers[0], clips, head)
        second, kept_second = forward_layer(first, layers[1], clips, head)
    hidden = swap_out(first, second, micro)

    g_start = swap_in(out_grad)
    g = g_start
    for phase in range(pairs):
        if phase > 0:
            came = lax.ppermute(d_first, "pair", [(i + 1, i) for i in range(pairs - 1)])
            g = pick(pair == pairs - 1, g_start, came)
        last = phase == pairs - 1
        d_second, grads_second = backward_layer(kept_second, g, layers[1], clips, head, last)
        d_first, grads_first = backward_layer(kept_first, d_second, layers[0], clips, head, last)
    input_grads = swap_out(d_first, d_second, micro)

    reduced = []
    for layer, grads in ((1, grads_second), (0, grads_first)):
        items = [reduce_rows(item, layer) for item in (grads[3], grads[2], grads[1], grads[0])]
        items.append(reduce_rows(pack_small(*grads[4:], shards), layer))
        reduced.append(items)
    down, up, out, qkv, packed = [
        pick(core == 0, zero, one).astype(F32) for one, zero in zip(*reduced)
    ]
    packed = packed.reshape(-1)
    heads = packed[: 8 * part].reshape(8, part)
    return (
        hidden[None],
        input_grads[None],
        heads[0:2][None],
        heads[2:4][None],
        qkv[None],
        out[None],
        up[None],
        down[None],
        heads[4:8][None],
        packed[8 * part :][None],
    )


def solution(mesh):
    sections, groups, shards = (mesh.shape[name] for name in ("section", "seq", "shard"))
    cut = Mesh(
        mesh.devices.reshape(sections // 2, 2, 2, groups // 2, 2, shards // 2),
        AXES,
    )
    section, seq, shard = ("pair", "core"), ("half", "quad"), ("side", "rest")
    rows = seq + shard
    return jax.shard_map(
        per_device,
        mesh=cut,
        in_specs=(
            P(None, rows, None),
            P(None, rows, None),
            P(section, None, shard),
            P(section, None, shard),
            P(section, shard, None),
            P(section, shard, None),
            P(section, shard, None),
            P(section, shard, None),
            P(section, None, shard),
            P(section, shard),
        ),
        out_specs=(
            P(section, None, rows, None),
            P(section, None, rows, None),
            P(section, None, shard),
            P(section, None, shard),
            P(section, shard, None),
            P(section, shard, None),
            P(section, shard, None),
            P(section, shard, None),
            P(section, None, shard),
            P(section, shard),
        ),
        check_vma=False,
    )
```

```python
import math

import jax
import jax.numpy as jnp
from jax import lax
from jax.experimental import pallas as pl
from jax.experimental.pallas import tpu as pltpu
from jax.sharding import Mesh
from jax.sharding import PartitionSpec as P

HEADS = 12
norm_eps = 1e-05
F32 = jnp.float32
BF16 = jnp.bfloat16
VMEM_LIMIT = 56 * 1024 * 1024
AXES = ("pair", "core", "half", "quad", "side", "rest")
HEAD_GROUPS = 4


def call(body, out_shapes, grid=None, in_specs=None, out_specs=None, scratch=(), flops=0, moved=0):
    extra = {} if grid is None else dict(grid=grid, in_specs=in_specs, out_specs=out_specs)
    return pl.pallas_call(
        body,
        out_shape=out_shapes,
        scratch_shapes=scratch,
        compiler_params=pltpu.CompilerParams(vmem_limit_bytes=VMEM_LIMIT),
        cost_estimate=pl.CostEstimate(flops=flops, bytes_accessed=moved, transcendentals=0),
        **extra,
    )


def dot(left, right):
    return jnp.dot(left, right, preferred_element_type=F32)


def dot_t(left, right):
    return lax.dot_general(left, right, (((1,), (1,)), ((), ())), preferred_element_type=F32)


def t_dot(left, right):
    return lax.dot_general(left, right, (((0,), (0,)), ((), ())), preferred_element_type=F32)


def norm_parts(values):
    center = values - jnp.mean(values, axis=-1, keepdims=True)
    inverse = lax.rsqrt(jnp.mean(center * center, axis=-1, keepdims=True) + norm_eps)
    return center * inverse, inverse


def norm_back(upstream, scaled, inverse, gain_row):
    weighted = upstream * gain_row
    return inverse * (
        weighted
        - jnp.mean(weighted, axis=-1, keepdims=True)
        - scaled * jnp.mean(weighted * scaled, axis=-1, keepdims=True)
    )


def qkv_body(x_ref, gain_ref, shift_ref, w_ref, bias_ref, out_ref, normed_ref):
    @pl.when(pl.program_id(0) == 0)
    def _():
        scaled, _ = norm_parts(x_ref[...].astype(F32))
        normed_ref[...] = (scaled * gain_ref[...] + shift_ref[...]).astype(BF16)

    span = out_ref.shape[2] // 3
    piece = (dot(normed_ref[...], w_ref[...]) + bias_ref[...]).astype(BF16)
    for part in range(3):

        @pl.when(pl.program_id(0) == part)
        def _(part=part):
            for g in range(HEAD_GROUPS):
                out_ref[g, :, part * span : (part + 1) * span] = piece[:, g * span : (g + 1) * span]


def qkv_forward(x, gain, shift, joined, bias):
    rows, width = x.shape
    span = width // HEAD_GROUPS
    return call(
        qkv_body,
        (
            jax.ShapeDtypeStruct((HEAD_GROUPS, rows, 3 * span), BF16),
            jax.ShapeDtypeStruct((rows, width), BF16),
        ),
        grid=(3,),
        in_specs=[
            whole((rows, width)),
            whole((1, width)),
            whole((1, width)),
            pl.BlockSpec((width, width), lambda i: (0, i)),
            pl.BlockSpec((1, width), lambda i: (0, i)),
        ],
        out_specs=(whole((HEAD_GROUPS, rows, 3 * span)), whole((rows, width))),
        flops=2 * rows * width * 3 * width,
        moved=6 * width * width + 10 * x.size,
    )(x, gain, shift, joined, bias)


def key_chunks(own_ref, other_ref):
    place = 0
    for ref in (own_ref, other_ref):
        total = ref.shape[1]
        step = 256 if total % 256 == 0 else total
        for start in range(0, total, step):
            yield ref, start, place, step
            place += step


def attend_body(q_ref, own_ref, other_ref, out_ref, log_ref, score_ref, *, head):
    span = q_ref.shape[2] // 3
    queries = q_ref.shape[1]
    scale = 1.0 / math.sqrt(head)
    for h in range(span // head):
        q = q_ref[0, :, h * head : (h + 1) * head] * scale
        top = jnp.full((1, queries), -jnp.inf, F32)
        for ref, start, place, step in key_chunks(own_ref, other_ref):
            k = ref[0, start : start + step, span + h * head : span + (h + 1) * head]
            scores = dot_t(k, q)
            score_ref[place : place + step, :] = scores
            top = jnp.maximum(top, jnp.max(scores, axis=0, keepdims=True))
        total = jnp.zeros((1, queries), F32)
        acc = jnp.zeros((head, queries), F32)
        for ref, start, place, step in key_chunks(own_ref, other_ref):
            v = ref[0, start : start + step, 2 * span + h * head : 2 * span + (h + 1) * head]
            e = jnp.exp(score_ref[place : place + step, :] - top)
            total = total + jnp.sum(e, axis=0, keepdims=True)
            acc = acc + t_dot(v, e.astype(BF16))
        out_ref[0, :, h * head : (h + 1) * head] = jnp.transpose(acc / total).astype(BF16)
        log_ref[0, h : h + 1, :] = top + jnp.log(total)


def query_block(queries):
    return 256 if queries % 256 == 0 else queries


def attend_forward(own, other, head):
    clips, queries, wide = own.shape
    span = wide // 3
    keys = queries + other.shape[1]
    block = query_block(queries)

    def body(*refs):
        attend_body(*refs, head=head)

    return call(
        body,
        (
            jax.ShapeDtypeStruct((clips, queries, span), BF16),
            jax.ShapeDtypeStruct((clips, span // head, queries), F32),
        ),
        grid=(clips, queries // block),
        in_specs=[
            pl.BlockSpec((1, block, wide), lambda m, i: (m, i, 0)),
            pl.BlockSpec((1, queries, wide), lambda m, i: (m, 0, 0)),
            pl.BlockSpec((1, other.shape[1], wide), lambda m, i: (m, 0, 0)),
        ],
        out_specs=(
            pl.BlockSpec((1, block, span), lambda m, i: (m, i, 0)),
            pl.BlockSpec((1, span // head, block), lambda m, i: (m, 0, i)),
        ),
        scratch=[pltpu.VMEM((keys, block), F32)],
        flops=16 * clips * queries * keys * span,
        moved=4 * (own.size + other.size),
    )(own, own, other)


def attend_back_body(
    q_ref,
    own_ref,
    other_ref,
    grad_ref,
    log_ref,
    dq_ref,
    dkv_own_ref,
    dkv_other_ref,
    p_ref,
    dp_ref,
    dk_acc,
    dv_acc,
    *,
    head,
):
    span = q_ref.shape[2] // 3
    queries = q_ref.shape[1]
    heads = span // head
    scale = 1.0 / math.sqrt(head)

    @pl.when(pl.program_id(1) == 0)
    def _():
        dk_acc[...] = jnp.zeros_like(dk_acc)
        dv_acc[...] = jnp.zeros_like(dv_acc)

    for h in range(heads):
        q = q_ref[0, :, h * head : (h + 1) * head] * scale
        d_out = grad_ref[0, :, h * head : (h + 1) * head]
        log_total = log_ref[0, h : h + 1, :]
        row_term = jnp.zeros((1, queries), F32)
        for ref, start, place, step in key_chunks(own_ref, other_ref):
            k = ref[0, start : start + step, span + h * head : span + (h + 1) * head]
            v = ref[0, start : start + step, 2 * span + h * head : 2 * span + (h + 1) * head]
            probs = jnp.exp(dot_t(k, q) - log_total)
            d_probs = dot_t(v, d_out)
            p_ref[place : place + step, :] = probs
            dp_ref[place : place + step, :] = d_probs
            row_term = row_term + jnp.sum(probs * d_probs, axis=0, keepdims=True)
            dv_acc[h, place : place + step, :] += dot(probs.astype(BF16), d_out)
        dq = jnp.zeros((head, queries), F32)
        for ref, start, place, step in key_chunks(own_ref, other_ref):
            k = ref[0, start : start + step, span + h * head : span + (h + 1) * head]
            d_scores = (
                p_ref[place : place + step, :] * (dp_ref[place : place + step, :] - row_term)
            ).astype(BF16)
            dk_acc[h, place : place + step, :] += dot(d_scores, q)
            dq = dq + t_dot(k, d_scores)
        dq_ref[0, :, h * head : (h + 1) * head] = jnp.transpose(dq * scale).astype(BF16)

    @pl.when(pl.program_id(1) == pl.num_programs(1) - 1)
    def _():
        place = 0
        for ref in (dkv_own_ref, dkv_other_ref):
            rows = ref.shape[1]
            for h in range(heads):
                ref[0, :, h * head : (h + 1) * head] = dk_acc[h, place : place + rows, :].astype(
                    ref.dtype
                )
                ref[0, :, span + h * head : span + (h + 1) * head] = dv_acc[
                    h, place : place + rows, :
                ].astype(ref.dtype)
            place += rows


def attend_backward(own, other, grad, log_total, head, after=()):
    clips, queries, wide = own.shape
    span = wide // 3
    others = other.shape[1]
    keys = queries + others
    block = query_block(queries)
    heads = span // head

    def body(*refs):
        attend_back_body(*refs[:5], *refs[5 + len(after) :], head=head)

    return call(
        body,
        (
            jax.ShapeDtypeStruct((clips, queries, span), BF16),
            jax.ShapeDtypeStruct((clips, queries, 2 * span), F32),
            jax.ShapeDtypeStruct((clips, others, 2 * span), BF16),
        ),
        grid=(clips, queries // block),
        in_specs=[
            pl.BlockSpec((1, block, wide), lambda m, i: (m, i, 0)),
            pl.BlockSpec((1, queries, wide), lambda m, i: (m, 0, 0)),
            pl.BlockSpec((1, others, wide), lambda m, i: (m, 0, 0)),
            pl.BlockSpec((1, block, span), lambda m, i: (m, i, 0)),
            pl.BlockSpec((1, heads, block), lambda m, i: (m, 0, i)),
        ]
        + [pl.BlockSpec(memory_space=pl.ANY)] * len(after),
        out_specs=(
            pl.BlockSpec((1, block, span), lambda m, i: (m, i, 0)),
            pl.BlockSpec((1, queries, 2 * span), lambda m, i: (m, 0, 0)),
            pl.BlockSpec((1, others, 2 * span), lambda m, i: (m, 0, 0)),
        ),
        scratch=[
            pltpu.VMEM((keys, block), F32),
            pltpu.VMEM((keys, block), F32),
            pltpu.VMEM((heads, keys, head), F32),
            pltpu.VMEM((heads, keys, head), F32),
        ],
        flops=40 * clips * queries * keys * span,
        moved=8 * (own.size + other.size),
    )(own, own, other, grad, log_total, *after)


def feed_body(
    x_ref,
    att_ref,
    w_out_ref,
    b_out_ref,
    gain_ref,
    shift_ref,
    w_up_ref,
    b_up_ref,
    w_down_ref,
    b_down_ref,
    y_ref,
    *rest,
):
    if len(rest) > 2:
        x1_ref, normed_ref, slope_ref, lifted_ref, flat_ref, acc = rest
    else:
        normed_ref, acc = rest
    span = att_ref.shape[2]

    @pl.when(pl.program_id(0) == 0)
    def _():
        middle = x_ref[...].astype(F32) + b_out_ref[...]
        for g in range(HEAD_GROUPS):
            middle = middle + dot(att_ref[g], w_out_ref[g * span : (g + 1) * span, :])
            if len(rest) > 2:
                flat_ref[:, g * span : (g + 1) * span] = att_ref[g]
        if len(rest) > 2:
            x1_ref[...] = middle
        scaled, _ = norm_parts(middle)
        normed_ref[...] = (scaled * gain_ref[...] + shift_ref[...]).astype(BF16)
        acc[...] = middle + b_down_ref[...]

    upper = dot(normed_ref[...], w_up_ref[...]) + b_up_ref[...]
    phi = 0.5 * (1.0 + lax.erf(upper * math.sqrt(0.5)))
    lifted = (upper * phi).astype(BF16)
    if len(rest) > 2:
        density = jnp.exp(-0.5 * upper * upper) * (1.0 / math.sqrt(2.0 * math.pi))
        slope_ref[...] = phi + upper * density
        lifted_ref[...] = lifted
    acc[...] += dot(lifted, w_down_ref[...])

    @pl.when(pl.program_id(0) == pl.num_programs(0) - 1)
    def _():
        y_ref[...] = acc[...].astype(BF16)


def whole(shape):
    return pl.BlockSpec(shape, lambda i: (0,) * len(shape))


def feed_forward(x, att, joined, b_out, gain, shift, b_up, w_down, b_down, keep):
    rows, width = x.shape
    hidden = w_down.shape[0]
    row = whole((1, width))
    full = whole((rows, width))
    part = pl.BlockSpec((rows, width), lambda i: (0, i))
    shapes = [jax.ShapeDtypeStruct((rows, width), BF16)]
    specs = [full]
    scratch = [pltpu.VMEM((rows, width), F32)]
    if keep:
        shapes += [
            jax.ShapeDtypeStruct((rows, width), F32),
            jax.ShapeDtypeStruct((rows, width), BF16),
            jax.ShapeDtypeStruct((rows, hidden), F32),
            jax.ShapeDtypeStruct((rows, hidden), BF16),
            jax.ShapeDtypeStruct((rows, width), BF16),
        ]
        specs += [full, full, part, part, full]
    else:
        scratch = [pltpu.VMEM((rows, width), BF16)] + scratch
    return call(
        feed_body,
        tuple(shapes),
        grid=(hidden // width,),
        in_specs=[
            full,
            whole(att.shape),
            pl.BlockSpec((width, width), lambda i: (0, 3)),
            row,
            row,
            row,
            pl.BlockSpec((width, width), lambda i: (0, 4 + i)),
            pl.BlockSpec((1, width), lambda i: (0, i)),
            pl.BlockSpec((width, width), lambda i: (i, 0)),
            row,
        ],
        out_specs=tuple(specs),
        scratch=scratch,
        flops=2 * rows * width * (2 * hidden + width),
        moved=4 * w_down.size + 2 * width * width + 10 * rows * hidden,
    )(x, att, joined, b_out, gain, shift, joined, b_up, w_down, b_down)


def feed_back_body(
    g_ref,
    slope_ref,
    w_down_ref,
    w_up_ref,
    w_out_ref,
    x1_ref,
    gain_ref,
    d_upper_ref,
    dx1_ref,
    branch_ref,
    datt_ref,
    sums_ref,
    up_sum_ref,
    acc,
):
    @pl.when(pl.program_id(0) == 0)
    def _():
        acc[...] = jnp.zeros_like(acc)

    d_upper = (dot_t(g_ref[...], w_down_ref[...]) * slope_ref[...]).astype(BF16)
    d_upper_ref[...] = d_upper
    up_sum_ref[...] = jnp.sum(d_upper.astype(F32), axis=0, keepdims=True)
    acc[...] += dot_t(d_upper, w_up_ref[...])

    @pl.when(pl.program_id(0) == pl.num_programs(0) - 1)
    def _():
        d_normed = acc[...]
        upstream = g_ref[...].astype(F32)
        scaled, inverse = norm_parts(x1_ref[...])
        d_middle = upstream + norm_back(d_normed, scaled, inverse, gain_ref[...])
        dx1_ref[...] = d_middle
        branch = d_middle.astype(BF16)
        branch_ref[...] = branch
        span = datt_ref.shape[2]
        for g in range(HEAD_GROUPS):
            datt_ref[g] = dot_t(branch, w_out_ref[g * span : (g + 1) * span, :]).astype(BF16)
        sums_ref[0:1, :] = jnp.sum(d_normed * scaled, axis=0, keepdims=True)
        sums_ref[1:2, :] = jnp.sum(d_normed, axis=0, keepdims=True)
        sums_ref[2:3, :] = jnp.sum(branch.astype(F32), axis=0, keepdims=True)
        sums_ref[3:4, :] = jnp.sum(upstream, axis=0, keepdims=True)


def feed_backward(g, slope, w_down, joined, x1, gain):
    rows, width = g.shape
    hidden = w_down.shape[0]
    chunk = width
    full = whole((rows, width))
    return call(
        feed_back_body,
        (
            jax.ShapeDtypeStruct((rows, hidden), BF16),
            jax.ShapeDtypeStruct((rows, width), F32),
            jax.ShapeDtypeStruct((rows, width), BF16),
            jax.ShapeDtypeStruct((HEAD_GROUPS, rows, width // HEAD_GROUPS), BF16),
            jax.ShapeDtypeStruct((4, width), F32),
            jax.ShapeDtypeStruct((1, hidden), F32),
        ),
        grid=(hidden // chunk,),
        in_specs=[
            full,
            pl.BlockSpec((rows, chunk), lambda i: (0, i)),
            pl.BlockSpec((chunk, width), lambda i: (i, 0)),
            pl.BlockSpec((width, chunk), lambda i: (0, 4 + i)),
            pl.BlockSpec((width, width), lambda i: (0, 3)),
            full,
            whole((1, width)),
        ],
        out_specs=(
            pl.BlockSpec((rows, chunk), lambda i: (0, i)),
            full,
            full,
            whole((HEAD_GROUPS, rows, width // HEAD_GROUPS)),
            whole((4, width)),
            pl.BlockSpec((1, chunk), lambda i: (0, i)),
        ),
        scratch=[pltpu.VMEM((rows, width), F32)],
        flops=2 * rows * width * (2 * hidden + width),
        moved=4 * w_down.size + 2 * width * width + 6 * rows * hidden,
    )(g, slope, w_down, joined, joined, x1, gain)


def qkv_back_body(
    grads_ref, w_ref, x_ref, dx1_ref, gain_ref, dx_ref, flat_ref, sums_ref, acc
):
    width = x_ref.shape[1]
    span = grads_ref.shape[2] // 3
    step = pl.program_id(0)
    for part in range(3):

        @pl.when(step == part)
        def _(part=part):
            cols = slice(part * width, (part + 1) * width)
            for g in range(HEAD_GROUPS):
                flat_ref[:, part * width + g * span : part * width + (g + 1) * span] = grads_ref[
                    g, :, part * span : (part + 1) * span
                ]
            came = dot_t(flat_ref[:, cols], w_ref[...])
            acc[...] = came if part == 0 else acc[...] + came

    @pl.when(step == 2)
    def _():
        d_normed = acc[...]
        scaled, inverse = norm_parts(x_ref[...].astype(F32))
        dx = dx1_ref[...] + norm_back(d_normed, scaled, inverse, gain_ref[...])
        dx_ref[...] = dx.astype(BF16)
        sums_ref[0:1, :] = jnp.sum(d_normed * scaled, axis=0, keepdims=True)
        sums_ref[1:2, :] = jnp.sum(d_normed, axis=0, keepdims=True)
        sums_ref[2:3, :] = jnp.sum(flat_ref[:, :width].astype(F32), axis=0, keepdims=True)
        sums_ref[3:4, :] = jnp.sum(flat_ref[:, 2 * width :].astype(F32), axis=0, keepdims=True)


def qkv_backward(grads, joined, x, dx1, gain, after=()):
    rows, width = x.shape

    def body(*refs):
        qkv_back_body(*refs[:5], *refs[5 + len(after) :])

    return call(
        body,
        (
            jax.ShapeDtypeStruct((rows, width), BF16),
            jax.ShapeDtypeStruct((rows, 3 * width), BF16),
            jax.ShapeDtypeStruct((4, width), F32),
        ),
        grid=(3,),
        in_specs=[
            whole(grads.shape),
            pl.BlockSpec((width, width), lambda i: (0, i)),
            whole((rows, width)),
            whole((rows, width)),
            whole((1, width)),
        ]
        + [pl.BlockSpec(memory_space=pl.ANY)] * len(after),
        out_specs=(whole((rows, width)), whole((rows, 3 * width)), whole((4, width))),
        scratch=[pltpu.VMEM((rows, width), F32)],
        flops=2 * rows * width * 3 * width,
        moved=6 * width * width + 20 * x.size,
    )(grads, joined, x, dx1, gain, *after)


def swap(block, axis):
    return lax.ppermute(block, axis, [(0, 1), (1, 0)])


def shift(block, distance):
    count = lax.axis_size("rest")
    return lax.ppermute(block, "rest", [(i, (i + distance) % count) for i in range(count)])


def spread(block):
    return lax.all_to_all(block, ("quad", "side"), 0, 0, tiled=True)


def to_clips(block, clips):
    groups, rows, wide = block.shape
    if clips == 1:
        return block.reshape(1, groups * rows, wide)
    block = block.reshape(groups, clips, rows // clips, wide)
    return jnp.swapaxes(block, 0, 1).reshape(clips, groups * (rows // clips), wide)


def to_tokens(block):
    clips, rows, wide = block.shape
    if clips == 1:
        return block.reshape(HEAD_GROUPS, rows // HEAD_GROUPS, wide)
    block = block.reshape(clips, HEAD_GROUPS, rows // HEAD_GROUPS, wide)
    return jnp.swapaxes(block, 0, 1).reshape(HEAD_GROUPS, -1, wide)


def other_keys(own):
    near = [shift(own, k) for k in range(1, lax.axis_size("rest"))]
    far = swap(jnp.concatenate([own] + near, axis=1) if near else own, "core")
    return jnp.concatenate(near + [far], axis=1) if near else far


def return_keys(kept, sent):
    queries = kept.shape[1]
    count = lax.axis_size("rest")
    near = (count - 1) * queries
    back = swap(sent[:, near:], "core").astype(F32)
    total = kept + back[:, :queries]
    for k in range(1, count):
        part = sent[:, (k - 1) * queries : k * queries].astype(F32)
        part = part + back[:, k * queries : (k + 1) * queries]
        total = total + shift(part.astype(BF16), -k).astype(F32)
    return total


def pick(flag, one, two):
    return jnp.where(flag, one, two)


def gather_weight(block):
    core = lax.axis_index("core")
    quads = lax.axis_size("quad")
    part = block.shape[0] // (2 * quads)
    quad = lax.axis_index("quad")

    def cut(which):
        return lax.dynamic_slice_in_dim(block, (which * quads + quad) * part, part, 0)

    own = cut(core)
    came = swap(cut(1 - core), "core")
    first = pick(core == 0, own, came)
    second = pick(core == 0, came, own)
    return [
        lax.all_gather(item, ("side", "rest", "core", "quad"), axis=0, tiled=True)
        for item in (first, second)
    ]


def add(one, two):
    return (one.astype(F32) + two.astype(F32)).astype(one.dtype)


def cut_columns(left, which):
    shards = lax.axis_size("side") * lax.axis_size("rest")
    part = left.shape[1] // (2 * shards)
    return jnp.concatenate(
        [
            lax.dynamic_slice_in_dim(left, (2 * s + which) * part, part, 1)
            for s in range(shards)
        ],
        axis=1,
    )


def weight_halves(left, right):
    core = lax.axis_index("core")
    return [
        t_dot(cut_columns(left, which), right).astype(BF16) for which in (1 - core, core)
    ]


def side_parts(sent, kept):
    side = lax.axis_index("side")
    came = swap(sent, "core")
    half = kept.shape[0] // 2

    def cut(which):
        return add(
            lax.dynamic_slice_in_dim(kept, which * half, half, 0),
            lax.dynamic_slice_in_dim(came, which * half, half, 0),
        )

    return cut(1 - side), cut(side)


def side_sum(sent, kept):
    total = add(kept, swap(sent, "side"))
    if lax.axis_size("rest") > 1:
        total = lax.psum_scatter(total, "rest", scatter_dimension=0, tiled=True)
    return total


def line_sum(*items):
    return lax.psum(items, ("half", "quad"))


def join_cores(first, second):
    core = lax.axis_index("core")
    came = swap(pick(core == 0, second, first), "core")
    mine = pick(core == 0, first, second)
    return jnp.concatenate([pick(core == 0, mine, came), pick(core == 0, came, mine)], axis=0)


def swap_in(block):
    core, half = lax.axis_index("core"), lax.axis_index("half")
    micro, rows, wide = block.shape
    block = block.reshape(2, (micro // 2) * rows, wide)
    own = lax.dynamic_index_in_dim(block, half, 0, keepdims=False)
    other = lax.dynamic_index_in_dim(block, 1 - half, 0, keepdims=False)
    came = lax.ppermute(other, ("core", "half"), [(1, 2), (2, 1)])
    return pick(core == half, own, came)


def swap_out(first, second, micro):
    rows, wide = first.shape
    both = jnp.stack([first, second])
    both = lax.all_to_all(both, "core", 0, 0, tiled=True)
    both = lax.all_to_all(both, "half", 0, 0, tiled=True)
    return both.reshape(micro, 2 * rows // micro, wide)


def forward_layer(x, weights, clips, head, keep):
    joined, w_down, gains, shifts, b_qkv, b_out, b_down, b_up = weights
    grouped, normed_one = qkv_forward(x, gains[0:1], shifts[0:1], joined, b_qkv)
    own = to_clips(spread(grouped), clips)
    other = other_keys(own)
    att, log_total = attend_forward(own, other, head)
    att = spread(to_tokens(att))
    y, *kept = feed_forward(
        x, att, joined, b_out, gains[1:2], shifts[1:2], b_up, w_down, b_down, keep
    )
    return y, (x, normed_one, own, other, log_total, *kept)


def attention_grads(kept, d_att, clips, head, after):
    own, other, log_total = kept[2:5]
    d_heads = to_clips(spread(d_att), clips)
    dq, kept_kv, sent_kv = attend_backward(own, other, d_heads, log_total, head, after)
    dkv = return_keys(kept_kv, sent_kv).astype(BF16)
    return spread(to_tokens(jnp.concatenate([dq, dkv], axis=2)))


def backward_lean(kept, g, weights, clips, head):
    x, _, _, _, _, x1, _, slope, _, _ = kept
    joined, w_down, gains = weights[:3]
    _, dx1, _, d_att, _, _ = feed_backward(g, slope, w_down, joined, x1, gains[1:2])
    d_tokens = attention_grads(kept, d_att, clips, head, ())
    return qkv_backward(d_tokens, joined, x, dx1, gains[0:1])[0]


def small_rows(sums_one, sums_two, up_sum, shards, wide):
    rows = jnp.concatenate(
        [
            sums_one[0:1],
            sums_two[0:1],
            sums_one[1:2],
            sums_two[1:2],
            sums_one[2:4],
            sums_two[2:4],
        ]
    )
    rows = jnp.swapaxes(rows.reshape(8, shards, -1), 0, 1).reshape(shards, -1)
    packed = jnp.concatenate([rows, up_sum.reshape(shards, -1)], axis=1).astype(BF16)
    packed = packed.reshape(shards, 2, -1)
    lines = -(-packed.shape[2] // wide)
    room = 16 * (-(-lines // 16)) * wide
    packed = jnp.pad(packed, ((0, 0), (0, 0), (0, room - packed.shape[2])))
    return packed.reshape(shards, 2, -1, wide)


def beside(weight, rows):
    shards, _, wide = rows.shape
    return jnp.concatenate([weight.reshape(shards, -1, wide), rows], axis=1).reshape(-1, wide)


def qkv_halves(normed_one, flat, sums_one, sums_two, up_sum, shards):
    core = lax.axis_index("core")
    rows = small_rows(sums_one, sums_two, up_sum, shards, flat.shape[1])
    return [
        beside(item, lax.dynamic_index_in_dim(rows, which, 1, keepdims=False))
        for item, which in zip(weight_halves(normed_one, flat), (1 - core, core))
    ]


def backward_all(kept_first, kept_second, g, layers, clips, head, shards):
    x, normed_one, _, _, _, x1, normed_two, slope, lifted, att = kept_second
    joined, w_down, gains = layers[1][:3]
    d_upper, dx1, branch, d_att, sums_two, up_sum = feed_backward(
        g, slope, w_down, joined, x1, gains[1:2]
    )
    down = weight_halves(lifted, g)
    up = weight_halves(normed_two, d_upper)
    d_tokens = attention_grads(kept_second, d_att, clips, head, (*down, *up))
    down, up = side_parts(*down), side_parts(*up)
    out = weight_halves(att, branch)
    d_second, flat, sums_one = qkv_backward(
        d_tokens, joined, x, dx1, gains[0:1], (*down, *up, *out)
    )
    qkv = qkv_halves(normed_one, flat, sums_one, sums_two, up_sum, shards)

    x, normed_one, _, _, _, x1, normed_two, slope, lifted, att = kept_first
    joined, w_down, gains = layers[0][:3]
    d_upper, dx1, branch, d_att, sums_two, up_sum = feed_backward(
        d_second, slope, w_down, joined, x1, gains[1:2]
    )
    down_two = side_sum(*down)
    down_one = weight_halves(lifted, d_second)
    up_one = weight_halves(normed_two, d_upper)
    d_tokens = attention_grads(
        kept_first, d_att, clips, head, (*qkv, *down_one, *up_one, down_two)
    )
    (down_two,) = line_sum(down_two)
    up_two = side_sum(*up)
    out, qkv = side_parts(*out), side_parts(*qkv)
    down_one, up_one = side_parts(*down_one), side_parts(*up_one)
    out_one = weight_halves(att, branch)
    d_first, flat, sums_one = qkv_backward(
        d_tokens, joined, x, dx1, gains[0:1], (up_two, *out, *qkv, *down_one, *up_one, *out_one)
    )
    up_two, held = lax.optimization_barrier((up_two, down_two))
    (up_two,) = line_sum(up_two)
    qkv_one = qkv_halves(normed_one, flat, sums_one, sums_two, up_sum, shards)
    out_two, qkv_two, _ = lax.optimization_barrier((side_sum(*out), side_sum(*qkv), up_two))
    out_two, qkv_two = line_sum(out_two, qkv_two)
    out_one, qkv_one = side_parts(*out_one), side_parts(*qkv_one)
    down_one, up_one, _ = lax.optimization_barrier(
        (side_sum(*down_one), side_sum(*up_one), qkv_two)
    )
    down_one, up_one = line_sum(down_one, up_one)
    out_one, qkv_one, _ = lax.optimization_barrier((side_sum(*out_one), side_sum(*qkv_one), up_one))
    out_one, qkv_one = line_sum(out_one, qkv_one)
    firsts = (qkv_one, out_one, up_one, down_one)
    seconds = (qkv_two, out_two, up_two, down_two)
    return d_first, d_second, [join_cores(a, b) for a, b in zip(firsts, seconds)]


def gather_small(block):
    core, side = lax.axis_index("core"), lax.axis_index("side")
    if lax.axis_size("rest") > 1:
        whole_block = lax.all_gather(block, ("core", "side", "rest"), axis=0, tiled=False)
        return whole_block.reshape(2, -1, block.shape[0])
    came = swap(block, "side")
    layer = jnp.stack([pick(side == 0, block, came), pick(side == 0, came, block)])
    came = swap(layer, "core")
    return jnp.stack([pick(core == 0, layer, came), pick(core == 0, came, layer)])


def per_device(
    frames, out_grad, norm_gain, norm_bias, w_qkv, w_out, w_up, w_down, proj_bias, up_bias
):
    pairs = lax.axis_size("pair")
    pair = lax.axis_index("pair")
    shards = lax.axis_size("side") * lax.axis_size("rest")
    micro, _, width = frames.shape
    clips = micro // 2
    head = width // HEADS
    part = width // shards

    joined = gather_weight(jnp.concatenate([w_qkv[0], w_out[0], w_up[0]], axis=1))
    downs = gather_weight(w_down[0])
    small = jnp.concatenate(
        [norm_gain.reshape(-1), norm_bias.reshape(-1), proj_bias.reshape(-1), up_bias.reshape(-1)]
    )
    small = gather_small(small).astype(F32)
    rows = jnp.swapaxes(small[:, :, : 8 * part].reshape(2, shards, 8, part), 1, 2)
    rows = rows.reshape(2, 8, width)
    ups = small[:, :, 8 * part :].reshape(2, 1, -1)
    x_start = swap_in(frames)
    layers = []
    for layer in range(2):
        r = rows[layer]
        b_qkv = jnp.concatenate([r[4:5], jnp.zeros_like(r[4:5]), r[5:6]], axis=1)
        layers.append(
            (joined[layer], downs[layer], r[0:2], r[2:4], b_qkv, r[6:7], r[7:8], ups[layer])
        )

    x = x_start
    for phase in range(pairs):
        if phase > 0:
            came = lax.ppermute(second, "pair", [(i, i + 1) for i in range(pairs - 1)])
            x = pick(pair == 0, x_start, came)
        keep = phase == pairs - 1
        first, kept_first = forward_layer(x, layers[0], clips, head, keep)
        second, kept_second = forward_layer(first, layers[1], clips, head, keep)
    hidden = swap_out(first, second, micro)

    g_start = swap_in(out_grad)
    g = g_start
    for phase in range(pairs - 1):
        d_second = backward_lean(kept_second, g, layers[1], clips, head)
        d_first = backward_lean(kept_first, d_second, layers[0], clips, head)
        came = lax.ppermute(d_first, "pair", [(i + 1, i) for i in range(pairs - 1)])
        g = pick(pair == pairs - 1, g_start, came)
    d_first, d_second, (qkv, out, up, down) = backward_all(
        kept_first, kept_second, g, layers, clips, head, shards
    )
    input_grads = swap_out(d_first, d_second, micro)

    own_rows = part // 2
    qkv = qkv.reshape(2, -1, 3 * width).astype(F32)
    packed = qkv[:, own_rows:].reshape(2, -1)[:, : (8 * part + up_bias.shape[1]) // 2].reshape(-1)
    heads = packed[: 8 * part].reshape(8, part)
    qkv = qkv[:, :own_rows].reshape(-1, 3 * width)
    return (
        hidden[None],
        input_grads[None],
        heads[0:2][None],
        heads[2:4][None],
        qkv[None],
        out.astype(F32)[None],
        up.astype(F32)[None],
        down.astype(F32)[None],
        heads[4:8][None],
        packed[8 * part :][None],
    )


def solution(mesh):
    sections, groups, shards = (mesh.shape[name] for name in ("section", "seq", "shard"))
    cut = Mesh(
        mesh.devices.reshape(sections // 2, 2, 2, groups // 2, 2, shards // 2),
        AXES,
    )
    section, seq, shard = ("pair", "core"), ("half", "quad"), ("side", "rest")
    rows = seq + shard
    return jax.shard_map(
        per_device,
        mesh=cut,
        in_specs=(
            P(None, rows, None),
            P(None, rows, None),
            P(section, None, shard),
            P(section, None, shard),
            P(section, shard, None),
            P(section, shard, None),
            P(section, shard, None),
            P(section, shard, None),
            P(section, None, shard),
            P(section, shard),
        ),
        out_specs=(
            P(section, None, rows, None),
            P(section, None, rows, None),
            P(section, None, shard),
            P(section, None, shard),
            P(section, shard, None),
            P(section, shard, None),
            P(section, shard, None),
            P(section, shard, None),
            P(section, None, shard),
            P(section, shard),
        ),
        check_vma=False,
    )
```

```python
import math

import jax
import jax.numpy as jnp
from jax import lax
from jax.experimental import pallas as pl
from jax.experimental.pallas import tpu as pltpu
from jax.sharding import Mesh
from jax.sharding import PartitionSpec as P

HEADS = 12
norm_eps = 1e-05
F32 = jnp.float32
BF16 = jnp.bfloat16
VMEM_LIMIT = 56 * 1024 * 1024
AXES = ("pair", "core", "half", "quad", "side", "rest")
HEAD_GROUPS = 4


def call(body, out_shapes, grid=None, in_specs=None, out_specs=None, scratch=(), flops=0, moved=0):
    extra = {} if grid is None else dict(grid=grid, in_specs=in_specs, out_specs=out_specs)
    return pl.pallas_call(
        body,
        out_shape=out_shapes,
        scratch_shapes=scratch,
        compiler_params=pltpu.CompilerParams(vmem_limit_bytes=VMEM_LIMIT),
        cost_estimate=pl.CostEstimate(flops=flops, bytes_accessed=moved, transcendentals=0),
        **extra,
    )


def dot(left, right):
    return jnp.dot(left, right, preferred_element_type=F32)


def dot_t(left, right):
    return lax.dot_general(left, right, (((1,), (1,)), ((), ())), preferred_element_type=F32)


def t_dot(left, right):
    return lax.dot_general(left, right, (((0,), (0,)), ((), ())), preferred_element_type=F32)


def norm_parts(values):
    center = values - jnp.mean(values, axis=-1, keepdims=True)
    inverse = lax.rsqrt(jnp.mean(center * center, axis=-1, keepdims=True) + norm_eps)
    return center * inverse, inverse


def norm_back(upstream, scaled, inverse, gain_row):
    weighted = upstream * gain_row
    return inverse * (
        weighted
        - jnp.mean(weighted, axis=-1, keepdims=True)
        - scaled * jnp.mean(weighted * scaled, axis=-1, keepdims=True)
    )


def qkv_body(x_ref, gain_ref, shift_ref, w_ref, bias_ref, out_ref, normed_ref):
    @pl.when(pl.program_id(0) == 0)
    def _():
        scaled, _ = norm_parts(x_ref[...].astype(F32))
        normed_ref[...] = (scaled * gain_ref[...] + shift_ref[...]).astype(BF16)

    span = out_ref.shape[2] // 3
    piece = (dot(normed_ref[...], w_ref[...]) + bias_ref[...]).astype(BF16)
    for part in range(3):

        @pl.when(pl.program_id(0) == part)
        def _(part=part):
            for g in range(HEAD_GROUPS):
                out_ref[g, :, part * span : (part + 1) * span] = piece[:, g * span : (g + 1) * span]


def qkv_forward(x, gain, shift, joined, bias):
    rows, width = x.shape
    span = width // HEAD_GROUPS
    return call(
        qkv_body,
        (
            jax.ShapeDtypeStruct((HEAD_GROUPS, rows, 3 * span), BF16),
            jax.ShapeDtypeStruct((rows, width), BF16),
        ),
        grid=(3,),
        in_specs=[
            whole((rows, width)),
            whole((1, width)),
            whole((1, width)),
            pl.BlockSpec((width, width), lambda i: (0, i)),
            pl.BlockSpec((1, width), lambda i: (0, i)),
        ],
        out_specs=(whole((HEAD_GROUPS, rows, 3 * span)), whole((rows, width))),
        flops=2 * rows * width * 3 * width,
        moved=6 * width * width + 10 * x.size,
    )(x, gain, shift, joined, bias)


def key_chunks(own_ref, other_ref):
    place = 0
    for ref in (own_ref, other_ref):
        total = ref.shape[1]
        step = 256 if total % 256 == 0 else total
        for start in range(0, total, step):
            yield ref, start, place, step
            place += step


def attend_body(q_ref, own_ref, other_ref, out_ref, log_ref, score_ref, *, head):
    span = q_ref.shape[2] // 3
    queries = q_ref.shape[1]
    scale = 1.0 / math.sqrt(head)
    for h in range(span // head):
        q = q_ref[0, :, h * head : (h + 1) * head] * scale
        top = jnp.full((1, queries), -jnp.inf, F32)
        for ref, start, place, step in key_chunks(own_ref, other_ref):
            k = ref[0, start : start + step, span + h * head : span + (h + 1) * head]
            scores = dot_t(k, q)
            score_ref[place : place + step, :] = scores
            top = jnp.maximum(top, jnp.max(scores, axis=0, keepdims=True))
        total = jnp.zeros((1, queries), F32)
        acc = jnp.zeros((head, queries), F32)
        for ref, start, place, step in key_chunks(own_ref, other_ref):
            v = ref[0, start : start + step, 2 * span + h * head : 2 * span + (h + 1) * head]
            e = jnp.exp(score_ref[place : place + step, :] - top)
            total = total + jnp.sum(e, axis=0, keepdims=True)
            acc = acc + t_dot(v, e.astype(BF16))
        out_ref[0, :, h * head : (h + 1) * head] = jnp.transpose(acc / total).astype(BF16)
        log_ref[0, h : h + 1, :] = top + jnp.log(total)


def query_block(queries):
    return 256 if queries % 256 == 0 else queries


def attend_forward(own, other, head):
    clips, queries, wide = own.shape
    span = wide // 3
    keys = queries + other.shape[1]
    block = query_block(queries)

    def body(*refs):
        attend_body(*refs, head=head)

    return call(
        body,
        (
            jax.ShapeDtypeStruct((clips, queries, span), BF16),
            jax.ShapeDtypeStruct((clips, span // head, queries), F32),
        ),
        grid=(clips, queries // block),
        in_specs=[
            pl.BlockSpec((1, block, wide), lambda m, i: (m, i, 0)),
            pl.BlockSpec((1, queries, wide), lambda m, i: (m, 0, 0)),
            pl.BlockSpec((1, other.shape[1], wide), lambda m, i: (m, 0, 0)),
        ],
        out_specs=(
            pl.BlockSpec((1, block, span), lambda m, i: (m, i, 0)),
            pl.BlockSpec((1, span // head, block), lambda m, i: (m, 0, i)),
        ),
        scratch=[pltpu.VMEM((keys, block), F32)],
        flops=16 * clips * queries * keys * span,
        moved=4 * (own.size + other.size),
    )(own, own, other)


def attend_back_body(
    q_ref,
    own_ref,
    other_ref,
    grad_ref,
    log_ref,
    dq_ref,
    dkv_own_ref,
    dkv_other_ref,
    p_ref,
    dp_ref,
    dk_acc,
    dv_acc,
    *,
    head,
):
    span = q_ref.shape[2] // 3
    queries = q_ref.shape[1]
    heads = span // head
    scale = 1.0 / math.sqrt(head)

    @pl.when(pl.program_id(1) == 0)
    def _():
        dk_acc[...] = jnp.zeros_like(dk_acc)
        dv_acc[...] = jnp.zeros_like(dv_acc)

    for h in range(heads):
        q = q_ref[0, :, h * head : (h + 1) * head] * scale
        d_out = grad_ref[0, :, h * head : (h + 1) * head]
        log_total = log_ref[0, h : h + 1, :]
        row_term = jnp.zeros((1, queries), F32)
        for ref, start, place, step in key_chunks(own_ref, other_ref):
            k = ref[0, start : start + step, span + h * head : span + (h + 1) * head]
            v = ref[0, start : start + step, 2 * span + h * head : 2 * span + (h + 1) * head]
            probs = jnp.exp(dot_t(k, q) - log_total)
            d_probs = dot_t(v, d_out)
            p_ref[place : place + step, :] = probs
            dp_ref[place : place + step, :] = d_probs
            row_term = row_term + jnp.sum(probs * d_probs, axis=0, keepdims=True)
            dv_acc[h, place : place + step, :] += dot(probs.astype(BF16), d_out)
        dq = jnp.zeros((head, queries), F32)
        for ref, start, place, step in key_chunks(own_ref, other_ref):
            k = ref[0, start : start + step, span + h * head : span + (h + 1) * head]
            d_scores = (
                p_ref[place : place + step, :] * (dp_ref[place : place + step, :] - row_term)
            ).astype(BF16)
            dk_acc[h, place : place + step, :] += dot(d_scores, q)
            dq = dq + t_dot(k, d_scores)
        dq_ref[0, :, h * head : (h + 1) * head] = jnp.transpose(dq * scale).astype(BF16)

    @pl.when(pl.program_id(1) == pl.num_programs(1) - 1)
    def _():
        place = 0
        for ref in (dkv_own_ref, dkv_other_ref):
            rows = ref.shape[1]
            for h in range(heads):
                ref[0, :, h * head : (h + 1) * head] = dk_acc[h, place : place + rows, :].astype(
                    ref.dtype
                )
                ref[0, :, span + h * head : span + (h + 1) * head] = dv_acc[
                    h, place : place + rows, :
                ].astype(ref.dtype)
            place += rows


def attend_backward(own, other, grad, log_total, head, after=()):
    clips, queries, wide = own.shape
    span = wide // 3
    others = other.shape[1]
    keys = queries + others
    block = query_block(queries)
    heads = span // head

    def body(*refs):
        attend_back_body(*refs[:5], *refs[5 + len(after) :], head=head)

    return call(
        body,
        (
            jax.ShapeDtypeStruct((clips, queries, span), BF16),
            jax.ShapeDtypeStruct((clips, queries, 2 * span), F32),
            jax.ShapeDtypeStruct((clips, others, 2 * span), BF16),
        ),
        grid=(clips, queries // block),
        in_specs=[
            pl.BlockSpec((1, block, wide), lambda m, i: (m, i, 0)),
            pl.BlockSpec((1, queries, wide), lambda m, i: (m, 0, 0)),
            pl.BlockSpec((1, others, wide), lambda m, i: (m, 0, 0)),
            pl.BlockSpec((1, block, span), lambda m, i: (m, i, 0)),
            pl.BlockSpec((1, heads, block), lambda m, i: (m, 0, i)),
        ]
        + [pl.BlockSpec(memory_space=pl.ANY)] * len(after),
        out_specs=(
            pl.BlockSpec((1, block, span), lambda m, i: (m, i, 0)),
            pl.BlockSpec((1, queries, 2 * span), lambda m, i: (m, 0, 0)),
            pl.BlockSpec((1, others, 2 * span), lambda m, i: (m, 0, 0)),
        ),
        scratch=[
            pltpu.VMEM((keys, block), F32),
            pltpu.VMEM((keys, block), F32),
            pltpu.VMEM((heads, keys, head), F32),
            pltpu.VMEM((heads, keys, head), F32),
        ],
        flops=40 * clips * queries * keys * span,
        moved=8 * (own.size + other.size),
    )(own, own, other, grad, log_total, *after)


def feed_body(
    x_ref,
    att_ref,
    w_out_ref,
    b_out_ref,
    gain_ref,
    shift_ref,
    w_up_ref,
    b_up_ref,
    w_down_ref,
    b_down_ref,
    y_ref,
    *rest,
):
    if len(rest) > 2:
        x1_ref, normed_ref, slope_ref, lifted_ref, flat_ref, acc = rest
    else:
        normed_ref, acc = rest
    span = att_ref.shape[2]

    @pl.when(pl.program_id(0) == 0)
    def _():
        middle = x_ref[...].astype(F32) + b_out_ref[...]
        for g in range(HEAD_GROUPS):
            middle = middle + dot(att_ref[g], w_out_ref[g * span : (g + 1) * span, :])
            if len(rest) > 2:
                flat_ref[:, g * span : (g + 1) * span] = att_ref[g]
        if len(rest) > 2:
            x1_ref[...] = middle
        scaled, _ = norm_parts(middle)
        normed_ref[...] = (scaled * gain_ref[...] + shift_ref[...]).astype(BF16)
        acc[...] = middle + b_down_ref[...]

    upper = dot(normed_ref[...], w_up_ref[...]) + b_up_ref[...]
    phi = 0.5 * (1.0 + lax.erf(upper * math.sqrt(0.5)))
    lifted = (upper * phi).astype(BF16)
    if len(rest) > 2:
        density = jnp.exp(-0.5 * upper * upper) * (1.0 / math.sqrt(2.0 * math.pi))
        slope_ref[...] = phi + upper * density
        lifted_ref[...] = lifted
    acc[...] += dot(lifted, w_down_ref[...])

    @pl.when(pl.program_id(0) == pl.num_programs(0) - 1)
    def _():
        y_ref[...] = acc[...].astype(BF16)


def whole(shape):
    return pl.BlockSpec(shape, lambda i: (0,) * len(shape))


def feed_forward(x, att, joined, b_out, gain, shift, b_up, w_down, b_down, keep):
    rows, width = x.shape
    hidden = w_down.shape[0]
    row = whole((1, width))
    full = whole((rows, width))
    part = pl.BlockSpec((rows, width), lambda i: (0, i))
    shapes = [jax.ShapeDtypeStruct((rows, width), BF16)]
    specs = [full]
    scratch = [pltpu.VMEM((rows, width), F32)]
    if keep:
        shapes += [
            jax.ShapeDtypeStruct((rows, width), F32),
            jax.ShapeDtypeStruct((rows, width), BF16),
            jax.ShapeDtypeStruct((rows, hidden), F32),
            jax.ShapeDtypeStruct((rows, hidden), BF16),
            jax.ShapeDtypeStruct((rows, width), BF16),
        ]
        specs += [full, full, part, part, full]
    else:
        scratch = [pltpu.VMEM((rows, width), BF16)] + scratch
    return call(
        feed_body,
        tuple(shapes),
        grid=(hidden // width,),
        in_specs=[
            full,
            whole(att.shape),
            pl.BlockSpec((width, width), lambda i: (0, 3)),
            row,
            row,
            row,
            pl.BlockSpec((width, width), lambda i: (0, 4 + i)),
            pl.BlockSpec((1, width), lambda i: (0, i)),
            pl.BlockSpec((width, width), lambda i: (i, 0)),
            row,
        ],
        out_specs=tuple(specs),
        scratch=scratch,
        flops=2 * rows * width * (2 * hidden + width),
        moved=4 * w_down.size + 2 * width * width + 10 * rows * hidden,
    )(x, att, joined, b_out, gain, shift, joined, b_up, w_down, b_down)


def feed_back_body(
    g_ref,
    slope_ref,
    w_down_ref,
    w_up_ref,
    w_out_ref,
    x1_ref,
    gain_ref,
    d_upper_ref,
    dx1_ref,
    branch_ref,
    datt_ref,
    sums_ref,
    up_sum_ref,
    acc,
):
    @pl.when(pl.program_id(0) == 0)
    def _():
        acc[...] = jnp.zeros_like(acc)

    d_upper = (dot_t(g_ref[...], w_down_ref[...]) * slope_ref[...]).astype(BF16)
    d_upper_ref[...] = d_upper
    up_sum_ref[...] = jnp.sum(d_upper.astype(F32), axis=0, keepdims=True)
    acc[...] += dot_t(d_upper, w_up_ref[...])

    @pl.when(pl.program_id(0) == pl.num_programs(0) - 1)
    def _():
        d_normed = acc[...]
        upstream = g_ref[...].astype(F32)
        scaled, inverse = norm_parts(x1_ref[...])
        d_middle = upstream + norm_back(d_normed, scaled, inverse, gain_ref[...])
        dx1_ref[...] = d_middle
        branch = d_middle.astype(BF16)
        branch_ref[...] = branch
        span = datt_ref.shape[2]
        for g in range(HEAD_GROUPS):
            datt_ref[g] = dot_t(branch, w_out_ref[g * span : (g + 1) * span, :]).astype(BF16)
        sums_ref[0:1, :] = jnp.sum(d_normed * scaled, axis=0, keepdims=True)
        sums_ref[1:2, :] = jnp.sum(d_normed, axis=0, keepdims=True)
        sums_ref[2:3, :] = jnp.sum(branch.astype(F32), axis=0, keepdims=True)
        sums_ref[3:4, :] = jnp.sum(upstream, axis=0, keepdims=True)


def feed_backward(g, slope, w_down, joined, x1, gain):
    rows, width = g.shape
    hidden = w_down.shape[0]
    chunk = width
    full = whole((rows, width))
    return call(
        feed_back_body,
        (
            jax.ShapeDtypeStruct((rows, hidden), BF16),
            jax.ShapeDtypeStruct((rows, width), F32),
            jax.ShapeDtypeStruct((rows, width), BF16),
            jax.ShapeDtypeStruct((HEAD_GROUPS, rows, width // HEAD_GROUPS), BF16),
            jax.ShapeDtypeStruct((4, width), F32),
            jax.ShapeDtypeStruct((1, hidden), F32),
        ),
        grid=(hidden // chunk,),
        in_specs=[
            full,
            pl.BlockSpec((rows, chunk), lambda i: (0, i)),
            pl.BlockSpec((chunk, width), lambda i: (i, 0)),
            pl.BlockSpec((width, chunk), lambda i: (0, 4 + i)),
            pl.BlockSpec((width, width), lambda i: (0, 3)),
            full,
            whole((1, width)),
        ],
        out_specs=(
            pl.BlockSpec((rows, chunk), lambda i: (0, i)),
            full,
            full,
            whole((HEAD_GROUPS, rows, width // HEAD_GROUPS)),
            whole((4, width)),
            pl.BlockSpec((1, chunk), lambda i: (0, i)),
        ),
        scratch=[pltpu.VMEM((rows, width), F32)],
        flops=2 * rows * width * (2 * hidden + width),
        moved=4 * w_down.size + 2 * width * width + 6 * rows * hidden,
    )(g, slope, w_down, joined, joined, x1, gain)


def qkv_back_body(
    grads_ref, w_ref, x_ref, dx1_ref, gain_ref, dx_ref, flat_ref, sums_ref, acc
):
    width = x_ref.shape[1]
    span = grads_ref.shape[2] // 3
    step = pl.program_id(0)
    for part in range(3):

        @pl.when(step == part)
        def _(part=part):
            cols = slice(part * width, (part + 1) * width)
            for g in range(HEAD_GROUPS):
                flat_ref[:, part * width + g * span : part * width + (g + 1) * span] = grads_ref[
                    g, :, part * span : (part + 1) * span
                ]
            came = dot_t(flat_ref[:, cols], w_ref[...])
            acc[...] = came if part == 0 else acc[...] + came

    @pl.when(step == 2)
    def _():
        d_normed = acc[...]
        scaled, inverse = norm_parts(x_ref[...].astype(F32))
        dx = dx1_ref[...] + norm_back(d_normed, scaled, inverse, gain_ref[...])
        dx_ref[...] = dx.astype(BF16)
        sums_ref[0:1, :] = jnp.sum(d_normed * scaled, axis=0, keepdims=True)
        sums_ref[1:2, :] = jnp.sum(d_normed, axis=0, keepdims=True)
        sums_ref[2:3, :] = jnp.sum(flat_ref[:, :width].astype(F32), axis=0, keepdims=True)
        sums_ref[3:4, :] = jnp.sum(flat_ref[:, 2 * width :].astype(F32), axis=0, keepdims=True)


def qkv_backward(grads, joined, x, dx1, gain, after=()):
    rows, width = x.shape

    def body(*refs):
        qkv_back_body(*refs[:5], *refs[5 + len(after) :])

    return call(
        body,
        (
            jax.ShapeDtypeStruct((rows, width), BF16),
            jax.ShapeDtypeStruct((rows, 3 * width), BF16),
            jax.ShapeDtypeStruct((4, width), F32),
        ),
        grid=(3,),
        in_specs=[
            whole(grads.shape),
            pl.BlockSpec((width, width), lambda i: (0, i)),
            whole((rows, width)),
            whole((rows, width)),
            whole((1, width)),
        ]
        + [pl.BlockSpec(memory_space=pl.ANY)] * len(after),
        out_specs=(whole((rows, width)), whole((rows, 3 * width)), whole((4, width))),
        scratch=[pltpu.VMEM((rows, width), F32)],
        flops=2 * rows * width * 3 * width,
        moved=6 * width * width + 20 * x.size,
    )(grads, joined, x, dx1, gain, *after)


def add_body(one_ref, two_ref, *rest):
    rest[-1][...] = (one_ref[...].astype(F32) + two_ref[...].astype(F32)).astype(BF16)


def add_after(one, two, after):
    rows, wide = one.shape
    block = next((n for n in (256, 208, 192, 128, 96, 64, 48) if rows % n == 0), rows)
    spec = pl.BlockSpec((block, wide), lambda i: (i, 0))
    return call(
        add_body,
        jax.ShapeDtypeStruct((rows, wide), BF16),
        grid=(rows // block,),
        in_specs=[spec, spec] + [pl.BlockSpec(memory_space=pl.ANY)] * len(after),
        out_specs=spec,
        flops=one.size,
        moved=6 * one.size,
    )(one, two, *after)


def swap(block, axis):
    return lax.ppermute(block, axis, [(0, 1), (1, 0)])


def shift(block, distance):
    count = lax.axis_size("rest")
    return lax.ppermute(block, "rest", [(i, (i + distance) % count) for i in range(count)])


def spread(block):
    return lax.all_to_all(block, ("quad", "side"), 0, 0, tiled=True)


def to_clips(block, clips):
    groups, rows, wide = block.shape
    if clips == 1:
        return block.reshape(1, groups * rows, wide)
    block = block.reshape(groups, clips, rows // clips, wide)
    return jnp.swapaxes(block, 0, 1).reshape(clips, groups * (rows // clips), wide)


def to_tokens(block):
    clips, rows, wide = block.shape
    if clips == 1:
        return block.reshape(HEAD_GROUPS, rows // HEAD_GROUPS, wide)
    block = block.reshape(clips, HEAD_GROUPS, rows // HEAD_GROUPS, wide)
    return jnp.swapaxes(block, 0, 1).reshape(HEAD_GROUPS, -1, wide)


def other_keys(own):
    near = [shift(own, k) for k in range(1, lax.axis_size("rest"))]
    far = swap(jnp.concatenate([own] + near, axis=1) if near else own, "core")
    return jnp.concatenate(near + [far], axis=1) if near else far


def return_keys(kept, sent):
    queries = kept.shape[1]
    count = lax.axis_size("rest")
    near = (count - 1) * queries
    back = swap(sent[:, near:], "core").astype(F32)
    total = kept + back[:, :queries]
    for k in range(1, count):
        part = sent[:, (k - 1) * queries : k * queries].astype(F32)
        part = part + back[:, k * queries : (k + 1) * queries]
        total = total + shift(part.astype(BF16), -k).astype(F32)
    return total


def pick(flag, one, two):
    return jnp.where(flag, one, two)


def gather_weight(*blocks):
    core = lax.axis_index("core")
    quads = lax.axis_size("quad")
    part = blocks[0].shape[0] // (2 * quads)
    quad = lax.axis_index("quad")

    def cut(which):
        start = (which * quads + quad) * part
        return jnp.concatenate(
            [lax.dynamic_slice_in_dim(block, start, part, 0) for block in blocks], axis=1
        )

    own = cut(core)
    came = swap(cut(1 - core), "core")
    first = pick(core == 0, own, came)
    second = pick(core == 0, came, own)
    return [
        lax.all_gather(item, ("side", "rest", "core", "quad"), axis=0, tiled=True)
        for item in (first, second)
    ]


def in_order(second, mine, other):
    return pick(second, other, mine), pick(second, mine, other)


def gather_by_swaps(block):
    if lax.axis_size("rest") > 1 or lax.axis_size("quad") != 2:
        return gather_weight(block)
    core, quad, side = (lax.axis_index(name) for name in ("core", "quad", "side"))
    part = block.shape[0] // 4
    layers = in_order(core == 1, block, swap(block, "core"))
    start = (core * 2 + quad) * part
    near = jnp.stack([lax.dynamic_slice_in_dim(item, start, part, 0) for item in layers])
    near = swap(near, "side")
    both = jnp.stack([near, swap(near, "quad")])
    far = swap(both, "core")
    here = in_order(quad == 1, both[0], both[1])
    there = in_order(quad == 1, far[0], far[1])
    rows = [
        *(pick(core == 1, b, a) for a, b in zip(here, there)),
        *(pick(core == 1, a, b) for a, b in zip(here, there)),
    ]
    result = []
    for layer in range(2):
        other = jnp.concatenate([row[layer] for row in rows], axis=0)
        result.append(jnp.concatenate(in_order(side == 1, layers[layer], other), axis=0))
    return result


def add(one, two):
    return (one.astype(F32) + two.astype(F32)).astype(one.dtype)


def cut_columns(left, which):
    shards = lax.axis_size("side") * lax.axis_size("rest")
    part = left.shape[1] // (2 * shards)
    return jnp.concatenate(
        [
            lax.dynamic_slice_in_dim(left, (2 * s + which) * part, part, 1)
            for s in range(shards)
        ],
        axis=1,
    )


def weight_halves(left, right):
    core = lax.axis_index("core")
    return [
        t_dot(cut_columns(left, which), right).astype(BF16) for which in (1 - core, core)
    ]


def side_parts(sent, kept):
    side = lax.axis_index("side")
    came = swap(sent, "core")
    half = kept.shape[0] // 2

    def cut(which):
        return add(
            lax.dynamic_slice_in_dim(kept, which * half, half, 0),
            lax.dynamic_slice_in_dim(came, which * half, half, 0),
        )

    return cut(1 - side), cut(side)


def side_sum(sent, kept, *after):
    total = add_after(kept, swap(sent, "side"), after)
    if lax.axis_size("rest") > 1:
        total = lax.psum_scatter(total, "rest", scatter_dimension=0, tiled=True)
    return total


def line_sum(*items, turned=False):
    return lax.psum(items, ("quad", "half") if turned else ("half", "quad"))


def join_cores(first, second):
    core = lax.axis_index("core")
    came = swap(pick(core == 0, second, first), "core")
    mine = pick(core == 0, first, second)
    return jnp.concatenate([pick(core == 0, mine, came), pick(core == 0, came, mine)], axis=0)


def swap_in(block):
    core, half = lax.axis_index("core"), lax.axis_index("half")
    micro, rows, wide = block.shape
    block = block.reshape(2, (micro // 2) * rows, wide)
    own = lax.dynamic_index_in_dim(block, half, 0, keepdims=False)
    other = lax.dynamic_index_in_dim(block, 1 - half, 0, keepdims=False)
    came = lax.ppermute(other, ("core", "half"), [(1, 2), (2, 1)])
    return pick(core == half, own, came)


def swap_out(first, second, micro):
    rows, wide = first.shape
    second_core, second_half = lax.axis_index("core") == 1, lax.axis_index("half") == 1
    mine, sent = in_order(second_core, first, second)
    parts = in_order(second_core, mine, swap(sent, "core"))
    mine, sent = in_order(second_half, *parts)
    clips = in_order(second_half, mine, swap(sent, "half"))
    return jnp.stack(clips).reshape(micro, 2 * rows // micro, wide)


def forward_layer(x, weights, clips, head, keep):
    joined, w_down, gains, shifts, b_qkv, b_out, b_down, b_up = weights
    grouped, normed_one = qkv_forward(x, gains[0:1], shifts[0:1], joined, b_qkv)
    own = to_clips(spread(grouped), clips)
    other = other_keys(own)
    att, log_total = attend_forward(own, other, head)
    att = spread(to_tokens(att))
    y, *kept = feed_forward(
        x, att, joined, b_out, gains[1:2], shifts[1:2], b_up, w_down, b_down, keep
    )
    return y, (x, normed_one, own, other, log_total, *kept)


def attention_grads(kept, d_att, clips, head, after):
    own, other, log_total = kept[2:5]
    d_heads = to_clips(spread(d_att), clips)
    dq, kept_kv, sent_kv = attend_backward(own, other, d_heads, log_total, head, after)
    dkv = return_keys(kept_kv, sent_kv).astype(BF16)
    return spread(to_tokens(jnp.concatenate([dq, dkv], axis=2))), dq


def backward_lean(kept, g, weights, clips, head):
    x, _, _, _, _, x1, _, slope, _, _ = kept
    joined, w_down, gains = weights[:3]
    _, dx1, _, d_att, _, _ = feed_backward(g, slope, w_down, joined, x1, gains[1:2])
    d_tokens, _ = attention_grads(kept, d_att, clips, head, ())
    return qkv_backward(d_tokens, joined, x, dx1, gains[0:1])[0]


def small_rows(sums_one, sums_two, up_sum, shards, wide):
    rows = jnp.concatenate(
        [
            sums_one[0:1],
            sums_two[0:1],
            sums_one[1:2],
            sums_two[1:2],
            sums_one[2:4],
            sums_two[2:4],
        ]
    )
    rows = jnp.swapaxes(rows.reshape(8, shards, -1), 0, 1).reshape(shards, -1)
    packed = jnp.concatenate([rows, up_sum.reshape(shards, -1)], axis=1).astype(BF16)
    packed = packed.reshape(shards, 2, -1)
    lines = -(-packed.shape[2] // wide)
    room = 16 * (-(-lines // 16)) * wide
    packed = jnp.pad(packed, ((0, 0), (0, 0), (0, room - packed.shape[2])))
    return packed.reshape(shards, 2, -1, wide)


def beside(weight, rows):
    shards, _, wide = rows.shape
    return jnp.concatenate([weight.reshape(shards, -1, wide), rows], axis=1).reshape(-1, wide)


def qkv_halves(normed_one, flat, sums_one, sums_two, up_sum, shards):
    core = lax.axis_index("core")
    rows = small_rows(sums_one, sums_two, up_sum, shards, flat.shape[1])
    return [
        beside(item, lax.dynamic_index_in_dim(rows, which, 1, keepdims=False))
        for item, which in zip(weight_halves(normed_one, flat), (1 - core, core))
    ]


def backward_all(kept_first, kept_second, g, layers, clips, head, shards):
    x, normed_one, _, _, _, x1, normed_two, slope, lifted, att = kept_second
    joined, w_down, gains = layers[1][:3]
    d_upper, dx1, branch, d_att, sums_two, up_sum = feed_backward(
        g, slope, w_down, joined, x1, gains[1:2]
    )
    down = weight_halves(lifted, g)
    up = weight_halves(normed_two, d_upper)
    d_tokens, _ = attention_grads(kept_second, d_att, clips, head, (*down, *up))
    down, up = side_parts(*down), side_parts(*up)
    out = weight_halves(att, branch)
    d_second, flat, sums_one = qkv_backward(
        d_tokens, joined, x, dx1, gains[0:1], (*down, *up, *out)
    )
    qkv = qkv_halves(normed_one, flat, sums_one, sums_two, up_sum, shards)

    x, normed_one, _, _, _, x1, normed_two, slope, lifted, att = kept_first
    joined, w_down, gains = layers[0][:3]
    d_upper, dx1, branch, d_att, sums_two, up_sum = feed_backward(
        d_second, slope, w_down, joined, x1, gains[1:2]
    )
    down_one = weight_halves(lifted, d_second)
    up_one = weight_halves(normed_two, d_upper)
    d_tokens, marker = attention_grads(
        kept_first, d_att, clips, head, (*qkv, *down_one, *up_one)
    )
    down_two, up_two = side_sum(*down, marker), side_sum(*up, marker)
    out, qkv = side_parts(*out), side_parts(*qkv)
    down_one, up_one = side_parts(*down_one), side_parts(*up_one)
    out_one = weight_halves(att, branch)
    d_first, flat, sums_one = qkv_backward(
        d_tokens,
        joined,
        x,
        dx1,
        gains[0:1],
        (down_two, up_two, *out, *qkv, *down_one, *up_one, *out_one),
    )
    down_two, up_two = line_sum(down_two, up_two)
    qkv_one = qkv_halves(normed_one, flat, sums_one, sums_two, up_sum, shards)
    out_two, qkv_two = side_sum(*out, *qkv_one), side_sum(*qkv, *qkv_one)
    out_one, qkv_one = side_parts(*out_one), side_parts(*qkv_one)
    out_two, qkv_two = line_sum(out_two, qkv_two, turned=True)
    late = (down_two, up_two, out_one[0], qkv_one[0])
    down_one, up_one = side_sum(*down_one, *late), side_sum(*up_one, *late)
    down_one, up_one = line_sum(down_one, up_one)
    late = (out_two, qkv_two)
    out_one, qkv_one = side_sum(*out_one, *late), side_sum(*qkv_one, *late)
    out_one, qkv_one = line_sum(out_one, qkv_one, turned=True)
    firsts = (qkv_one, out_one, up_one, down_one)
    seconds = (qkv_two, out_two, up_two, down_two)
    return d_first, d_second, [join_cores(a, b) for a, b in zip(firsts, seconds)]


def gather_small(block):
    core, side = lax.axis_index("core"), lax.axis_index("side")
    if lax.axis_size("rest") > 1:
        whole_block = lax.all_gather(block, ("core", "side", "rest"), axis=0, tiled=False)
        return whole_block.reshape(2, -1, block.shape[0])
    came = swap(block, "side")
    layer = jnp.stack([pick(side == 0, block, came), pick(side == 0, came, block)])
    came = swap(layer, "core")
    return jnp.stack([pick(core == 0, layer, came), pick(core == 0, came, layer)])


def per_device(
    frames, out_grad, norm_gain, norm_bias, w_qkv, w_out, w_up, w_down, proj_bias, up_bias
):
    pairs = lax.axis_size("pair")
    pair = lax.axis_index("pair")
    shards = lax.axis_size("side") * lax.axis_size("rest")
    micro, _, width = frames.shape
    clips = micro // 2
    head = width // HEADS
    part = width // shards

    joined = gather_weight(w_qkv[0], w_out[0], w_up[0])
    downs = gather_by_swaps(w_down[0])
    small = jnp.concatenate(
        [norm_gain.reshape(-1), norm_bias.reshape(-1), proj_bias.reshape(-1), up_bias.reshape(-1)]
    )
    small = gather_small(small).astype(F32)
    rows = jnp.swapaxes(small[:, :, : 8 * part].reshape(2, shards, 8, part), 1, 2)
    rows = rows.reshape(2, 8, width)
    ups = small[:, :, 8 * part :].reshape(2, 1, -1)
    x_start = swap_in(frames)
    layers = []
    for layer in range(2):
        r = rows[layer]
        b_qkv = jnp.concatenate([r[4:5], jnp.zeros_like(r[4:5]), r[5:6]], axis=1)
        layers.append(
            (joined[layer], downs[layer], r[0:2], r[2:4], b_qkv, r[6:7], r[7:8], ups[layer])
        )

    x = x_start
    for phase in range(pairs):
        if phase > 0:
            came = lax.ppermute(second, "pair", [(i, i + 1) for i in range(pairs - 1)])
            x = pick(pair == 0, x_start, came)
        keep = phase == pairs - 1
        first, kept_first = forward_layer(x, layers[0], clips, head, keep)
        second, kept_second = forward_layer(first, layers[1], clips, head, keep)
    hidden = swap_out(first, second, micro)

    g_start = swap_in(out_grad)
    g = g_start
    for phase in range(pairs - 1):
        d_second = backward_lean(kept_second, g, layers[1], clips, head)
        d_first = backward_lean(kept_first, d_second, layers[0], clips, head)
        came = lax.ppermute(d_first, "pair", [(i + 1, i) for i in range(pairs - 1)])
        g = pick(pair == pairs - 1, g_start, came)
    d_first, d_second, (qkv, out, up, down) = backward_all(
        kept_first, kept_second, g, layers, clips, head, shards
    )
    input_grads = swap_out(d_first, d_second, micro)

    own_rows = part // 2
    qkv = qkv.reshape(2, -1, 3 * width).astype(F32)
    packed = qkv[:, own_rows:].reshape(2, -1)[:, : (8 * part + up_bias.shape[1]) // 2].reshape(-1)
    heads = packed[: 8 * part].reshape(8, part)
    qkv = qkv[:, :own_rows].reshape(-1, 3 * width)
    return (
        hidden[None],
        input_grads[None],
        heads[0:2][None],
        heads[2:4][None],
        qkv[None],
        out.astype(F32)[None],
        up.astype(F32)[None],
        down.astype(F32)[None],
        heads[4:8][None],
        packed[8 * part :][None],
    )


def solution(mesh):
    sections, groups, shards = (mesh.shape[name] for name in ("section", "seq", "shard"))
    cut = Mesh(
        mesh.devices.reshape(sections // 2, 2, 2, groups // 2, 2, shards // 2),
        AXES,
    )
    section, seq, shard = ("pair", "core"), ("half", "quad"), ("side", "rest")
    rows = seq + shard
    return jax.shard_map(
        per_device,
        mesh=cut,
        in_specs=(
            P(None, rows, None),
            P(None, rows, None),
            P(section, None, shard),
            P(section, None, shard),
            P(section, shard, None),
            P(section, shard, None),
            P(section, shard, None),
            P(section, shard, None),
            P(section, None, shard),
            P(section, shard),
        ),
        out_specs=(
            P(section, None, rows, None),
            P(section, None, rows, None),
            P(section, None, shard),
            P(section, None, shard),
            P(section, shard, None),
            P(section, shard, None),
            P(section, shard, None),
            P(section, shard, None),
            P(section, None, shard),
            P(section, shard),
        ),
        check_vma=False,
    )
```

```python
import math

import jax
import jax.numpy as jnp
from jax import lax
from jax.experimental import pallas as pl
from jax.experimental.pallas import tpu as pltpu
from jax.sharding import Mesh
from jax.sharding import PartitionSpec as P

HEADS = 12
norm_eps = 1e-05
F32 = jnp.float32
BF16 = jnp.bfloat16
VMEM_LIMIT = 56 * 1024 * 1024
AXES = ("pair", "core", "half", "quad", "side", "rest")
HEAD_GROUPS = 4


def call(body, out_shapes, grid=None, in_specs=None, out_specs=None, scratch=(), flops=0, moved=0):
    extra = {} if grid is None else dict(grid=grid, in_specs=in_specs, out_specs=out_specs)
    return pl.pallas_call(
        body,
        out_shape=out_shapes,
        scratch_shapes=scratch,
        compiler_params=pltpu.CompilerParams(vmem_limit_bytes=VMEM_LIMIT),
        cost_estimate=pl.CostEstimate(flops=flops, bytes_accessed=moved, transcendentals=0),
        **extra,
    )


def dot(left, right):
    return jnp.dot(left, right, preferred_element_type=F32)


def dot_t(left, right):
    return lax.dot_general(left, right, (((1,), (1,)), ((), ())), preferred_element_type=F32)


def t_dot(left, right):
    return lax.dot_general(left, right, (((0,), (0,)), ((), ())), preferred_element_type=F32)


def norm_parts(values):
    center = values - jnp.mean(values, axis=-1, keepdims=True)
    inverse = lax.rsqrt(jnp.mean(center * center, axis=-1, keepdims=True) + norm_eps)
    return center * inverse, inverse


def norm_back(upstream, scaled, inverse, gain_row):
    weighted = upstream * gain_row
    return inverse * (
        weighted
        - jnp.mean(weighted, axis=-1, keepdims=True)
        - scaled * jnp.mean(weighted * scaled, axis=-1, keepdims=True)
    )


def qkv_body(x_ref, gain_ref, shift_ref, w_ref, bias_ref, out_ref, normed_ref):
    @pl.when(pl.program_id(0) == 0)
    def _():
        scaled, _ = norm_parts(x_ref[...].astype(F32))
        normed_ref[...] = (scaled * gain_ref[...] + shift_ref[...]).astype(BF16)

    span = out_ref.shape[2] // 3
    piece = (dot(normed_ref[...], w_ref[...]) + bias_ref[...]).astype(BF16)
    for part in range(3):

        @pl.when(pl.program_id(0) == part)
        def _(part=part):
            for g in range(HEAD_GROUPS):
                out_ref[g, :, part * span : (part + 1) * span] = piece[:, g * span : (g + 1) * span]


def qkv_forward(x, gain, shift, joined, bias):
    rows, width = x.shape
    span = width // HEAD_GROUPS
    return call(
        qkv_body,
        (
            jax.ShapeDtypeStruct((HEAD_GROUPS, rows, 3 * span), BF16),
            jax.ShapeDtypeStruct((rows, width), BF16),
        ),
        grid=(3,),
        in_specs=[
            whole((rows, width)),
            whole((1, width)),
            whole((1, width)),
            pl.BlockSpec((width, width), lambda i: (0, i)),
            pl.BlockSpec((1, width), lambda i: (0, i)),
        ],
        out_specs=(whole((HEAD_GROUPS, rows, 3 * span)), whole((rows, width))),
        flops=2 * rows * width * 3 * width,
        moved=6 * width * width + 10 * x.size,
    )(x, gain, shift, joined, bias)


def key_chunks(own_ref, other_ref):
    place = 0
    for ref in (own_ref, other_ref):
        total = ref.shape[1]
        step = 256 if total % 256 == 0 else total
        for start in range(0, total, step):
            yield ref, start, place, step
            place += step


def attend_body(q_ref, own_ref, other_ref, out_ref, log_ref, score_ref, *, head):
    span = q_ref.shape[2] // 3
    queries = q_ref.shape[1]
    scale = 1.0 / math.sqrt(head)
    for h in range(span // head):
        q = q_ref[0, :, h * head : (h + 1) * head] * scale
        top = jnp.full((1, queries), -jnp.inf, F32)
        for ref, start, place, step in key_chunks(own_ref, other_ref):
            k = ref[0, start : start + step, span + h * head : span + (h + 1) * head]
            scores = dot_t(k, q)
            score_ref[place : place + step, :] = scores
            top = jnp.maximum(top, jnp.max(scores, axis=0, keepdims=True))
        total = jnp.zeros((1, queries), F32)
        acc = jnp.zeros((head, queries), F32)
        for ref, start, place, step in key_chunks(own_ref, other_ref):
            v = ref[0, start : start + step, 2 * span + h * head : 2 * span + (h + 1) * head]
            e = jnp.exp(score_ref[place : place + step, :] - top)
            total = total + jnp.sum(e, axis=0, keepdims=True)
            acc = acc + t_dot(v, e.astype(BF16))
        out_ref[0, :, h * head : (h + 1) * head] = jnp.transpose(acc / total).astype(BF16)
        log_ref[0, h : h + 1, :] = top + jnp.log(total)


def query_block(queries):
    return 256 if queries % 256 == 0 else queries


def attend_forward(own, other, head):
    clips, queries, wide = own.shape
    span = wide // 3
    keys = queries + other.shape[1]
    block = query_block(queries)

    def body(*refs):
        attend_body(*refs, head=head)

    return call(
        body,
        (
            jax.ShapeDtypeStruct((clips, queries, span), BF16),
            jax.ShapeDtypeStruct((clips, span // head, queries), F32),
        ),
        grid=(clips, queries // block),
        in_specs=[
            pl.BlockSpec((1, block, wide), lambda m, i: (m, i, 0)),
            pl.BlockSpec((1, queries, wide), lambda m, i: (m, 0, 0)),
            pl.BlockSpec((1, other.shape[1], wide), lambda m, i: (m, 0, 0)),
        ],
        out_specs=(
            pl.BlockSpec((1, block, span), lambda m, i: (m, i, 0)),
            pl.BlockSpec((1, span // head, block), lambda m, i: (m, 0, i)),
        ),
        scratch=[pltpu.VMEM((keys, block), F32)],
        flops=16 * clips * queries * keys * span,
        moved=4 * (own.size + other.size),
    )(own, own, other)


def attend_back_body(
    q_ref,
    own_ref,
    other_ref,
    grad_ref,
    log_ref,
    dq_ref,
    dkv_own_ref,
    dkv_other_ref,
    p_ref,
    dp_ref,
    dk_acc,
    dv_acc,
    *,
    head,
):
    span = q_ref.shape[2] // 3
    queries = q_ref.shape[1]
    heads = span // head
    scale = 1.0 / math.sqrt(head)

    @pl.when(pl.program_id(1) == 0)
    def _():
        dk_acc[...] = jnp.zeros_like(dk_acc)
        dv_acc[...] = jnp.zeros_like(dv_acc)

    for h in range(heads):
        q = q_ref[0, :, h * head : (h + 1) * head] * scale
        d_out = grad_ref[0, :, h * head : (h + 1) * head]
        log_total = log_ref[0, h : h + 1, :]
        row_term = jnp.zeros((1, queries), F32)
        for ref, start, place, step in key_chunks(own_ref, other_ref):
            k = ref[0, start : start + step, span + h * head : span + (h + 1) * head]
            v = ref[0, start : start + step, 2 * span + h * head : 2 * span + (h + 1) * head]
            probs = jnp.exp(dot_t(k, q) - log_total)
            d_probs = dot_t(v, d_out)
            p_ref[place : place + step, :] = probs
            dp_ref[place : place + step, :] = d_probs
            row_term = row_term + jnp.sum(probs * d_probs, axis=0, keepdims=True)
            dv_acc[h, place : place + step, :] += dot(probs.astype(BF16), d_out)
        dq = jnp.zeros((head, queries), F32)
        for ref, start, place, step in key_chunks(own_ref, other_ref):
            k = ref[0, start : start + step, span + h * head : span + (h + 1) * head]
            d_scores = (
                p_ref[place : place + step, :] * (dp_ref[place : place + step, :] - row_term)
            ).astype(BF16)
            dk_acc[h, place : place + step, :] += dot(d_scores, q)
            dq = dq + t_dot(k, d_scores)
        dq_ref[0, :, h * head : (h + 1) * head] = jnp.transpose(dq * scale).astype(BF16)

    @pl.when(pl.program_id(1) == pl.num_programs(1) - 1)
    def _():
        place = 0
        for ref in (dkv_own_ref, dkv_other_ref):
            rows = ref.shape[1]
            for h in range(heads):
                ref[0, :, h * head : (h + 1) * head] = dk_acc[h, place : place + rows, :].astype(
                    ref.dtype
                )
                ref[0, :, span + h * head : span + (h + 1) * head] = dv_acc[
                    h, place : place + rows, :
                ].astype(ref.dtype)
            place += rows


def attend_backward(own, other, grad, log_total, head, after=()):
    clips, queries, wide = own.shape
    span = wide // 3
    others = other.shape[1]
    keys = queries + others
    block = query_block(queries)
    heads = span // head

    def body(*refs):
        attend_back_body(*refs[:5], *refs[5 + len(after) :], head=head)

    return call(
        body,
        (
            jax.ShapeDtypeStruct((clips, queries, span), BF16),
            jax.ShapeDtypeStruct((clips, queries, 2 * span), F32),
            jax.ShapeDtypeStruct((clips, others, 2 * span), BF16),
        ),
        grid=(clips, queries // block),
        in_specs=[
            pl.BlockSpec((1, block, wide), lambda m, i: (m, i, 0)),
            pl.BlockSpec((1, queries, wide), lambda m, i: (m, 0, 0)),
            pl.BlockSpec((1, others, wide), lambda m, i: (m, 0, 0)),
            pl.BlockSpec((1, block, span), lambda m, i: (m, i, 0)),
            pl.BlockSpec((1, heads, block), lambda m, i: (m, 0, i)),
        ]
        + [pl.BlockSpec(memory_space=pl.ANY)] * len(after),
        out_specs=(
            pl.BlockSpec((1, block, span), lambda m, i: (m, i, 0)),
            pl.BlockSpec((1, queries, 2 * span), lambda m, i: (m, 0, 0)),
            pl.BlockSpec((1, others, 2 * span), lambda m, i: (m, 0, 0)),
        ),
        scratch=[
            pltpu.VMEM((keys, block), F32),
            pltpu.VMEM((keys, block), F32),
            pltpu.VMEM((heads, keys, head), F32),
            pltpu.VMEM((heads, keys, head), F32),
        ],
        flops=40 * clips * queries * keys * span,
        moved=8 * (own.size + other.size),
    )(own, own, other, grad, log_total, *after)


def feed_body(
    x_ref,
    att_ref,
    w_out_ref,
    b_out_ref,
    gain_ref,
    shift_ref,
    w_up_ref,
    b_up_ref,
    w_down_ref,
    b_down_ref,
    y_ref,
    *rest,
):
    if len(rest) > 2:
        x1_ref, normed_ref, slope_ref, lifted_ref, flat_ref, acc = rest
    else:
        normed_ref, acc = rest
    span = att_ref.shape[2]

    @pl.when(pl.program_id(0) == 0)
    def _():
        middle = x_ref[...].astype(F32) + b_out_ref[...]
        for g in range(HEAD_GROUPS):
            middle = middle + dot(att_ref[g], w_out_ref[g * span : (g + 1) * span, :])
            if len(rest) > 2:
                flat_ref[:, g * span : (g + 1) * span] = att_ref[g]
        if len(rest) > 2:
            x1_ref[...] = middle
        scaled, _ = norm_parts(middle)
        normed_ref[...] = (scaled * gain_ref[...] + shift_ref[...]).astype(BF16)
        acc[...] = middle + b_down_ref[...]

    upper = dot(normed_ref[...], w_up_ref[...]) + b_up_ref[...]
    phi = 0.5 * (1.0 + lax.erf(upper * math.sqrt(0.5)))
    lifted = (upper * phi).astype(BF16)
    if len(rest) > 2:
        density = jnp.exp(-0.5 * upper * upper) * (1.0 / math.sqrt(2.0 * math.pi))
        slope_ref[...] = phi + upper * density
        lifted_ref[...] = lifted
    acc[...] += dot(lifted, w_down_ref[...])

    @pl.when(pl.program_id(0) == pl.num_programs(0) - 1)
    def _():
        y_ref[...] = acc[...].astype(BF16)


def whole(shape):
    return pl.BlockSpec(shape, lambda i: (0,) * len(shape))


def feed_forward(x, att, joined, b_out, gain, shift, b_up, w_down, b_down, keep):
    rows, width = x.shape
    hidden = w_down.shape[0]
    row = whole((1, width))
    full = whole((rows, width))
    part = pl.BlockSpec((rows, width), lambda i: (0, i))
    shapes = [jax.ShapeDtypeStruct((rows, width), BF16)]
    specs = [full]
    scratch = [pltpu.VMEM((rows, width), F32)]
    if keep:
        shapes += [
            jax.ShapeDtypeStruct((rows, width), F32),
            jax.ShapeDtypeStruct((rows, width), BF16),
            jax.ShapeDtypeStruct((rows, hidden), F32),
            jax.ShapeDtypeStruct((rows, hidden), BF16),
            jax.ShapeDtypeStruct((rows, width), BF16),
        ]
        specs += [full, full, part, part, full]
    else:
        scratch = [pltpu.VMEM((rows, width), BF16)] + scratch
    return call(
        feed_body,
        tuple(shapes),
        grid=(hidden // width,),
        in_specs=[
            full,
            whole(att.shape),
            pl.BlockSpec((width, width), lambda i: (0, 3)),
            row,
            row,
            row,
            pl.BlockSpec((width, width), lambda i: (0, 4 + i)),
            pl.BlockSpec((1, width), lambda i: (0, i)),
            pl.BlockSpec((width, width), lambda i: (i, 0)),
            row,
        ],
        out_specs=tuple(specs),
        scratch=scratch,
        flops=2 * rows * width * (2 * hidden + width),
        moved=4 * w_down.size + 2 * width * width + 10 * rows * hidden,
    )(x, att, joined, b_out, gain, shift, joined, b_up, w_down, b_down)


def feed_back_body(
    g_ref,
    slope_ref,
    w_down_ref,
    w_up_ref,
    w_out_ref,
    x1_ref,
    gain_ref,
    d_upper_ref,
    dx1_ref,
    branch_ref,
    datt_ref,
    sums_ref,
    up_sum_ref,
    acc,
):
    @pl.when(pl.program_id(0) == 0)
    def _():
        acc[...] = jnp.zeros_like(acc)

    d_upper = (dot_t(g_ref[...], w_down_ref[...]) * slope_ref[...]).astype(BF16)
    d_upper_ref[...] = d_upper
    up_sum_ref[...] = jnp.sum(d_upper.astype(F32), axis=0, keepdims=True)
    acc[...] += dot_t(d_upper, w_up_ref[...])

    @pl.when(pl.program_id(0) == pl.num_programs(0) - 1)
    def _():
        d_normed = acc[...]
        upstream = g_ref[...].astype(F32)
        scaled, inverse = norm_parts(x1_ref[...])
        d_middle = upstream + norm_back(d_normed, scaled, inverse, gain_ref[...])
        dx1_ref[...] = d_middle
        branch = d_middle.astype(BF16)
        branch_ref[...] = branch
        span = datt_ref.shape[2]
        for g in range(HEAD_GROUPS):
            datt_ref[g] = dot_t(branch, w_out_ref[g * span : (g + 1) * span, :]).astype(BF16)
        sums_ref[0:1, :] = jnp.sum(d_normed * scaled, axis=0, keepdims=True)
        sums_ref[1:2, :] = jnp.sum(d_normed, axis=0, keepdims=True)
        sums_ref[2:3, :] = jnp.sum(branch.astype(F32), axis=0, keepdims=True)
        sums_ref[3:4, :] = jnp.sum(upstream, axis=0, keepdims=True)


def feed_backward(g, slope, w_down, joined, x1, gain):
    rows, width = g.shape
    hidden = w_down.shape[0]
    chunk = width
    full = whole((rows, width))
    return call(
        feed_back_body,
        (
            jax.ShapeDtypeStruct((rows, hidden), BF16),
            jax.ShapeDtypeStruct((rows, width), F32),
            jax.ShapeDtypeStruct((rows, width), BF16),
            jax.ShapeDtypeStruct((HEAD_GROUPS, rows, width // HEAD_GROUPS), BF16),
            jax.ShapeDtypeStruct((4, width), F32),
            jax.ShapeDtypeStruct((1, hidden), F32),
        ),
        grid=(hidden // chunk,),
        in_specs=[
            full,
            pl.BlockSpec((rows, chunk), lambda i: (0, i)),
            pl.BlockSpec((chunk, width), lambda i: (i, 0)),
            pl.BlockSpec((width, chunk), lambda i: (0, 4 + i)),
            pl.BlockSpec((width, width), lambda i: (0, 3)),
            full,
            whole((1, width)),
        ],
        out_specs=(
            pl.BlockSpec((rows, chunk), lambda i: (0, i)),
            full,
            full,
            whole((HEAD_GROUPS, rows, width // HEAD_GROUPS)),
            whole((4, width)),
            pl.BlockSpec((1, chunk), lambda i: (0, i)),
        ),
        scratch=[pltpu.VMEM((rows, width), F32)],
        flops=2 * rows * width * (2 * hidden + width),
        moved=4 * w_down.size + 2 * width * width + 6 * rows * hidden,
    )(g, slope, w_down, joined, joined, x1, gain)


def qkv_back_body(
    grads_ref, w_ref, x_ref, dx1_ref, gain_ref, dx_ref, flat_ref, sums_ref, acc
):
    width = x_ref.shape[1]
    span = grads_ref.shape[2] // 3
    step = pl.program_id(0)
    for part in range(3):

        @pl.when(step == part)
        def _(part=part):
            cols = slice(part * width, (part + 1) * width)
            for g in range(HEAD_GROUPS):
                flat_ref[:, part * width + g * span : part * width + (g + 1) * span] = grads_ref[
                    g, :, part * span : (part + 1) * span
                ]
            came = dot_t(flat_ref[:, cols], w_ref[...])
            acc[...] = came if part == 0 else acc[...] + came

    @pl.when(step == 2)
    def _():
        d_normed = acc[...]
        scaled, inverse = norm_parts(x_ref[...].astype(F32))
        dx = dx1_ref[...] + norm_back(d_normed, scaled, inverse, gain_ref[...])
        dx_ref[...] = dx.astype(BF16)
        sums_ref[0:1, :] = jnp.sum(d_normed * scaled, axis=0, keepdims=True)
        sums_ref[1:2, :] = jnp.sum(d_normed, axis=0, keepdims=True)
        sums_ref[2:3, :] = jnp.sum(flat_ref[:, :width].astype(F32), axis=0, keepdims=True)
        sums_ref[3:4, :] = jnp.sum(flat_ref[:, 2 * width :].astype(F32), axis=0, keepdims=True)


def qkv_backward(grads, joined, x, dx1, gain, after=()):
    rows, width = x.shape

    def body(*refs):
        qkv_back_body(*refs[:5], *refs[5 + len(after) :])

    return call(
        body,
        (
            jax.ShapeDtypeStruct((rows, width), BF16),
            jax.ShapeDtypeStruct((rows, 3 * width), BF16),
            jax.ShapeDtypeStruct((4, width), F32),
        ),
        grid=(3,),
        in_specs=[
            whole(grads.shape),
            pl.BlockSpec((width, width), lambda i: (0, i)),
            whole((rows, width)),
            whole((rows, width)),
            whole((1, width)),
        ]
        + [pl.BlockSpec(memory_space=pl.ANY)] * len(after),
        out_specs=(whole((rows, width)), whole((rows, 3 * width)), whole((4, width))),
        scratch=[pltpu.VMEM((rows, width), F32)],
        flops=2 * rows * width * 3 * width,
        moved=6 * width * width + 20 * x.size,
    )(grads, joined, x, dx1, gain, *after)


def add_body(one_ref, two_ref, *rest):
    rest[-1][...] = (one_ref[...].astype(F32) + two_ref[...].astype(F32)).astype(BF16)


def add_after(one, two, after):
    rows, wide = one.shape
    block = next((n for n in (256, 208, 192, 128, 96, 64, 48) if rows % n == 0), rows)
    spec = pl.BlockSpec((block, wide), lambda i: (i, 0))
    return call(
        add_body,
        jax.ShapeDtypeStruct((rows, wide), BF16),
        grid=(rows // block,),
        in_specs=[spec, spec] + [pl.BlockSpec(memory_space=pl.ANY)] * len(after),
        out_specs=spec,
        flops=one.size,
        moved=6 * one.size,
    )(one, two, *after)


def copy_body(one_ref, *rest):
    rest[-1][...] = one_ref[...]


def copy_after(one, after):
    spec = pl.BlockSpec(one.shape, lambda i: (0, 0))
    return call(
        copy_body,
        jax.ShapeDtypeStruct(one.shape, one.dtype),
        grid=(1,),
        in_specs=[spec] + [pl.BlockSpec(memory_space=pl.ANY)] * len(after),
        out_specs=spec,
        flops=one.size,
        moved=4 * one.size,
    )(one, *after)


def join_body(dq_ref, kept_ref, back_ref, *rest):
    out_ref = rest[-1]
    span = dq_ref.shape[2]
    out_ref[:, :, :span] = dq_ref[...]
    out_ref[:, :, span:] = (kept_ref[...] + back_ref[...].astype(F32)).astype(BF16)


def join_grads(dq, kept, back, after):
    clips, rows, span = dq.shape

    def spec(wide):
        return pl.BlockSpec((1, rows, wide), lambda i: (i, 0, 0))

    return call(
        join_body,
        jax.ShapeDtypeStruct((clips, rows, 3 * span), BF16),
        grid=(clips,),
        in_specs=[spec(span), spec(2 * span), spec(2 * span)]
        + [pl.BlockSpec(memory_space=pl.ANY)] * len(after),
        out_specs=spec(3 * span),
        flops=kept.size,
        moved=8 * kept.size,
    )(dq, kept, back, *after)


def swap(block, axis):
    return lax.ppermute(block, axis, [(0, 1), (1, 0)])


def shift(block, distance):
    count = lax.axis_size("rest")
    return lax.ppermute(block, "rest", [(i, (i + distance) % count) for i in range(count)])


def spread(block):
    return lax.all_to_all(block, ("quad", "side"), 0, 0, tiled=True)


def to_clips(block, clips):
    groups, rows, wide = block.shape
    if clips == 1:
        return block.reshape(1, groups * rows, wide)
    block = block.reshape(groups, clips, rows // clips, wide)
    return jnp.swapaxes(block, 0, 1).reshape(clips, groups * (rows // clips), wide)


def to_tokens(block):
    clips, rows, wide = block.shape
    if clips == 1:
        return block.reshape(HEAD_GROUPS, rows // HEAD_GROUPS, wide)
    block = block.reshape(clips, HEAD_GROUPS, rows // HEAD_GROUPS, wide)
    return jnp.swapaxes(block, 0, 1).reshape(HEAD_GROUPS, -1, wide)


def other_keys(grouped, own, clips):
    if lax.axis_size("rest") == 1:
        return to_clips(swap(grouped, "core"), clips)
    near = [shift(own, k) for k in range(1, lax.axis_size("rest"))]
    far = swap(jnp.concatenate([own] + near, axis=1), "core")
    return jnp.concatenate(near + [far], axis=1)


def return_keys(kept, sent):
    queries = kept.shape[1]
    count = lax.axis_size("rest")
    near = (count - 1) * queries
    back = swap(sent[:, near:], "core")
    total = kept
    for k in range(1, count):
        part = sent[:, (k - 1) * queries : k * queries].astype(F32)
        part = part + back[:, k * queries : (k + 1) * queries].astype(F32)
        total = total + shift(part.astype(BF16), -k).astype(F32)
    return total, back[:, :queries]


def pick(flag, one, two):
    return jnp.where(flag, one, two)


def gather_weight(*blocks):
    core = lax.axis_index("core")
    quads = lax.axis_size("quad")
    part = blocks[0].shape[0] // (2 * quads)
    quad = lax.axis_index("quad")

    def cut(which):
        start = (which * quads + quad) * part
        return jnp.concatenate(
            [lax.dynamic_slice_in_dim(block, start, part, 0) for block in blocks], axis=1
        )

    own = cut(core)
    came = swap(cut(1 - core), "core")
    first = pick(core == 0, own, came)
    second = pick(core == 0, came, own)
    return [
        lax.all_gather(item, ("side", "rest", "core", "quad"), axis=0, tiled=True)
        for item in (first, second)
    ]


def in_order(second, mine, other):
    return pick(second, other, mine), pick(second, mine, other)


def gather_downs(block, after):
    if lax.axis_size("rest") > 1 or lax.axis_size("quad") != 2:
        return gather_weight(block)
    core, quad, side = (lax.axis_index(name) for name in ("core", "quad", "side"))
    part = block.shape[0] // 4
    start = (core * 2 + quad) * part
    came = swap(block, "core")
    mine, second = in_order(core == 1, block, came)
    near, line = (lax.dynamic_slice_in_dim(item, start, part, 0) for item in (mine, second))
    second = lax.all_gather(line, ("side", "rest", "core", "quad"), axis=0, tiled=True)
    near = swap(copy_after(near, after), "side")
    both = jnp.stack([near, swap(near, "quad")])
    far = swap(both, "core")
    here = in_order(quad == 1, both[0], both[1])
    there = in_order(quad == 1, far[0], far[1])
    rows = [
        *(pick(core == 1, b, a) for a, b in zip(here, there)),
        *(pick(core == 1, a, b) for a, b in zip(here, there)),
    ]
    other = jnp.concatenate(rows, axis=0)
    return [jnp.concatenate(in_order(side == 1, mine, other), axis=0), second]


def add(one, two):
    return (one.astype(F32) + two.astype(F32)).astype(one.dtype)


def cut_columns(left, which):
    shards = lax.axis_size("side") * lax.axis_size("rest")
    part = left.shape[1] // (2 * shards)
    return jnp.concatenate(
        [
            lax.dynamic_slice_in_dim(left, (2 * s + which) * part, part, 1)
            for s in range(shards)
        ],
        axis=1,
    )


def weight_halves(left, right):
    core = lax.axis_index("core")
    return [
        t_dot(cut_columns(left, which), right).astype(BF16) for which in (1 - core, core)
    ]


def side_parts(sent, kept):
    side = lax.axis_index("side")
    came = swap(sent, "core")
    half = kept.shape[0] // 2

    def cut(which):
        return add(
            lax.dynamic_slice_in_dim(kept, which * half, half, 0),
            lax.dynamic_slice_in_dim(came, which * half, half, 0),
        )

    return cut(1 - side), cut(side)


def side_sum(sent, kept, *after):
    total = add_after(kept, swap(sent, "side"), after)
    if lax.axis_size("rest") > 1:
        total = lax.psum_scatter(total, "rest", scatter_dimension=0, tiled=True)
    return total


def line_sum(*items, turned=False):
    return lax.psum(items, ("quad", "half") if turned else ("half", "quad"))


def join_cores(first, second):
    core = lax.axis_index("core")
    came = swap(pick(core == 0, second, first), "core")
    mine = pick(core == 0, first, second)
    return jnp.concatenate([pick(core == 0, mine, came), pick(core == 0, came, mine)], axis=0)


def swap_in(block):
    core, half = lax.axis_index("core"), lax.axis_index("half")
    micro, rows, wide = block.shape
    block = block.reshape(2, (micro // 2) * rows, wide)
    own = lax.dynamic_index_in_dim(block, half, 0, keepdims=False)
    other = lax.dynamic_index_in_dim(block, 1 - half, 0, keepdims=False)
    came = lax.ppermute(other, ("core", "half"), [(1, 2), (2, 1)])
    return pick(core == half, own, came)


def swap_out(first, second, micro):
    rows, wide = first.shape
    second_core, second_half = lax.axis_index("core") == 1, lax.axis_index("half") == 1
    mine, sent = in_order(second_core, first, second)
    parts = in_order(second_core, mine, swap(sent, "core"))
    mine, sent = in_order(second_half, *parts)
    clips = in_order(second_half, mine, swap(sent, "half"))
    return jnp.stack(clips).reshape(micro, 2 * rows // micro, wide)


def forward_layer(x, weights, clips, head, keep):
    joined, w_down, gains, shifts, b_qkv, b_out, b_down, b_up = weights
    grouped, normed_one = qkv_forward(x, gains[0:1], shifts[0:1], joined, b_qkv)
    grouped = spread(grouped)
    own = to_clips(grouped, clips)
    other = other_keys(grouped, own, clips)
    att, log_total = attend_forward(own, other, head)
    att = spread(to_tokens(att))
    y, *kept = feed_forward(
        x, att, joined, b_out, gains[1:2], shifts[1:2], b_up, w_down, b_down, keep
    )
    return y, (x, normed_one, own, other, log_total, *kept)


def attention_grads(kept, d_att, clips, head, after):
    own, other, log_total = kept[2:5]
    d_heads = to_clips(spread(d_att), clips)
    dq, kept_kv, sent_kv = attend_backward(own, other, d_heads, log_total, head, after)
    return (dq, *return_keys(kept_kv, sent_kv))


def spread_grads(grads, after=()):
    return spread(to_tokens(join_grads(*grads, after)))


def backward_lean(kept, g, weights, clips, head):
    x, _, _, _, _, x1, _, slope, _, _ = kept
    joined, w_down, gains = weights[:3]
    _, dx1, _, d_att, _, _ = feed_backward(g, slope, w_down, joined, x1, gains[1:2])
    d_tokens = spread_grads(attention_grads(kept, d_att, clips, head, ()))
    return qkv_backward(d_tokens, joined, x, dx1, gains[0:1])[0]


def small_rows(sums_one, sums_two, up_sum, shards, wide):
    rows = jnp.concatenate(
        [
            sums_one[0:1],
            sums_two[0:1],
            sums_one[1:2],
            sums_two[1:2],
            sums_one[2:4],
            sums_two[2:4],
        ]
    )
    rows = jnp.swapaxes(rows.reshape(8, shards, -1), 0, 1).reshape(shards, -1)
    packed = jnp.concatenate([rows, up_sum.reshape(shards, -1)], axis=1).astype(BF16)
    packed = packed.reshape(shards, 2, -1)
    lines = -(-packed.shape[2] // wide)
    room = 16 * (-(-lines // 16)) * wide
    packed = jnp.pad(packed, ((0, 0), (0, 0), (0, room - packed.shape[2])))
    return packed.reshape(shards, 2, -1, wide)


def beside(weight, rows):
    shards, _, wide = rows.shape
    return jnp.concatenate([weight.reshape(shards, -1, wide), rows], axis=1).reshape(-1, wide)


def qkv_halves(normed_one, flat, sums_one, sums_two, up_sum, shards):
    core = lax.axis_index("core")
    rows = small_rows(sums_one, sums_two, up_sum, shards, flat.shape[1])
    return [
        beside(item, lax.dynamic_index_in_dim(rows, which, 1, keepdims=False))
        for item, which in zip(weight_halves(normed_one, flat), (1 - core, core))
    ]


def backward_all(kept_first, kept_second, g, layers, clips, head, shards):
    x, normed_one, _, _, _, x1, normed_two, slope, lifted, att = kept_second
    joined, w_down, gains = layers[1][:3]
    d_upper, dx1, branch, d_att, sums_two, up_sum = feed_backward(
        g, slope, w_down, joined, x1, gains[1:2]
    )
    down = weight_halves(lifted, g)
    up = weight_halves(normed_two, d_upper)
    grads = attention_grads(kept_second, d_att, clips, head, (*down, *up))
    down, up = side_parts(*down), side_parts(*up)
    d_tokens = spread_grads(grads, (*down, *up))
    out = weight_halves(att, branch)
    d_second, flat, sums_one = qkv_backward(d_tokens, joined, x, dx1, gains[0:1], out)
    qkv = qkv_halves(normed_one, flat, sums_one, sums_two, up_sum, shards)

    x, normed_one, _, _, _, x1, normed_two, slope, lifted, att = kept_first
    joined, w_down, gains = layers[0][:3]
    d_upper, dx1, branch, d_att, sums_two, up_sum = feed_backward(
        d_second, slope, w_down, joined, x1, gains[1:2]
    )
    down_one = weight_halves(lifted, d_second)
    up_one = weight_halves(normed_two, d_upper)
    grads = attention_grads(kept_first, d_att, clips, head, (*qkv, *down_one, *up_one))
    down_two, up_two = side_sum(*down, grads[0]), side_sum(*up, grads[0])
    out, qkv = side_parts(*out), side_parts(*qkv)
    d_tokens = spread_grads(grads, (down_two, up_two, *out, *qkv))
    down_two, up_two = line_sum(down_two, up_two)
    down_one, up_one = side_parts(*down_one), side_parts(*up_one)
    out_one = weight_halves(att, branch)
    d_first, flat, sums_one = qkv_backward(
        d_tokens, joined, x, dx1, gains[0:1], (*down_one, *up_one, *out_one)
    )
    qkv_one = qkv_halves(normed_one, flat, sums_one, sums_two, up_sum, shards)
    out_two, qkv_two = side_sum(*out, *qkv_one), side_sum(*qkv, *qkv_one)
    out_one, qkv_one = side_parts(*out_one), side_parts(*qkv_one)
    late = (out_one[0], qkv_one[0], out_two, qkv_two)
    down_one, up_one = side_sum(*down_one, *late), side_sum(*up_one, *late)
    late = (down_two, up_two, down_one, up_one)
    out_two, qkv_two, down_one, up_one = line_sum(
        out_two, qkv_two, down_one, up_one, turned=True
    )
    out_one, qkv_one = side_sum(*out_one, *late), side_sum(*qkv_one, *late)
    out_one, qkv_one = line_sum(out_one, qkv_one)
    firsts = (qkv_one, out_one, up_one, down_one)
    seconds = (qkv_two, out_two, up_two, down_two)
    return d_first, d_second, [join_cores(a, b) for a, b in zip(firsts, seconds)]


def gather_small(block):
    core, side = lax.axis_index("core"), lax.axis_index("side")
    if lax.axis_size("rest") > 1:
        whole_block = lax.all_gather(block, ("core", "side", "rest"), axis=0, tiled=False)
        return whole_block.reshape(2, -1, block.shape[0])
    came = swap(block, "side")
    layer = jnp.stack([pick(side == 0, block, came), pick(side == 0, came, block)])
    came = swap(layer, "core")
    return jnp.stack([pick(core == 0, layer, came), pick(core == 0, came, layer)])


def per_device(
    frames, out_grad, norm_gain, norm_bias, w_qkv, w_out, w_up, w_down, proj_bias, up_bias
):
    pairs = lax.axis_size("pair")
    pair = lax.axis_index("pair")
    shards = lax.axis_size("side") * lax.axis_size("rest")
    micro, _, width = frames.shape
    clips = micro // 2
    head = width // HEADS
    part = width // shards

    joined = gather_weight(w_qkv[0], w_out[0], w_up[0])
    downs = gather_downs(w_down[0], joined[:1])
    small = jnp.concatenate(
        [norm_gain.reshape(-1), norm_bias.reshape(-1), proj_bias.reshape(-1), up_bias.reshape(-1)]
    )
    small = gather_small(small).astype(F32)
    rows = jnp.swapaxes(small[:, :, : 8 * part].reshape(2, shards, 8, part), 1, 2)
    rows = rows.reshape(2, 8, width)
    ups = small[:, :, 8 * part :].reshape(2, 1, -1)
    x_start = swap_in(frames)
    layers = []
    for layer in range(2):
        r = rows[layer]
        b_qkv = jnp.concatenate([r[4:5], jnp.zeros_like(r[4:5]), r[5:6]], axis=1)
        layers.append(
            (joined[layer], downs[layer], r[0:2], r[2:4], b_qkv, r[6:7], r[7:8], ups[layer])
        )

    x = x_start
    for phase in range(pairs):
        if phase > 0:
            came = lax.ppermute(second, "pair", [(i, i + 1) for i in range(pairs - 1)])
            x = pick(pair == 0, x_start, came)
        keep = phase == pairs - 1
        first, kept_first = forward_layer(x, layers[0], clips, head, keep)
        second, kept_second = forward_layer(first, layers[1], clips, head, keep)
    hidden = swap_out(first, second, micro)

    g_start = swap_in(out_grad)
    g = g_start
    for phase in range(pairs - 1):
        d_second = backward_lean(kept_second, g, layers[1], clips, head)
        d_first = backward_lean(kept_first, d_second, layers[0], clips, head)
        came = lax.ppermute(d_first, "pair", [(i + 1, i) for i in range(pairs - 1)])
        g = pick(pair == pairs - 1, g_start, came)
    d_first, d_second, (qkv, out, up, down) = backward_all(
        kept_first, kept_second, g, layers, clips, head, shards
    )
    input_grads = swap_out(d_first, d_second, micro)

    own_rows = part // 2
    qkv = qkv.reshape(2, -1, 3 * width).astype(F32)
    packed = qkv[:, own_rows:].reshape(2, -1)[:, : (8 * part + up_bias.shape[1]) // 2].reshape(-1)
    heads = packed[: 8 * part].reshape(8, part)
    qkv = qkv[:, :own_rows].reshape(-1, 3 * width)
    return (
        hidden[None],
        input_grads[None],
        heads[0:2][None],
        heads[2:4][None],
        qkv[None],
        out.astype(F32)[None],
        up.astype(F32)[None],
        down.astype(F32)[None],
        heads[4:8][None],
        packed[8 * part :][None],
    )


def solution(mesh):
    sections, groups, shards = (mesh.shape[name] for name in ("section", "seq", "shard"))
    cut = Mesh(
        mesh.devices.reshape(sections // 2, 2, 2, groups // 2, 2, shards // 2),
        AXES,
    )
    section, seq, shard = ("pair", "core"), ("half", "quad"), ("side", "rest")
    rows = seq + shard
    return jax.shard_map(
        per_device,
        mesh=cut,
        in_specs=(
            P(None, rows, None),
            P(None, rows, None),
            P(section, None, shard),
            P(section, None, shard),
            P(section, shard, None),
            P(section, shard, None),
            P(section, shard, None),
            P(section, shard, None),
            P(section, None, shard),
            P(section, shard),
        ),
        out_specs=(
            P(section, None, rows, None),
            P(section, None, rows, None),
            P(section, None, shard),
            P(section, None, shard),
            P(section, shard, None),
            P(section, shard, None),
            P(section, shard, None),
            P(section, shard, None),
            P(section, None, shard),
            P(section, shard),
        ),
        check_vma=False,
    )
```

```python
import math

import jax
import jax.numpy as jnp
from jax import lax
from jax.experimental import pallas as pl
from jax.experimental.pallas import tpu as pltpu
from jax.sharding import Mesh
from jax.sharding import PartitionSpec as P

HEADS = 12
norm_eps = 1e-05
F32 = jnp.float32
BF16 = jnp.bfloat16
VMEM_LIMIT = 56 * 1024 * 1024
AXES = ("pair", "core", "half", "quad", "side", "rest")
HEAD_GROUPS = 4


def call(body, out_shapes, grid=None, in_specs=None, out_specs=None, scratch=(), flops=0, moved=0):
    extra = {} if grid is None else dict(grid=grid, in_specs=in_specs, out_specs=out_specs)
    return pl.pallas_call(
        body,
        out_shape=out_shapes,
        scratch_shapes=scratch,
        compiler_params=pltpu.CompilerParams(vmem_limit_bytes=VMEM_LIMIT),
        cost_estimate=pl.CostEstimate(flops=flops, bytes_accessed=moved, transcendentals=0),
        **extra,
    )


def dot(left, right):
    return jnp.dot(left, right, preferred_element_type=F32)


def dot_t(left, right):
    return lax.dot_general(left, right, (((1,), (1,)), ((), ())), preferred_element_type=F32)


def t_dot(left, right):
    return lax.dot_general(left, right, (((0,), (0,)), ((), ())), preferred_element_type=F32)


def norm_parts(values):
    center = values - jnp.mean(values, axis=-1, keepdims=True)
    inverse = lax.rsqrt(jnp.mean(center * center, axis=-1, keepdims=True) + norm_eps)
    return center * inverse, inverse


def norm_back(upstream, scaled, inverse, gain_row):
    weighted = upstream * gain_row
    return inverse * (
        weighted
        - jnp.mean(weighted, axis=-1, keepdims=True)
        - scaled * jnp.mean(weighted * scaled, axis=-1, keepdims=True)
    )


def qkv_body(x_ref, gain_ref, shift_ref, w_ref, bias_ref, out_ref, normed_ref):
    @pl.when(pl.program_id(0) == 0)
    def _():
        scaled, _ = norm_parts(x_ref[...].astype(F32))
        normed_ref[...] = (scaled * gain_ref[...] + shift_ref[...]).astype(BF16)

    span = out_ref.shape[2] // 3
    piece = (dot(normed_ref[...], w_ref[...]) + bias_ref[...]).astype(BF16)
    for part in range(3):

        @pl.when(pl.program_id(0) == part)
        def _(part=part):
            for g in range(HEAD_GROUPS):
                out_ref[g, :, part * span : (part + 1) * span] = piece[:, g * span : (g + 1) * span]


def qkv_forward(x, gain, shift, joined, bias):
    rows, width = x.shape
    span = width // HEAD_GROUPS
    return call(
        qkv_body,
        (
            jax.ShapeDtypeStruct((HEAD_GROUPS, rows, 3 * span), BF16),
            jax.ShapeDtypeStruct((rows, width), BF16),
        ),
        grid=(3,),
        in_specs=[
            whole((rows, width)),
            whole((1, width)),
            whole((1, width)),
            pl.BlockSpec((width, width), lambda i: (0, i)),
            pl.BlockSpec((1, width), lambda i: (0, i)),
        ],
        out_specs=(whole((HEAD_GROUPS, rows, 3 * span)), whole((rows, width))),
        flops=2 * rows * width * 3 * width,
        moved=6 * width * width + 10 * x.size,
    )(x, gain, shift, joined, bias)


def key_chunks(own_ref, other_ref):
    place = 0
    for ref in (own_ref, other_ref):
        total = ref.shape[1]
        step = 256 if total % 256 == 0 else total
        for start in range(0, total, step):
            yield ref, start, place, step
            place += step


def attend_body(q_ref, own_ref, other_ref, out_ref, log_ref, score_ref, *, head):
    span = q_ref.shape[2] // 3
    queries = q_ref.shape[1]
    scale = 1.0 / math.sqrt(head)
    for h in range(span // head):
        q = q_ref[0, :, h * head : (h + 1) * head] * scale
        top = jnp.full((1, queries), -jnp.inf, F32)
        for ref, start, place, step in key_chunks(own_ref, other_ref):
            k = ref[0, start : start + step, span + h * head : span + (h + 1) * head]
            scores = dot_t(k, q)
            score_ref[place : place + step, :] = scores
            top = jnp.maximum(top, jnp.max(scores, axis=0, keepdims=True))
        total = jnp.zeros((1, queries), F32)
        acc = jnp.zeros((head, queries), F32)
        for ref, start, place, step in key_chunks(own_ref, other_ref):
            v = ref[0, start : start + step, 2 * span + h * head : 2 * span + (h + 1) * head]
            e = jnp.exp(score_ref[place : place + step, :] - top)
            total = total + jnp.sum(e, axis=0, keepdims=True)
            acc = acc + t_dot(v, e.astype(BF16))
        out_ref[0, :, h * head : (h + 1) * head] = jnp.transpose(acc / total).astype(BF16)
        log_ref[0, h : h + 1, :] = top + jnp.log(total)


def query_block(queries):
    return 256 if queries % 256 == 0 else queries


def attend_forward(own, other, head):
    clips, queries, wide = own.shape
    span = wide // 3
    keys = queries + other.shape[1]
    block = query_block(queries)

    def body(*refs):
        attend_body(*refs, head=head)

    return call(
        body,
        (
            jax.ShapeDtypeStruct((clips, queries, span), BF16),
            jax.ShapeDtypeStruct((clips, span // head, queries), F32),
        ),
        grid=(clips, queries // block),
        in_specs=[
            pl.BlockSpec((1, block, wide), lambda m, i: (m, i, 0)),
            pl.BlockSpec((1, queries, wide), lambda m, i: (m, 0, 0)),
            pl.BlockSpec((1, other.shape[1], wide), lambda m, i: (m, 0, 0)),
        ],
        out_specs=(
            pl.BlockSpec((1, block, span), lambda m, i: (m, i, 0)),
            pl.BlockSpec((1, span // head, block), lambda m, i: (m, 0, i)),
        ),
        scratch=[pltpu.VMEM((keys, block), F32)],
        flops=16 * clips * queries * keys * span,
        moved=4 * (own.size + other.size),
    )(own, own, other)


def attend_back_body(
    q_ref,
    own_ref,
    other_ref,
    grad_ref,
    log_ref,
    dq_ref,
    dkv_own_ref,
    dkv_other_ref,
    p_ref,
    dp_ref,
    dk_acc,
    dv_acc,
    *,
    head,
):
    span = q_ref.shape[2] // 3
    queries = q_ref.shape[1]
    heads = span // head
    scale = 1.0 / math.sqrt(head)

    @pl.when(pl.program_id(1) == 0)
    def _():
        dk_acc[...] = jnp.zeros_like(dk_acc)
        dv_acc[...] = jnp.zeros_like(dv_acc)

    for h in range(heads):
        q = q_ref[0, :, h * head : (h + 1) * head] * scale
        d_out = grad_ref[0, :, h * head : (h + 1) * head]
        log_total = log_ref[0, h : h + 1, :]
        row_term = jnp.zeros((1, queries), F32)
        for ref, start, place, step in key_chunks(own_ref, other_ref):
            k = ref[0, start : start + step, span + h * head : span + (h + 1) * head]
            v = ref[0, start : start + step, 2 * span + h * head : 2 * span + (h + 1) * head]
            probs = jnp.exp(dot_t(k, q) - log_total)
            d_probs = dot_t(v, d_out)
            p_ref[place : place + step, :] = probs
            dp_ref[place : place + step, :] = d_probs
            row_term = row_term + jnp.sum(probs * d_probs, axis=0, keepdims=True)
            dv_acc[h, place : place + step, :] += dot(probs.astype(BF16), d_out)
        dq = jnp.zeros((head, queries), F32)
        for ref, start, place, step in key_chunks(own_ref, other_ref):
            k = ref[0, start : start + step, span + h * head : span + (h + 1) * head]
            d_scores = (
                p_ref[place : place + step, :] * (dp_ref[place : place + step, :] - row_term)
            ).astype(BF16)
            dk_acc[h, place : place + step, :] += dot(d_scores, q)
            dq = dq + t_dot(k, d_scores)
        dq_ref[0, :, h * head : (h + 1) * head] = jnp.transpose(dq * scale).astype(BF16)

    @pl.when(pl.program_id(1) == pl.num_programs(1) - 1)
    def _():
        place = 0
        for ref in (dkv_own_ref, dkv_other_ref):
            rows = ref.shape[1]
            for h in range(heads):
                ref[0, :, h * head : (h + 1) * head] = dk_acc[h, place : place + rows, :].astype(
                    ref.dtype
                )
                ref[0, :, span + h * head : span + (h + 1) * head] = dv_acc[
                    h, place : place + rows, :
                ].astype(ref.dtype)
            place += rows


def attend_backward(own, other, grad, log_total, head, after=()):
    clips, queries, wide = own.shape
    span = wide // 3
    others = other.shape[1]
    keys = queries + others
    block = query_block(queries)
    heads = span // head

    def body(*refs):
        attend_back_body(*refs[:5], *refs[5 + len(after) :], head=head)

    return call(
        body,
        (
            jax.ShapeDtypeStruct((clips, queries, span), BF16),
            jax.ShapeDtypeStruct((clips, queries, 2 * span), F32),
            jax.ShapeDtypeStruct((clips, others, 2 * span), BF16),
        ),
        grid=(clips, queries // block),
        in_specs=[
            pl.BlockSpec((1, block, wide), lambda m, i: (m, i, 0)),
            pl.BlockSpec((1, queries, wide), lambda m, i: (m, 0, 0)),
            pl.BlockSpec((1, others, wide), lambda m, i: (m, 0, 0)),
            pl.BlockSpec((1, block, span), lambda m, i: (m, i, 0)),
            pl.BlockSpec((1, heads, block), lambda m, i: (m, 0, i)),
        ]
        + [pl.BlockSpec(memory_space=pl.ANY)] * len(after),
        out_specs=(
            pl.BlockSpec((1, block, span), lambda m, i: (m, i, 0)),
            pl.BlockSpec((1, queries, 2 * span), lambda m, i: (m, 0, 0)),
            pl.BlockSpec((1, others, 2 * span), lambda m, i: (m, 0, 0)),
        ),
        scratch=[
            pltpu.VMEM((keys, block), F32),
            pltpu.VMEM((keys, block), F32),
            pltpu.VMEM((heads, keys, head), F32),
            pltpu.VMEM((heads, keys, head), F32),
        ],
        flops=40 * clips * queries * keys * span,
        moved=8 * (own.size + other.size),
    )(own, own, other, grad, log_total, *after)


def feed_body(
    x_ref,
    att_ref,
    w_out_ref,
    b_out_ref,
    gain_ref,
    shift_ref,
    w_up_ref,
    b_up_ref,
    w_down_ref,
    b_down_ref,
    y_ref,
    *rest,
):
    if len(rest) > 2:
        x1_ref, normed_ref, slope_ref, lifted_ref, flat_ref, acc = rest
    else:
        normed_ref, acc = rest
    span = att_ref.shape[2]

    @pl.when(pl.program_id(0) == 0)
    def _():
        middle = x_ref[...].astype(F32) + b_out_ref[...]
        for g in range(HEAD_GROUPS):
            middle = middle + dot(att_ref[g], w_out_ref[g * span : (g + 1) * span, :])
            if len(rest) > 2:
                flat_ref[:, g * span : (g + 1) * span] = att_ref[g]
        if len(rest) > 2:
            x1_ref[...] = middle
        scaled, _ = norm_parts(middle)
        normed_ref[...] = (scaled * gain_ref[...] + shift_ref[...]).astype(BF16)
        acc[...] = middle + b_down_ref[...]

    upper = dot(normed_ref[...], w_up_ref[...]) + b_up_ref[...]
    phi = 0.5 * (1.0 + lax.erf(upper * math.sqrt(0.5)))
    lifted = (upper * phi).astype(BF16)
    if len(rest) > 2:
        density = jnp.exp(-0.5 * upper * upper) * (1.0 / math.sqrt(2.0 * math.pi))
        slope_ref[...] = phi + upper * density
        lifted_ref[...] = lifted
    acc[...] += dot(lifted, w_down_ref[...])

    @pl.when(pl.program_id(0) == pl.num_programs(0) - 1)
    def _():
        y_ref[...] = acc[...].astype(BF16)


def whole(shape):
    return pl.BlockSpec(shape, lambda i: (0,) * len(shape))


def feed_forward(x, att, joined, b_out, gain, shift, b_up, w_down, b_down, keep):
    rows, width = x.shape
    hidden = w_down.shape[0]
    row = whole((1, width))
    full = whole((rows, width))
    part = pl.BlockSpec((rows, width), lambda i: (0, i))
    shapes = [jax.ShapeDtypeStruct((rows, width), BF16)]
    specs = [full]
    scratch = [pltpu.VMEM((rows, width), F32)]
    if keep:
        shapes += [
            jax.ShapeDtypeStruct((rows, width), F32),
            jax.ShapeDtypeStruct((rows, width), BF16),
            jax.ShapeDtypeStruct((rows, hidden), F32),
            jax.ShapeDtypeStruct((rows, hidden), BF16),
            jax.ShapeDtypeStruct((rows, width), BF16),
        ]
        specs += [full, full, part, part, full]
    else:
        scratch = [pltpu.VMEM((rows, width), BF16)] + scratch
    return call(
        feed_body,
        tuple(shapes),
        grid=(hidden // width,),
        in_specs=[
            full,
            whole(att.shape),
            pl.BlockSpec((width, width), lambda i: (0, 3)),
            row,
            row,
            row,
            pl.BlockSpec((width, width), lambda i: (0, 4 + i)),
            pl.BlockSpec((1, width), lambda i: (0, i)),
            pl.BlockSpec((width, width), lambda i: (i, 0)),
            row,
        ],
        out_specs=tuple(specs),
        scratch=scratch,
        flops=2 * rows * width * (2 * hidden + width),
        moved=4 * w_down.size + 2 * width * width + 10 * rows * hidden,
    )(x, att, joined, b_out, gain, shift, joined, b_up, w_down, b_down)


def feed_back_body(
    g_ref,
    slope_ref,
    w_down_ref,
    w_up_ref,
    w_out_ref,
    x1_ref,
    gain_ref,
    d_upper_ref,
    dx1_ref,
    branch_ref,
    datt_ref,
    sums_ref,
    up_sum_ref,
    acc,
):
    @pl.when(pl.program_id(0) == 0)
    def _():
        acc[...] = jnp.zeros_like(acc)

    d_upper = (dot_t(g_ref[...], w_down_ref[...]) * slope_ref[...]).astype(BF16)
    d_upper_ref[...] = d_upper
    up_sum_ref[...] = jnp.sum(d_upper.astype(F32), axis=0, keepdims=True)
    acc[...] += dot_t(d_upper, w_up_ref[...])

    @pl.when(pl.program_id(0) == pl.num_programs(0) - 1)
    def _():
        d_normed = acc[...]
        upstream = g_ref[...].astype(F32)
        scaled, inverse = norm_parts(x1_ref[...])
        d_middle = upstream + norm_back(d_normed, scaled, inverse, gain_ref[...])
        dx1_ref[...] = d_middle
        branch = d_middle.astype(BF16)
        branch_ref[...] = branch
        span = datt_ref.shape[2]
        for g in range(HEAD_GROUPS):
            datt_ref[g] = dot_t(branch, w_out_ref[g * span : (g + 1) * span, :]).astype(BF16)
        sums_ref[0:1, :] = jnp.sum(d_normed * scaled, axis=0, keepdims=True)
        sums_ref[1:2, :] = jnp.sum(d_normed, axis=0, keepdims=True)
        sums_ref[2:3, :] = jnp.sum(branch.astype(F32), axis=0, keepdims=True)
        sums_ref[3:4, :] = jnp.sum(upstream, axis=0, keepdims=True)


def feed_backward(g, slope, w_down, joined, x1, gain):
    rows, width = g.shape
    hidden = w_down.shape[0]
    chunk = width
    full = whole((rows, width))
    return call(
        feed_back_body,
        (
            jax.ShapeDtypeStruct((rows, hidden), BF16),
            jax.ShapeDtypeStruct((rows, width), F32),
            jax.ShapeDtypeStruct((rows, width), BF16),
            jax.ShapeDtypeStruct((HEAD_GROUPS, rows, width // HEAD_GROUPS), BF16),
            jax.ShapeDtypeStruct((4, width), F32),
            jax.ShapeDtypeStruct((1, hidden), F32),
        ),
        grid=(hidden // chunk,),
        in_specs=[
            full,
            pl.BlockSpec((rows, chunk), lambda i: (0, i)),
            pl.BlockSpec((chunk, width), lambda i: (i, 0)),
            pl.BlockSpec((width, chunk), lambda i: (0, 4 + i)),
            pl.BlockSpec((width, width), lambda i: (0, 3)),
            full,
            whole((1, width)),
        ],
        out_specs=(
            pl.BlockSpec((rows, chunk), lambda i: (0, i)),
            full,
            full,
            whole((HEAD_GROUPS, rows, width // HEAD_GROUPS)),
            whole((4, width)),
            pl.BlockSpec((1, chunk), lambda i: (0, i)),
        ),
        scratch=[pltpu.VMEM((rows, width), F32)],
        flops=2 * rows * width * (2 * hidden + width),
        moved=4 * w_down.size + 2 * width * width + 6 * rows * hidden,
    )(g, slope, w_down, joined, joined, x1, gain)


def qkv_back_body(
    grads_ref, w_ref, x_ref, dx1_ref, gain_ref, dx_ref, flat_ref, sums_ref, acc
):
    width = x_ref.shape[1]
    span = grads_ref.shape[2] // 3
    step = pl.program_id(0)
    for part in range(3):

        @pl.when(step == part)
        def _(part=part):
            cols = slice(part * width, (part + 1) * width)
            for g in range(HEAD_GROUPS):
                flat_ref[:, part * width + g * span : part * width + (g + 1) * span] = grads_ref[
                    g, :, part * span : (part + 1) * span
                ]
            came = dot_t(flat_ref[:, cols], w_ref[...])
            acc[...] = came if part == 0 else acc[...] + came

    @pl.when(step == 2)
    def _():
        d_normed = acc[...]
        scaled, inverse = norm_parts(x_ref[...].astype(F32))
        dx = dx1_ref[...] + norm_back(d_normed, scaled, inverse, gain_ref[...])
        dx_ref[...] = dx.astype(BF16)
        sums_ref[0:1, :] = jnp.sum(d_normed * scaled, axis=0, keepdims=True)
        sums_ref[1:2, :] = jnp.sum(d_normed, axis=0, keepdims=True)
        sums_ref[2:3, :] = jnp.sum(flat_ref[:, :width].astype(F32), axis=0, keepdims=True)
        sums_ref[3:4, :] = jnp.sum(flat_ref[:, 2 * width :].astype(F32), axis=0, keepdims=True)


def qkv_backward(grads, joined, x, dx1, gain, after=()):
    rows, width = x.shape

    def body(*refs):
        qkv_back_body(*refs[:5], *refs[5 + len(after) :])

    return call(
        body,
        (
            jax.ShapeDtypeStruct((rows, width), BF16),
            jax.ShapeDtypeStruct((rows, 3 * width), BF16),
            jax.ShapeDtypeStruct((4, width), F32),
        ),
        grid=(3,),
        in_specs=[
            whole(grads.shape),
            pl.BlockSpec((width, width), lambda i: (0, i)),
            whole((rows, width)),
            whole((rows, width)),
            whole((1, width)),
        ]
        + [pl.BlockSpec(memory_space=pl.ANY)] * len(after),
        out_specs=(whole((rows, width)), whole((rows, 3 * width)), whole((4, width))),
        scratch=[pltpu.VMEM((rows, width), F32)],
        flops=2 * rows * width * 3 * width,
        moved=6 * width * width + 20 * x.size,
    )(grads, joined, x, dx1, gain, *after)


def add_body(one_ref, two_ref, *rest):
    rest[-1][...] = (one_ref[...].astype(F32) + two_ref[...].astype(F32)).astype(BF16)


def add_after(one, two, after):
    rows, wide = one.shape
    block = next((n for n in (272, 256, 192, 128, 96, 80, 64, 48) if rows % n == 0), rows)
    spec = pl.BlockSpec((block, wide), lambda i: (i, 0))
    return call(
        add_body,
        jax.ShapeDtypeStruct((rows, wide), BF16),
        grid=(rows // block,),
        in_specs=[spec, spec] + [pl.BlockSpec(memory_space=pl.ANY)] * len(after),
        out_specs=spec,
        flops=one.size,
        moved=6 * one.size,
    )(one, two, *after)


def copy_body(one_ref, *rest):
    rest[-1][...] = one_ref[...]


def copy_after(one, after):
    spec = pl.BlockSpec(one.shape, lambda i: (0, 0))
    return call(
        copy_body,
        jax.ShapeDtypeStruct(one.shape, one.dtype),
        grid=(1,),
        in_specs=[spec] + [pl.BlockSpec(memory_space=pl.ANY)] * len(after),
        out_specs=spec,
        flops=one.size,
        moved=4 * one.size,
    )(one, *after)


def join_body(dq_ref, kept_ref, back_ref, *rest):
    out_ref = rest[-1]
    span = dq_ref.shape[2]
    out_ref[:, :, :span] = dq_ref[...]
    out_ref[:, :, span:] = (kept_ref[...] + back_ref[...].astype(F32)).astype(BF16)


def join_grads(dq, kept, back, after):
    clips, rows, span = dq.shape

    def spec(wide):
        return pl.BlockSpec((1, rows, wide), lambda i: (i, 0, 0))

    return call(
        join_body,
        jax.ShapeDtypeStruct((clips, rows, 3 * span), BF16),
        grid=(clips,),
        in_specs=[spec(span), spec(2 * span), spec(2 * span)]
        + [pl.BlockSpec(memory_space=pl.ANY)] * len(after),
        out_specs=spec(3 * span),
        flops=kept.size,
        moved=8 * kept.size,
    )(dq, kept, back, *after)


def swap(block, axis):
    return lax.ppermute(block, axis, [(0, 1), (1, 0)])


def shift(block, distance):
    count = lax.axis_size("rest")
    return lax.ppermute(block, "rest", [(i, (i + distance) % count) for i in range(count)])


def spread(block):
    return lax.all_to_all(block, ("quad", "side"), 0, 0, tiled=True)


def to_clips(block, clips):
    groups, rows, wide = block.shape
    if clips == 1:
        return block.reshape(1, groups * rows, wide)
    block = block.reshape(groups, clips, rows // clips, wide)
    return jnp.swapaxes(block, 0, 1).reshape(clips, groups * (rows // clips), wide)


def to_tokens(block):
    clips, rows, wide = block.shape
    if clips == 1:
        return block.reshape(HEAD_GROUPS, rows // HEAD_GROUPS, wide)
    block = block.reshape(clips, HEAD_GROUPS, rows // HEAD_GROUPS, wide)
    return jnp.swapaxes(block, 0, 1).reshape(HEAD_GROUPS, -1, wide)


def other_keys(grouped, own, clips):
    if lax.axis_size("rest") == 1:
        return to_clips(swap(grouped, "core"), clips)
    near = [shift(own, k) for k in range(1, lax.axis_size("rest"))]
    far = swap(jnp.concatenate([own] + near, axis=1), "core")
    return jnp.concatenate(near + [far], axis=1)


def return_keys(kept, sent):
    queries = kept.shape[1]
    count = lax.axis_size("rest")
    near = (count - 1) * queries
    back = swap(sent[:, near:], "core")
    total = kept
    for k in range(1, count):
        part = sent[:, (k - 1) * queries : k * queries].astype(F32)
        part = part + back[:, k * queries : (k + 1) * queries].astype(F32)
        total = total + shift(part.astype(BF16), -k).astype(F32)
    return total, back[:, :queries]


def pick(flag, one, two):
    return jnp.where(flag, one, two)


def gather_weight(*blocks):
    core = lax.axis_index("core")
    quads = lax.axis_size("quad")
    part = blocks[0].shape[0] // (2 * quads)
    quad = lax.axis_index("quad")

    def cut(which):
        start = (which * quads + quad) * part
        return jnp.concatenate(
            [lax.dynamic_slice_in_dim(block, start, part, 0) for block in blocks], axis=1
        )

    own = cut(core)
    came = swap(cut(1 - core), "core")
    first = pick(core == 0, own, came)
    second = pick(core == 0, came, own)
    return [
        lax.all_gather(item, ("side", "rest", "core", "quad"), axis=0, tiled=True)
        for item in (first, second)
    ]


def in_order(second, mine, other):
    return pick(second, other, mine), pick(second, mine, other)


def start_downs(block, after):
    if lax.axis_size("rest") > 1 or lax.axis_size("quad") != 2:
        first, second = gather_weight(block)
        return None, first, second
    core, quad = lax.axis_index("core"), lax.axis_index("quad")
    part = block.shape[0] // 4
    mine, other = in_order(core == 1, block, swap(block, "core"))
    line = lax.dynamic_slice_in_dim(other, (core * 2 + quad) * part, part, 0)
    second = lax.all_gather(line, ("side", "rest", "core", "quad"), axis=0, tiled=True)
    near = lax.dynamic_slice_in_dim(mine, core * 2 * part, 2 * part, 0)
    return swap(copy_after(near, after), "side"), mine, second


def finish_down(near, mine, after):
    if near is None:
        return mine
    core, side = lax.axis_index("core"), lax.axis_index("side")
    near = copy_after(near, after)
    other = jnp.concatenate(in_order(core == 1, near, swap(near, "core")), axis=0)
    return jnp.concatenate(in_order(side == 1, mine, other), axis=0)


def add(one, two):
    return (one.astype(F32) + two.astype(F32)).astype(one.dtype)


def cut_columns(left, which):
    shards = lax.axis_size("side") * lax.axis_size("rest")
    part = left.shape[1] // (2 * shards)
    return jnp.concatenate(
        [
            lax.dynamic_slice_in_dim(left, (2 * s + which) * part, part, 1)
            for s in range(shards)
        ],
        axis=1,
    )


def weight_halves(left, right):
    core = lax.axis_index("core")
    return [
        t_dot(cut_columns(left, which), right).astype(BF16) for which in (1 - core, core)
    ]


def side_parts(sent, kept):
    side = lax.axis_index("side")
    came = swap(sent, "core")
    half = kept.shape[0] // 2

    def cut(which):
        return add(
            lax.dynamic_slice_in_dim(kept, which * half, half, 0),
            lax.dynamic_slice_in_dim(came, which * half, half, 0),
        )

    return cut(1 - side), cut(side)


def side_sum(sent, kept, *after):
    total = add_after(kept, swap(sent, "side"), after)
    if lax.axis_size("rest") > 1:
        total = lax.psum_scatter(total, "rest", scatter_dimension=0, tiled=True)
    return total


def line_sum(*items):
    return lax.psum(items, ("half", "quad"))


def line_hop(block, pairs):
    return lax.ppermute(block, ("half", "quad"), pairs)


def line_sums(sides):
    inward, across, outward = [(0, 1), (3, 2)], [(1, 2), (2, 1)], [(1, 0), (2, 3)]
    inner = lax.axis_index("half") != lax.axis_index("quad")
    count = len(sides)
    totals, mark = [None] * count, ()
    results = []
    for turn in range(count + 2):
        if turn < count:
            totals[turn] = sides[turn](*mark)
            mark = (totals[turn],)
        for hops, at in ((inward, turn - 1), (across, turn - 2)):
            if 0 <= at < count:
                totals[at] = add_after(totals[at], line_hop(totals[at], hops), mark)
                mark = (totals[at],)
                if hops is across:
                    results.append(pick(inner, totals[at], line_hop(totals[at], outward)))
    return results


def join_cores(first, second):
    core = lax.axis_index("core")
    came = swap(pick(core == 0, second, first), "core")
    mine = pick(core == 0, first, second)
    return jnp.concatenate([pick(core == 0, mine, came), pick(core == 0, came, mine)], axis=0)


def swap_in(block):
    core, half = lax.axis_index("core"), lax.axis_index("half")
    micro, rows, wide = block.shape
    block = block.reshape(2, (micro // 2) * rows, wide)
    own = lax.dynamic_index_in_dim(block, half, 0, keepdims=False)
    other = lax.dynamic_index_in_dim(block, 1 - half, 0, keepdims=False)
    came = lax.ppermute(other, ("core", "half"), [(1, 2), (2, 1)])
    return pick(core == half, own, came)


def swap_out(first, second, micro):
    rows, wide = first.shape
    second_core, second_half = lax.axis_index("core") == 1, lax.axis_index("half") == 1
    mine, sent = in_order(second_core, first, second)
    parts = in_order(second_core, mine, swap(sent, "core"))
    mine, sent = in_order(second_half, *parts)
    clips = in_order(second_half, mine, swap(sent, "half"))
    return jnp.stack(clips).reshape(micro, 2 * rows // micro, wide)


def forward_layer(x, weights, clips, head, keep):
    joined, w_down, gains, shifts, b_qkv, b_out, b_down, b_up = weights
    grouped, normed_one = qkv_forward(x, gains[0:1], shifts[0:1], joined, b_qkv)
    grouped = spread(grouped)
    own = to_clips(grouped, clips)
    other = other_keys(grouped, own, clips)
    att, log_total = attend_forward(own, other, head)
    if callable(w_down):
        w_down = w_down(log_total)
        weights = (joined, w_down, *weights[2:])
    att = spread(to_tokens(att))
    y, *kept = feed_forward(
        x, att, joined, b_out, gains[1:2], shifts[1:2], b_up, w_down, b_down, keep
    )
    return y, (x, normed_one, own, other, log_total, *kept), weights


def attention_grads(kept, d_att, clips, head, after):
    own, other, log_total = kept[2:5]
    d_heads = to_clips(spread(d_att), clips)
    dq, kept_kv, sent_kv = attend_backward(own, other, d_heads, log_total, head, after)
    return (dq, *return_keys(kept_kv, sent_kv))


def spread_grads(grads, after=()):
    return spread(to_tokens(join_grads(*grads, after)))


def backward_lean(kept, g, weights, clips, head):
    x, _, _, _, _, x1, _, slope, _, _ = kept
    joined, w_down, gains = weights[:3]
    _, dx1, _, d_att, _, _ = feed_backward(g, slope, w_down, joined, x1, gains[1:2])
    d_tokens = spread_grads(attention_grads(kept, d_att, clips, head, ()))
    return qkv_backward(d_tokens, joined, x, dx1, gains[0:1])[0]


def small_rows(sums_one, sums_two, up_sum, shards, wide):
    rows = jnp.concatenate(
        [
            sums_one[0:1],
            sums_two[0:1],
            sums_one[1:2],
            sums_two[1:2],
            sums_one[2:4],
            sums_two[2:4],
        ]
    )
    rows = jnp.swapaxes(rows.reshape(8, shards, -1), 0, 1).reshape(shards, -1)
    packed = jnp.concatenate([rows, up_sum.reshape(shards, -1)], axis=1).astype(BF16)
    packed = packed.reshape(shards, 2, -1)
    lines = -(-packed.shape[2] // wide)
    room = 16 * (-(-lines // 16)) * wide
    packed = jnp.pad(packed, ((0, 0), (0, 0), (0, room - packed.shape[2])))
    return packed.reshape(shards, 2, -1, wide)


def beside(weight, *rows):
    shards, _, wide = rows[0].shape
    return jnp.concatenate([weight.reshape(shards, -1, wide), *rows], axis=1).reshape(-1, wide)


def rest_halves(normed_one, flat, out, sums_one, sums_two, up_sum, shards):
    core = lax.axis_index("core")
    wide = flat.shape[1]
    rows = small_rows(sums_one, sums_two, up_sum, shards, wide)
    return [
        beside(
            item,
            lax.dynamic_index_in_dim(rows, which, 1, keepdims=False),
            outs.reshape(shards, -1, wide),
        )
        for item, outs, which in zip(weight_halves(normed_one, flat), out, (1 - core, core))
    ]


def backward_all(kept_first, kept_second, g, layers, clips, head, shards):
    x, normed_one, _, _, _, x1, normed_two, slope, lifted, att = kept_second
    joined, w_down, gains = layers[1][:3]
    d_upper, dx1, branch, d_att, sums_two, up_sum = feed_backward(
        g, slope, w_down, joined, x1, gains[1:2]
    )
    down = weight_halves(lifted, g)
    up = weight_halves(normed_two, d_upper)
    grads = attention_grads(kept_second, d_att, clips, head, (*down, *up))
    down, up = side_parts(*down), side_parts(*up)
    d_tokens = spread_grads(grads, (*down, *up))
    out = weight_halves(att, branch)
    d_second, flat, sums_one = qkv_backward(d_tokens, joined, x, dx1, gains[0:1], out)
    rest = rest_halves(normed_one, flat, out, sums_one, sums_two, up_sum, shards)

    x, normed_one, _, _, _, x1, normed_two, slope, lifted, att = kept_first
    joined, w_down, gains = layers[0][:3]
    d_upper, dx1, branch, d_att, sums_two, up_sum = feed_backward(
        d_second, slope, w_down, joined, x1, gains[1:2]
    )
    down_one = weight_halves(lifted, d_second)
    up_one = weight_halves(normed_two, d_upper)
    rest = side_parts(*rest)
    grads = attention_grads(kept_first, d_att, clips, head, (*rest, *down_one, *up_one))
    down_two, up_two, rest_two = (side_sum(*item, grads[0]) for item in (down, up, rest))
    d_tokens = spread_grads(grads, (down_two, up_two, rest_two))
    seconds = line_sum(rest_two, up_two, down_two)
    down_one, up_one = side_parts(*down_one), side_parts(*up_one)
    out_one = weight_halves(att, branch)
    d_first, flat, sums_one = qkv_backward(
        d_tokens, joined, x, dx1, gains[0:1], (*down_one, *up_one, *out_one)
    )
    rest_one = rest_halves(normed_one, flat, out_one, sums_one, sums_two, up_sum, shards)
    rest_one = side_parts(*rest_one)
    sides = [
        lambda *after, item=item: side_sum(*item, *after, rest_one[0])
        for item in (down_one, up_one, rest_one)
    ]
    if lax.axis_size("quad") == 2:
        firsts = line_sums(sides)
    else:
        firsts = line_sum(*(item() for item in sides))
    firsts = (firsts[2], firsts[1], firsts[0])
    return d_first, d_second, [join_cores(a, b) for a, b in zip(firsts, seconds)]


def gather_small(block):
    core, side = lax.axis_index("core"), lax.axis_index("side")
    if lax.axis_size("rest") > 1:
        whole_block = lax.all_gather(block, ("core", "side", "rest"), axis=0, tiled=False)
        return whole_block.reshape(2, -1, block.shape[0])
    came = swap(block, "side")
    layer = jnp.stack([pick(side == 0, block, came), pick(side == 0, came, block)])
    came = swap(layer, "core")
    return jnp.stack([pick(core == 0, layer, came), pick(core == 0, came, layer)])


def per_device(
    frames, out_grad, norm_gain, norm_bias, w_qkv, w_out, w_up, w_down, proj_bias, up_bias
):
    pairs = lax.axis_size("pair")
    pair = lax.axis_index("pair")
    shards = lax.axis_size("side") * lax.axis_size("rest")
    micro, _, width = frames.shape
    clips = micro // 2
    head = width // HEADS
    part = width // shards

    joined = gather_weight(w_qkv[0], w_out[0], w_up[0])
    near, mine, second_down = start_downs(w_down[0], joined[:1])
    downs = [lambda *after: finish_down(near, mine, after), lambda *after: second_down]
    small = jnp.concatenate(
        [norm_gain.reshape(-1), norm_bias.reshape(-1), proj_bias.reshape(-1), up_bias.reshape(-1)]
    )
    small = gather_small(small).astype(F32)
    rows = jnp.swapaxes(small[:, :, : 8 * part].reshape(2, shards, 8, part), 1, 2)
    rows = rows.reshape(2, 8, width)
    ups = small[:, :, 8 * part :].reshape(2, 1, -1)
    x_start = swap_in(frames)
    layers = []
    for layer in range(2):
        r = rows[layer]
        b_qkv = jnp.concatenate([r[4:5], jnp.zeros_like(r[4:5]), r[5:6]], axis=1)
        layers.append(
            (joined[layer], downs[layer], r[0:2], r[2:4], b_qkv, r[6:7], r[7:8], ups[layer])
        )

    x = x_start
    for phase in range(pairs):
        if phase > 0:
            came = lax.ppermute(second, "pair", [(i, i + 1) for i in range(pairs - 1)])
            x = pick(pair == 0, x_start, came)
        keep = phase == pairs - 1
        first, kept_first, layers[0] = forward_layer(x, layers[0], clips, head, keep)
        second, kept_second, layers[1] = forward_layer(first, layers[1], clips, head, keep)
    hidden = swap_out(first, second, micro)

    g_start = swap_in(out_grad)
    g = g_start
    for phase in range(pairs - 1):
        d_second = backward_lean(kept_second, g, layers[1], clips, head)
        d_first = backward_lean(kept_first, d_second, layers[0], clips, head)
        came = lax.ppermute(d_first, "pair", [(i + 1, i) for i in range(pairs - 1)])
        g = pick(pair == pairs - 1, g_start, came)
    d_first, d_second, (rest, up, down) = backward_all(
        kept_first, kept_second, g, layers, clips, head, shards
    )
    input_grads = swap_out(d_first, d_second, micro)

    own_rows = part // 2
    rest = rest.reshape(2, -1, 3 * width)
    out_rows = own_rows // 3
    qkv = rest[:, :own_rows].reshape(-1, 3 * width)
    out = rest[:, rest.shape[1] - out_rows :].reshape(-1, width)
    packed = rest[:, own_rows : rest.shape[1] - out_rows].astype(F32)
    packed = packed.reshape(2, -1)[:, : (8 * part + up_bias.shape[1]) // 2].reshape(-1)
    heads = packed[: 8 * part].reshape(8, part)
    return (
        hidden[None],
        input_grads[None],
        heads[0:2][None],
        heads[2:4][None],
        qkv.astype(F32)[None],
        out.astype(F32)[None],
        up.astype(F32)[None],
        down.astype(F32)[None],
        heads[4:8][None],
        packed[8 * part :][None],
    )


def solution(mesh):
    sections, groups, shards = (mesh.shape[name] for name in ("section", "seq", "shard"))
    cut = Mesh(
        mesh.devices.reshape(sections // 2, 2, 2, groups // 2, 2, shards // 2),
        AXES,
    )
    section, seq, shard = ("pair", "core"), ("half", "quad"), ("side", "rest")
    rows = seq + shard
    return jax.shard_map(
        per_device,
        mesh=cut,
        in_specs=(
            P(None, rows, None),
            P(None, rows, None),
            P(section, None, shard),
            P(section, None, shard),
            P(section, shard, None),
            P(section, shard, None),
            P(section, shard, None),
            P(section, shard, None),
            P(section, None, shard),
            P(section, shard),
        ),
        out_specs=(
            P(section, None, rows, None),
            P(section, None, rows, None),
            P(section, None, shard),
            P(section, None, shard),
            P(section, shard, None),
            P(section, shard, None),
            P(section, shard, None),
            P(section, shard, None),
            P(section, None, shard),
            P(section, shard),
        ),
        check_vma=False,
    )
```

```python
import math

import jax
import jax.numpy as jnp
from jax import lax
from jax.experimental import pallas as pl
from jax.experimental.pallas import tpu as pltpu
from jax.sharding import Mesh
from jax.sharding import PartitionSpec as P

HEADS = 12
norm_eps = 1e-05
F32 = jnp.float32
BF16 = jnp.bfloat16
VMEM_LIMIT = 56 * 1024 * 1024
AXES = ("pair", "core", "half", "quad", "side", "rest")
HEAD_GROUPS = 4
ROW_BLOCKS = (272, 256, 192, 128, 96, 80, 64, 48)


def call(body, out_shapes, grid=None, in_specs=None, out_specs=None, scratch=(), flops=0, moved=0):
    extra = {} if grid is None else dict(grid=grid, in_specs=in_specs, out_specs=out_specs)
    return pl.pallas_call(
        body,
        out_shape=out_shapes,
        scratch_shapes=scratch,
        compiler_params=pltpu.CompilerParams(vmem_limit_bytes=VMEM_LIMIT),
        cost_estimate=pl.CostEstimate(flops=flops, bytes_accessed=moved, transcendentals=0),
        **extra,
    )


def dot(left, right):
    return jnp.dot(left, right, preferred_element_type=F32)


def dot_t(left, right):
    return lax.dot_general(left, right, (((1,), (1,)), ((), ())), preferred_element_type=F32)


def t_dot(left, right):
    return lax.dot_general(left, right, (((0,), (0,)), ((), ())), preferred_element_type=F32)


def norm_parts(values):
    center = values - jnp.mean(values, axis=-1, keepdims=True)
    inverse = lax.rsqrt(jnp.mean(center * center, axis=-1, keepdims=True) + norm_eps)
    return center * inverse, inverse


def norm_back(upstream, scaled, inverse, gain_row):
    weighted = upstream * gain_row
    return inverse * (
        weighted
        - jnp.mean(weighted, axis=-1, keepdims=True)
        - scaled * jnp.mean(weighted * scaled, axis=-1, keepdims=True)
    )


def qkv_body(x_ref, gain_ref, shift_ref, w_ref, bias_ref, out_ref, normed_ref):
    scaled, _ = norm_parts(x_ref[...].astype(F32))
    normed = (scaled * gain_ref[...] + shift_ref[...]).astype(BF16)
    normed_ref[...] = normed
    span = out_ref.shape[2] // 3
    width = x_ref.shape[1]
    for part in range(3):
        cols = slice(part * width, (part + 1) * width)
        piece = (dot(normed, w_ref[:, cols]) + bias_ref[:, cols]).astype(BF16)
        for g in range(HEAD_GROUPS):
            out_ref[g, :, part * span : (part + 1) * span] = piece[:, g * span : (g + 1) * span]


def qkv_forward(x, gain, shift, joined, bias):
    rows, width = x.shape
    span = width // HEAD_GROUPS
    return call(
        qkv_body,
        (
            jax.ShapeDtypeStruct((HEAD_GROUPS, rows, 3 * span), BF16),
            jax.ShapeDtypeStruct((rows, width), BF16),
        ),
        grid=(1,),
        in_specs=[
            whole((rows, width)),
            whole((1, width)),
            whole((1, width)),
            whole((width, 3 * width)),
            whole((1, 3 * width)),
        ],
        out_specs=(whole((HEAD_GROUPS, rows, 3 * span)), whole((rows, width))),
        flops=2 * rows * width * 3 * width,
        moved=6 * width * width + 10 * x.size,
    )(x, gain, shift, joined, bias)


def key_chunks(own_ref, other_ref):
    place = 0
    for ref in (own_ref, other_ref):
        total = ref.shape[1]
        step = 256 if total % 256 == 0 else total
        for start in range(0, total, step):
            yield ref, start, place, step
            place += step


def attend_body(q_ref, own_ref, other_ref, out_ref, log_ref, score_ref, *, head):
    span = q_ref.shape[2] // 3
    queries = q_ref.shape[1]
    scale = 1.0 / math.sqrt(head)
    for h in range(span // head):
        q = q_ref[0, :, h * head : (h + 1) * head] * scale
        top = jnp.full((1, queries), -jnp.inf, F32)
        for ref, start, place, step in key_chunks(own_ref, other_ref):
            k = ref[0, start : start + step, span + h * head : span + (h + 1) * head]
            scores = dot_t(k, q)
            score_ref[place : place + step, :] = scores
            top = jnp.maximum(top, jnp.max(scores, axis=0, keepdims=True))
        total = jnp.zeros((1, queries), F32)
        acc = jnp.zeros((head, queries), F32)
        for ref, start, place, step in key_chunks(own_ref, other_ref):
            v = ref[0, start : start + step, 2 * span + h * head : 2 * span + (h + 1) * head]
            e = jnp.exp(score_ref[place : place + step, :] - top)
            total = total + jnp.sum(e, axis=0, keepdims=True)
            acc = acc + t_dot(v, e.astype(BF16))
        out_ref[0, :, h * head : (h + 1) * head] = jnp.transpose(acc / total).astype(BF16)
        log_ref[0, h : h + 1, :] = top + jnp.log(total)


def query_block(queries):
    return 256 if queries % 256 == 0 else queries


def attend_forward(own, other, head):
    clips, queries, wide = own.shape
    span = wide // 3
    keys = queries + other.shape[1]
    block = query_block(queries)

    def body(*refs):
        attend_body(*refs, head=head)

    return call(
        body,
        (
            jax.ShapeDtypeStruct((clips, queries, span), BF16),
            jax.ShapeDtypeStruct((clips, span // head, queries), F32),
        ),
        grid=(clips, queries // block),
        in_specs=[
            pl.BlockSpec((1, block, wide), lambda m, i: (m, i, 0)),
            pl.BlockSpec((1, queries, wide), lambda m, i: (m, 0, 0)),
            pl.BlockSpec((1, other.shape[1], wide), lambda m, i: (m, 0, 0)),
        ],
        out_specs=(
            pl.BlockSpec((1, block, span), lambda m, i: (m, i, 0)),
            pl.BlockSpec((1, span // head, block), lambda m, i: (m, 0, i)),
        ),
        scratch=[pltpu.VMEM((keys, block), F32)],
        flops=16 * clips * queries * keys * span,
        moved=4 * (own.size + other.size),
    )(own, own, other)


def attend_back_body(
    q_ref,
    own_ref,
    other_ref,
    grad_ref,
    log_ref,
    dq_ref,
    dkv_own_ref,
    dkv_other_ref,
    p_ref,
    dp_ref,
    dk_acc,
    dv_acc,
    *,
    head,
):
    span = q_ref.shape[2] // 3
    queries = q_ref.shape[1]
    heads = span // head
    scale = 1.0 / math.sqrt(head)

    @pl.when(pl.program_id(1) == 0)
    def _():
        dk_acc[...] = jnp.zeros_like(dk_acc)
        dv_acc[...] = jnp.zeros_like(dv_acc)

    for h in range(heads):
        q = q_ref[0, :, h * head : (h + 1) * head] * scale
        d_out = grad_ref[0, :, h * head : (h + 1) * head]
        log_total = log_ref[0, h : h + 1, :]
        row_term = jnp.zeros((1, queries), F32)
        for ref, start, place, step in key_chunks(own_ref, other_ref):
            k = ref[0, start : start + step, span + h * head : span + (h + 1) * head]
            v = ref[0, start : start + step, 2 * span + h * head : 2 * span + (h + 1) * head]
            probs = jnp.exp(dot_t(k, q) - log_total)
            d_probs = dot_t(v, d_out)
            p_ref[place : place + step, :] = probs
            dp_ref[place : place + step, :] = d_probs
            row_term = row_term + jnp.sum(probs * d_probs, axis=0, keepdims=True)
            dv_acc[h, place : place + step, :] += dot(probs.astype(BF16), d_out)
        dq = jnp.zeros((head, queries), F32)
        for ref, start, place, step in key_chunks(own_ref, other_ref):
            k = ref[0, start : start + step, span + h * head : span + (h + 1) * head]
            d_scores = (
                p_ref[place : place + step, :] * (dp_ref[place : place + step, :] - row_term)
            ).astype(BF16)
            dk_acc[h, place : place + step, :] += dot(d_scores, q)
            dq = dq + t_dot(k, d_scores)
        dq_ref[0, :, h * head : (h + 1) * head] = jnp.transpose(dq * scale).astype(BF16)

    @pl.when(pl.program_id(1) == pl.num_programs(1) - 1)
    def _():
        place = 0
        for ref in (dkv_own_ref, dkv_other_ref):
            rows = ref.shape[1]
            for h in range(heads):
                ref[0, :, h * head : (h + 1) * head] = dk_acc[h, place : place + rows, :].astype(
                    ref.dtype
                )
                ref[0, :, span + h * head : span + (h + 1) * head] = dv_acc[
                    h, place : place + rows, :
                ].astype(ref.dtype)
            place += rows


def attend_backward(own, other, grad, log_total, head, after=()):
    clips, queries, wide = own.shape
    span = wide // 3
    others = other.shape[1]
    keys = queries + others
    block = query_block(queries)
    heads = span // head

    def body(*refs):
        attend_back_body(*refs[:5], *refs[5 + len(after) :], head=head)

    return call(
        body,
        (
            jax.ShapeDtypeStruct((clips, queries, span), BF16),
            jax.ShapeDtypeStruct((clips, queries, 2 * span), F32),
            jax.ShapeDtypeStruct((clips, others, 2 * span), BF16),
        ),
        grid=(clips, queries // block),
        in_specs=[
            pl.BlockSpec((1, block, wide), lambda m, i: (m, i, 0)),
            pl.BlockSpec((1, queries, wide), lambda m, i: (m, 0, 0)),
            pl.BlockSpec((1, others, wide), lambda m, i: (m, 0, 0)),
            pl.BlockSpec((1, block, span), lambda m, i: (m, i, 0)),
            pl.BlockSpec((1, heads, block), lambda m, i: (m, 0, i)),
        ]
        + [pl.BlockSpec(memory_space=pl.ANY)] * len(after),
        out_specs=(
            pl.BlockSpec((1, block, span), lambda m, i: (m, i, 0)),
            pl.BlockSpec((1, queries, 2 * span), lambda m, i: (m, 0, 0)),
            pl.BlockSpec((1, others, 2 * span), lambda m, i: (m, 0, 0)),
        ),
        scratch=[
            pltpu.VMEM((keys, block), F32),
            pltpu.VMEM((keys, block), F32),
            pltpu.VMEM((heads, keys, head), F32),
            pltpu.VMEM((heads, keys, head), F32),
        ],
        flops=40 * clips * queries * keys * span,
        moved=8 * (own.size + other.size),
    )(own, own, other, grad, log_total, *after)


def feed_body(
    x_ref,
    att_ref,
    w_out_ref,
    b_out_ref,
    gain_ref,
    shift_ref,
    w_up_ref,
    b_up_ref,
    w_down_ref,
    b_down_ref,
    y_ref,
    *rest,
):
    if len(rest) > 2:
        x1_ref, normed_ref, slope_ref, lifted_ref, flat_ref, acc = rest
    else:
        normed_ref, acc = rest
    span = att_ref.shape[2]

    @pl.when(pl.program_id(0) == 0)
    def _():
        middle = x_ref[...].astype(F32) + b_out_ref[...]
        for g in range(HEAD_GROUPS):
            middle = middle + dot(att_ref[g], w_out_ref[g * span : (g + 1) * span, :])
            if len(rest) > 2:
                flat_ref[:, g * span : (g + 1) * span] = att_ref[g]
        if len(rest) > 2:
            x1_ref[...] = middle
        scaled, _ = norm_parts(middle)
        normed_ref[...] = (scaled * gain_ref[...] + shift_ref[...]).astype(BF16)
        acc[...] = middle + b_down_ref[...]

    upper = dot(normed_ref[...], w_up_ref[...]) + b_up_ref[...]
    phi = 0.5 * (1.0 + lax.erf(upper * math.sqrt(0.5)))
    lifted = (upper * phi).astype(BF16)
    if len(rest) > 2:
        density = jnp.exp(-0.5 * upper * upper) * (1.0 / math.sqrt(2.0 * math.pi))
        slope_ref[...] = phi + upper * density
        lifted_ref[...] = lifted
    acc[...] += dot(lifted, w_down_ref[...])

    @pl.when(pl.program_id(0) == pl.num_programs(0) - 1)
    def _():
        y_ref[...] = acc[...].astype(BF16)


def whole(shape):
    return pl.BlockSpec(shape, lambda i: (0,) * len(shape))


def feed_forward(x, att, joined, b_out, gain, shift, b_up, w_down, b_down, keep):
    rows, width = x.shape
    hidden = w_down.shape[0]
    row = whole((1, width))
    full = whole((rows, width))
    part = pl.BlockSpec((rows, width), lambda i: (0, i))
    shapes = [jax.ShapeDtypeStruct((rows, width), BF16)]
    specs = [full]
    scratch = [pltpu.VMEM((rows, width), F32)]
    if keep:
        shapes += [
            jax.ShapeDtypeStruct((rows, width), F32),
            jax.ShapeDtypeStruct((rows, width), BF16),
            jax.ShapeDtypeStruct((rows, hidden), F32),
            jax.ShapeDtypeStruct((rows, hidden), BF16),
            jax.ShapeDtypeStruct((rows, width), BF16),
        ]
        specs += [full, full, part, part, full]
    else:
        scratch = [pltpu.VMEM((rows, width), BF16)] + scratch
    return call(
        feed_body,
        tuple(shapes),
        grid=(hidden // width,),
        in_specs=[
            full,
            whole(att.shape),
            pl.BlockSpec((width, width), lambda i: (0, 3)),
            row,
            row,
            row,
            pl.BlockSpec((width, width), lambda i: (0, 4 + i)),
            pl.BlockSpec((1, width), lambda i: (0, i)),
            pl.BlockSpec((width, width), lambda i: (i, 0)),
            row,
        ],
        out_specs=tuple(specs),
        scratch=scratch,
        flops=2 * rows * width * (2 * hidden + width),
        moved=4 * w_down.size + 2 * width * width + 10 * rows * hidden,
    )(x, att, joined, b_out, gain, shift, joined, b_up, w_down, b_down)


def feed_back_body(
    g_ref,
    slope_ref,
    w_down_ref,
    w_up_ref,
    w_out_ref,
    x1_ref,
    gain_ref,
    d_upper_ref,
    dx1_ref,
    branch_ref,
    datt_ref,
    sums_ref,
    up_sum_ref,
    acc,
):
    @pl.when(pl.program_id(0) == 0)
    def _():
        acc[...] = jnp.zeros_like(acc)

    d_upper = (dot_t(g_ref[...], w_down_ref[...]) * slope_ref[...]).astype(BF16)
    d_upper_ref[...] = d_upper
    up_sum_ref[...] = jnp.sum(d_upper.astype(F32), axis=0, keepdims=True)
    acc[...] += dot_t(d_upper, w_up_ref[...])

    @pl.when(pl.program_id(0) == pl.num_programs(0) - 1)
    def _():
        d_normed = acc[...]
        upstream = g_ref[...].astype(F32)
        scaled, inverse = norm_parts(x1_ref[...])
        d_middle = upstream + norm_back(d_normed, scaled, inverse, gain_ref[...])
        dx1_ref[...] = d_middle
        branch = d_middle.astype(BF16)
        branch_ref[...] = branch
        span = datt_ref.shape[2]
        for g in range(HEAD_GROUPS):
            datt_ref[g] = dot_t(branch, w_out_ref[g * span : (g + 1) * span, :]).astype(BF16)
        sums_ref[0:1, :] = jnp.sum(d_normed * scaled, axis=0, keepdims=True)
        sums_ref[1:2, :] = jnp.sum(d_normed, axis=0, keepdims=True)
        sums_ref[2:3, :] = jnp.sum(branch.astype(F32), axis=0, keepdims=True)
        sums_ref[3:4, :] = jnp.sum(upstream, axis=0, keepdims=True)


def feed_backward(g, slope, w_down, joined, x1, gain):
    rows, width = g.shape
    hidden = w_down.shape[0]
    chunk = width
    full = whole((rows, width))
    return call(
        feed_back_body,
        (
            jax.ShapeDtypeStruct((rows, hidden), BF16),
            jax.ShapeDtypeStruct((rows, width), F32),
            jax.ShapeDtypeStruct((rows, width), BF16),
            jax.ShapeDtypeStruct((HEAD_GROUPS, rows, width // HEAD_GROUPS), BF16),
            jax.ShapeDtypeStruct((4, width), F32),
            jax.ShapeDtypeStruct((1, hidden), F32),
        ),
        grid=(hidden // chunk,),
        in_specs=[
            full,
            pl.BlockSpec((rows, chunk), lambda i: (0, i)),
            pl.BlockSpec((chunk, width), lambda i: (i, 0)),
            pl.BlockSpec((width, chunk), lambda i: (0, 4 + i)),
            pl.BlockSpec((width, width), lambda i: (0, 3)),
            full,
            whole((1, width)),
        ],
        out_specs=(
            pl.BlockSpec((rows, chunk), lambda i: (0, i)),
            full,
            full,
            whole((HEAD_GROUPS, rows, width // HEAD_GROUPS)),
            whole((4, width)),
            pl.BlockSpec((1, chunk), lambda i: (0, i)),
        ),
        scratch=[pltpu.VMEM((rows, width), F32)],
        flops=2 * rows * width * (2 * hidden + width),
        moved=4 * w_down.size + 2 * width * width + 6 * rows * hidden,
    )(g, slope, w_down, joined, joined, x1, gain)


def qkv_back_body(grads_ref, w_ref, x_ref, dx1_ref, gain_ref, dx_ref, flat_ref, sums_ref):
    width = x_ref.shape[1]
    span = grads_ref.shape[2] // 3
    for g in range(HEAD_GROUPS):
        for part in range(3):
            flat_ref[:, part * width + g * span : part * width + (g + 1) * span] = grads_ref[
                g, :, part * span : (part + 1) * span
            ]
    d_normed = dot_t(flat_ref[...], w_ref[...])
    scaled, inverse = norm_parts(x_ref[...].astype(F32))
    dx = dx1_ref[...] + norm_back(d_normed, scaled, inverse, gain_ref[...])
    dx_ref[...] = dx.astype(BF16)
    sums_ref[0:1, :] = jnp.sum(d_normed * scaled, axis=0, keepdims=True)
    sums_ref[1:2, :] = jnp.sum(d_normed, axis=0, keepdims=True)
    sums_ref[2:3, :] = jnp.sum(flat_ref[:, :width].astype(F32), axis=0, keepdims=True)
    sums_ref[3:4, :] = jnp.sum(flat_ref[:, 2 * width :].astype(F32), axis=0, keepdims=True)


def qkv_backward(grads, joined, x, dx1, gain, after=()):
    rows, width = x.shape

    def body(*refs):
        qkv_back_body(*refs[:5], *refs[5 + len(after) :])

    return call(
        body,
        (
            jax.ShapeDtypeStruct((rows, width), BF16),
            jax.ShapeDtypeStruct((rows, 3 * width), BF16),
            jax.ShapeDtypeStruct((4, width), F32),
        ),
        grid=(1,),
        in_specs=[
            whole(grads.shape),
            whole((width, 3 * width)),
            whole((rows, width)),
            whole((rows, width)),
            whole((1, width)),
        ]
        + [pl.BlockSpec(memory_space=pl.ANY)] * len(after),
        out_specs=(whole((rows, width)), whole((rows, 3 * width)), whole((4, width))),
        flops=2 * rows * width * 3 * width,
        moved=6 * width * width + 20 * x.size,
    )(grads, joined, x, dx1, gain, *after)


def add_body(one_ref, two_ref, *rest):
    rest[-1][...] = (one_ref[...].astype(F32) + two_ref[...].astype(F32)).astype(BF16)


def add_after(one, two, after):
    rows, wide = one.shape
    block = next((n for n in ROW_BLOCKS if rows % n == 0), rows)
    spec = pl.BlockSpec((block, wide), lambda i: (i, 0))
    return call(
        add_body,
        jax.ShapeDtypeStruct((rows, wide), BF16),
        grid=(rows // block,),
        in_specs=[spec, spec] + [pl.BlockSpec(memory_space=pl.ANY)] * len(after),
        out_specs=spec,
        flops=one.size,
        moved=6 * one.size,
    )(one, two, *after)


def copy_body(one_ref, *rest):
    rest[-1][...] = one_ref[...]


def copy_after(one, after):
    spec = pl.BlockSpec(one.shape, lambda i: (0, 0))
    return call(
        copy_body,
        jax.ShapeDtypeStruct(one.shape, one.dtype),
        grid=(1,),
        in_specs=[spec] + [pl.BlockSpec(memory_space=pl.ANY)] * len(after),
        out_specs=spec,
        flops=one.size,
        moved=4 * one.size,
    )(one, *after)


def join_body(dq_ref, kept_ref, back_ref, *rest):
    out_ref = rest[-1]
    span = dq_ref.shape[2]
    out_ref[:, :, :span] = dq_ref[...]
    out_ref[:, :, span:] = (kept_ref[...] + back_ref[...].astype(F32)).astype(BF16)


def join_grads(dq, kept, back, after):
    clips, rows, span = dq.shape

    def spec(wide):
        return pl.BlockSpec((1, rows, wide), lambda i: (i, 0, 0))

    return call(
        join_body,
        jax.ShapeDtypeStruct((clips, rows, 3 * span), BF16),
        grid=(clips,),
        in_specs=[spec(span), spec(2 * span), spec(2 * span)]
        + [pl.BlockSpec(memory_space=pl.ANY)] * len(after),
        out_specs=spec(3 * span),
        flops=kept.size,
        moved=8 * kept.size,
    )(dq, kept, back, *after)


def swap(block, axis):
    return lax.ppermute(block, axis, [(0, 1), (1, 0)])


def shift(block, distance):
    count = lax.axis_size("rest")
    return lax.ppermute(block, "rest", [(i, (i + distance) % count) for i in range(count)])


def spread(block):
    return lax.all_to_all(block, ("quad", "side"), 0, 0, tiled=True)


def to_clips(block, clips):
    groups, rows, wide = block.shape
    if clips == 1:
        return block.reshape(1, groups * rows, wide)
    block = block.reshape(groups, clips, rows // clips, wide)
    return jnp.swapaxes(block, 0, 1).reshape(clips, groups * (rows // clips), wide)


def to_tokens(block):
    clips, rows, wide = block.shape
    if clips == 1:
        return block.reshape(HEAD_GROUPS, rows // HEAD_GROUPS, wide)
    block = block.reshape(clips, HEAD_GROUPS, rows // HEAD_GROUPS, wide)
    return jnp.swapaxes(block, 0, 1).reshape(HEAD_GROUPS, -1, wide)


def other_keys(grouped, own, clips):
    if lax.axis_size("rest") == 1:
        return to_clips(swap(grouped, "core"), clips)
    near = [shift(own, k) for k in range(1, lax.axis_size("rest"))]
    far = swap(jnp.concatenate([own] + near, axis=1), "core")
    return jnp.concatenate(near + [far], axis=1)


def return_keys(kept, sent):
    queries = kept.shape[1]
    count = lax.axis_size("rest")
    near = (count - 1) * queries
    back = swap(sent[:, near:], "core")
    total = kept
    for k in range(1, count):
        part = sent[:, (k - 1) * queries : k * queries].astype(F32)
        part = part + back[:, k * queries : (k + 1) * queries].astype(F32)
        total = total + shift(part.astype(BF16), -k).astype(F32)
    return total, back[:, :queries]


def pick(flag, one, two):
    return jnp.where(flag, one, two)


def gather_weight(*blocks):
    core = lax.axis_index("core")
    quads = lax.axis_size("quad")
    part = blocks[0].shape[0] // (2 * quads)
    quad = lax.axis_index("quad")

    def cut(which):
        start = (which * quads + quad) * part
        return jnp.concatenate(
            [lax.dynamic_slice_in_dim(block, start, part, 0) for block in blocks], axis=1
        )

    own = cut(core)
    came = swap(cut(1 - core), "core")
    first = pick(core == 0, own, came)
    second = pick(core == 0, came, own)
    return [
        lax.all_gather(item, ("side", "rest", "core", "quad"), axis=0, tiled=True)
        for item in (first, second)
    ]


def in_order(second, mine, other):
    return pick(second, other, mine), pick(second, mine, other)


def start_downs(block, after):
    if lax.axis_size("rest") > 1 or lax.axis_size("quad") != 2:
        first, second = gather_weight(block)
        return None, first, second
    core, quad = lax.axis_index("core"), lax.axis_index("quad")
    part = block.shape[0] // 4
    mine, other = in_order(core == 1, block, swap(block, "core"))
    line = lax.dynamic_slice_in_dim(other, (core * 2 + quad) * part, part, 0)
    second = lax.all_gather(line, ("side", "rest", "core", "quad"), axis=0, tiled=True)
    near = lax.dynamic_slice_in_dim(mine, core * 2 * part, 2 * part, 0)
    return swap(copy_after(near, after), "side"), mine, second


def finish_down(near, mine, after):
    if near is None:
        return mine
    core, side = lax.axis_index("core"), lax.axis_index("side")
    near = copy_after(near, after)
    other = jnp.concatenate(in_order(core == 1, near, swap(near, "core")), axis=0)
    return jnp.concatenate(in_order(side == 1, mine, other), axis=0)


def add(one, two):
    return (one.astype(F32) + two.astype(F32)).astype(one.dtype)


def cut_columns(left, which):
    shards = lax.axis_size("side") * lax.axis_size("rest")
    part = left.shape[1] // (2 * shards)
    return jnp.concatenate(
        [
            lax.dynamic_slice_in_dim(left, (2 * s + which) * part, part, 1)
            for s in range(shards)
        ],
        axis=1,
    )


def weight_halves(left, right):
    core = lax.axis_index("core")
    return [
        t_dot(cut_columns(left, which), right).astype(BF16) for which in (1 - core, core)
    ]


def parts_body(side_ref, *refs):
    far_one, far_two, near_one, near_two = refs[:4]
    sent_ref, kept_ref = refs[-2:]
    sent_ref[...] = (far_one[...].astype(F32) + far_two[...].astype(F32)).astype(BF16)
    kept_ref[...] = (near_one[...].astype(F32) + near_two[...].astype(F32)).astype(BF16)


def side_parts(sent, kept, *after):
    came = swap(sent, "core")
    rows, wide = kept.shape
    half = rows // 2
    block = next((n for n in ROW_BLOCKS if half % n == 0), half)
    steps = half // block
    far = pl.BlockSpec((block, wide), lambda i, side: ((1 - side[0]) * steps + i, 0))
    near = pl.BlockSpec((block, wide), lambda i, side: (side[0] * steps + i, 0))
    out = pl.BlockSpec((block, wide), lambda i, side: (i, 0))
    return pl.pallas_call(
        parts_body,
        out_shape=(jax.ShapeDtypeStruct((half, wide), BF16),) * 2,
        grid_spec=pltpu.PrefetchScalarGridSpec(
            num_scalar_prefetch=1,
            grid=(steps,),
            in_specs=[far, far, near, near]
            + [pl.BlockSpec(memory_space=pl.ANY)] * len(after),
            out_specs=(out, out),
        ),
        compiler_params=pltpu.CompilerParams(vmem_limit_bytes=VMEM_LIMIT),
        cost_estimate=pl.CostEstimate(
            flops=kept.size, bytes_accessed=6 * kept.size, transcendentals=0
        ),
    )(lax.axis_index("side").astype(jnp.int32).reshape(1), kept, came, kept, came, *after)


def side_sum(sent, kept, *after):
    total = add_after(kept, swap(sent, "side"), after)
    if lax.axis_size("rest") > 1:
        total = lax.psum_scatter(total, "rest", scatter_dimension=0, tiled=True)
    return total


def line_sum(*items):
    return lax.psum(items, ("half", "quad"))


def line_hop(block, pairs):
    return lax.ppermute(block, ("half", "quad"), pairs)


def line_sums(sides, last):
    inward, across, outward = [(0, 1), (3, 2)], [(1, 2), (2, 1)], [(1, 0), (2, 3)]
    inner = lax.axis_index("half") != lax.axis_index("quad")
    count = len(sides)
    totals, mark = [None] * count, ()
    results = []
    for turn in range(count + 2):
        if turn < count:
            totals[turn] = sides[turn](*mark)
            mark = (totals[turn],)
        for hops, at in ((inward, turn - 1), (across, turn - 2)):
            if 0 <= at < count:
                if turn == count + 1:
                    mark = (*mark, *last)
                totals[at] = add_after(totals[at], line_hop(totals[at], hops), mark)
                mark = (totals[at],)
                if hops is across:
                    results.append(pick(inner, totals[at], line_hop(totals[at], outward)))
    return results, mark[0]


def join_cores(first, second):
    core = lax.axis_index("core")
    came = swap(pick(core == 0, second, first), "core")
    mine = pick(core == 0, first, second)
    return jnp.concatenate([pick(core == 0, mine, came), pick(core == 0, came, mine)], axis=0)


def swap_in(block):
    core, half = lax.axis_index("core"), lax.axis_index("half")
    micro, rows, wide = block.shape
    block = block.reshape(2, (micro // 2) * rows, wide)
    own = lax.dynamic_index_in_dim(block, half, 0, keepdims=False)
    other = lax.dynamic_index_in_dim(block, 1 - half, 0, keepdims=False)
    came = lax.ppermute(other, ("core", "half"), [(1, 2), (2, 1)])
    return pick(core == half, own, came)


def swap_out(first, second, micro, *after):
    rows, wide = first.shape
    second_core, second_half = lax.axis_index("core") == 1, lax.axis_index("half") == 1
    mine, sent = in_order(second_core, first, second)
    parts = in_order(second_core, mine, swap(sent, "core"))
    mine, sent = in_order(second_half, *parts)
    came = swap(sent, "half")
    if after:
        came = copy_after(came, after)
    clips = in_order(second_half, mine, came)
    return jnp.stack(clips).reshape(micro, 2 * rows // micro, wide)


def forward_layer(x, weights, clips, head, keep):
    joined, w_down, gains, shifts, b_qkv, b_out, b_down, b_up = weights
    grouped, normed_one = qkv_forward(x, gains[0:1], shifts[0:1], joined, b_qkv)
    grouped = spread(grouped)
    own = to_clips(grouped, clips)
    other = other_keys(grouped, own, clips)
    att, log_total = attend_forward(own, other, head)
    if callable(w_down):
        w_down = w_down(log_total)
        weights = (joined, w_down, *weights[2:])
    att = spread(to_tokens(att))
    y, *kept = feed_forward(
        x, att, joined, b_out, gains[1:2], shifts[1:2], b_up, w_down, b_down, keep
    )
    return y, (x, normed_one, own, other, log_total, *kept), weights


def attention_grads(kept, d_att, clips, head, after):
    return heads_back(kept, to_clips(spread(d_att), clips), head, after)


def heads_back(kept, d_heads, head, after):
    own, other, log_total = kept[2:5]
    dq, kept_kv, sent_kv = attend_backward(own, other, d_heads, log_total, head, after)
    return (dq, *return_keys(kept_kv, sent_kv))


def spread_grads(grads, after=()):
    return spread(to_tokens(join_grads(*grads, after)))


def backward_lean(kept, g, weights, clips, head, *after):
    x, _, _, _, _, x1, _, slope, _, _ = kept
    joined, w_down, gains = weights[:3]
    _, dx1, _, d_att, _, _ = feed_backward(g, slope, w_down, joined, x1, gains[1:2])
    d_tokens = spread_grads(attention_grads(kept, d_att, clips, head, after))
    return qkv_backward(d_tokens, joined, x, dx1, gains[0:1])[0]


def small_rows(sums_one, sums_two, up_sum, shards, wide):
    rows = jnp.concatenate(
        [
            sums_one[0:1],
            sums_two[0:1],
            sums_one[1:2],
            sums_two[1:2],
            sums_one[2:4],
            sums_two[2:4],
        ]
    )
    rows = jnp.swapaxes(rows.reshape(8, shards, -1), 0, 1).reshape(shards, -1)
    packed = jnp.concatenate([rows, up_sum.reshape(shards, -1)], axis=1).astype(BF16)
    packed = packed.reshape(shards, 2, -1)
    lines = -(-packed.shape[2] // wide)
    room = 16 * (-(-lines // 16)) * wide
    packed = jnp.pad(packed, ((0, 0), (0, 0), (0, room - packed.shape[2])))
    return packed.reshape(shards, 2, -1, wide)


def beside(weight, *rows):
    shards, _, wide = rows[0].shape
    return jnp.concatenate([weight.reshape(shards, -1, wide), *rows], axis=1).reshape(-1, wide)


def rest_halves(normed_one, flat, out, sums_one, sums_two, up_sum, shards):
    core = lax.axis_index("core")
    wide = flat.shape[1]
    rows = small_rows(sums_one, sums_two, up_sum, shards, wide)
    return [
        beside(
            item,
            lax.dynamic_index_in_dim(rows, which, 1, keepdims=False),
            outs.reshape(shards, -1, wide),
        )
        for item, outs, which in zip(weight_halves(normed_one, flat), out, (1 - core, core))
    ]


def backward_all(kept_first, kept_second, g, layers, clips, head, shards):
    x, normed_one, _, _, _, x1, normed_two, slope, lifted, att = kept_second
    joined, w_down, gains = layers[1][:3]
    d_upper, dx1, branch, d_att, sums_two, up_sum = feed_backward(
        g, slope, w_down, joined, x1, gains[1:2]
    )
    down = weight_halves(lifted, g)
    up = weight_halves(normed_two, d_upper)
    grads = attention_grads(kept_second, d_att, clips, head, (*down, *up))
    d_tokens = spread_grads(grads)
    out = weight_halves(att, branch)
    down = side_parts(*down, d_tokens)
    d_second, flat, sums_one = qkv_backward(
        d_tokens, joined, x, dx1, gains[0:1], (*down, *out)
    )
    rest = rest_halves(normed_one, flat, out, sums_one, sums_two, up_sum, shards)

    x, normed_one, _, _, _, x1, normed_two, slope, lifted, att = kept_first
    joined, w_down, gains = layers[0][:3]
    d_upper, dx1, branch, d_att, sums_two, up_sum = feed_backward(
        d_second, slope, w_down, joined, x1, gains[1:2]
    )
    down_one = weight_halves(lifted, d_second)
    up_one = weight_halves(normed_two, d_upper)
    d_heads = to_clips(spread(d_att), clips)
    up = side_parts(*up, d_heads)
    down_two = side_sum(*down)
    grads = heads_back(
        kept_first, d_heads, head, (down_two, *up, *rest, *down_one, *up_one)
    )
    rest = side_parts(*rest, grads[0])
    up_two = side_sum(*up, grads[0])
    d_tokens = spread_grads(grads, (up_two, *rest))
    rest_two = side_sum(*rest)
    down_one, up_one = side_parts(*down_one), side_parts(*up_one)
    out_one = weight_halves(att, branch)
    d_first, flat, sums_one = qkv_backward(
        d_tokens, joined, x, dx1, gains[0:1], (rest_two, *down_one, *up_one, *out_one)
    )
    seconds = line_sum(rest_two, up_two, down_two)
    rest_one = rest_halves(normed_one, flat, out_one, sums_one, sums_two, up_sum, shards)
    rest_one = side_parts(*rest_one)
    sides = [
        lambda *after, item=item: side_sum(*item, *after, rest_one[0])
        for item in (down_one, up_one, rest_one)
    ]
    if lax.axis_size("quad") == 2:
        firsts, mark = line_sums(sides, seconds)
    else:
        firsts = line_sum(*(item() for item in sides))
        mark = firsts[2]
    firsts = (firsts[2], firsts[1], firsts[0])
    return d_first, d_second, mark, [join_cores(a, b) for a, b in zip(firsts, seconds)]


def gather_small(block):
    core, side = lax.axis_index("core"), lax.axis_index("side")
    if lax.axis_size("rest") > 1:
        whole_block = lax.all_gather(block, ("core", "side", "rest"), axis=0, tiled=False)
        return whole_block.reshape(2, -1, block.shape[0])
    came = swap(block, "side")
    layer = jnp.stack([pick(side == 0, block, came), pick(side == 0, came, block)])
    came = swap(layer, "core")
    return jnp.stack([pick(core == 0, layer, came), pick(core == 0, came, layer)])


def per_device(
    frames, out_grad, norm_gain, norm_bias, w_qkv, w_out, w_up, w_down, proj_bias, up_bias
):
    pairs = lax.axis_size("pair")
    pair = lax.axis_index("pair")
    shards = lax.axis_size("side") * lax.axis_size("rest")
    micro, _, width = frames.shape
    clips = micro // 2
    head = width // HEADS
    part = width // shards

    joined = gather_weight(w_qkv[0], w_out[0], w_up[0])
    near, mine, second_down = start_downs(w_down[0], joined[:1])
    downs = [lambda *after: finish_down(near, mine, after), lambda *after: second_down]
    small = jnp.concatenate(
        [norm_gain.reshape(-1), norm_bias.reshape(-1), proj_bias.reshape(-1), up_bias.reshape(-1)]
    )
    small = gather_small(small).astype(F32)
    rows = jnp.swapaxes(small[:, :, : 8 * part].reshape(2, shards, 8, part), 1, 2)
    rows = rows.reshape(2, 8, width)
    ups = small[:, :, 8 * part :].reshape(2, 1, -1)
    x_start = swap_in(frames)
    layers = []
    for layer in range(2):
        r = rows[layer]
        b_qkv = jnp.concatenate([r[4:5], jnp.zeros_like(r[4:5]), r[5:6]], axis=1)
        layers.append(
            (joined[layer], downs[layer], r[0:2], r[2:4], b_qkv, r[6:7], r[7:8], ups[layer])
        )

    x = x_start
    for phase in range(pairs):
        if phase > 0:
            came = lax.ppermute(second, "pair", [(i, i + 1) for i in range(pairs - 1)])
            x = pick(pair == 0, x_start, came)
        keep = phase == pairs - 1
        first, kept_first, layers[0] = forward_layer(x, layers[0], clips, head, keep)
        second, kept_second, layers[1] = forward_layer(first, layers[1], clips, head, keep)
    hidden = swap_out(first, second, micro)

    g_start = swap_in(out_grad)
    g = g_start
    for phase in range(pairs - 1):
        d_second = backward_lean(kept_second, g, layers[1], clips, head, hidden)
        d_first = backward_lean(kept_first, d_second, layers[0], clips, head)
        came = lax.ppermute(d_first, "pair", [(i + 1, i) for i in range(pairs - 1)])
        g = pick(pair == pairs - 1, g_start, came)
    d_first, d_second, mark, (rest, up, down) = backward_all(
        kept_first, kept_second, g, layers, clips, head, shards
    )
    input_grads = swap_out(d_first, d_second, micro, mark)

    own_rows = part // 2
    rest = rest.reshape(2, -1, 3 * width)
    out_rows = own_rows // 3
    qkv = rest[:, :own_rows].reshape(-1, 3 * width)
    out = rest[:, rest.shape[1] - out_rows :].reshape(-1, width)
    packed = rest[:, own_rows : rest.shape[1] - out_rows].astype(F32)
    packed = packed.reshape(2, -1)[:, : (8 * part + up_bias.shape[1]) // 2].reshape(-1)
    heads = packed[: 8 * part].reshape(8, part)
    return (
        hidden[None],
        input_grads[None],
        heads[0:2][None],
        heads[2:4][None],
        qkv.astype(F32)[None],
        out.astype(F32)[None],
        up.astype(F32)[None],
        down.astype(F32)[None],
        heads[4:8][None],
        packed[8 * part :][None],
    )


def solution(mesh):
    sections, groups, shards = (mesh.shape[name] for name in ("section", "seq", "shard"))
    cut = Mesh(
        mesh.devices.reshape(sections // 2, 2, 2, groups // 2, 2, shards // 2),
        AXES,
    )
    section, seq, shard = ("pair", "core"), ("half", "quad"), ("side", "rest")
    rows = seq + shard
    return jax.shard_map(
        per_device,
        mesh=cut,
        in_specs=(
            P(None, rows, None),
            P(None, rows, None),
            P(section, None, shard),
            P(section, None, shard),
            P(section, shard, None),
            P(section, shard, None),
            P(section, shard, None),
            P(section, shard, None),
            P(section, None, shard),
            P(section, shard),
        ),
        out_specs=(
            P(section, None, rows, None),
            P(section, None, rows, None),
            P(section, None, shard),
            P(section, None, shard),
            P(section, shard, None),
            P(section, shard, None),
            P(section, shard, None),
            P(section, shard, None),
            P(section, None, shard),
            P(section, shard),
        ),
        check_vma=False,
    )
```

```python
import math

import jax
import jax.numpy as jnp
from jax import lax
from jax.experimental import pallas as pl
from jax.experimental.pallas import tpu as pltpu
from jax.sharding import Mesh
from jax.sharding import PartitionSpec as P

HEADS = 12
norm_eps = 1e-05
F32 = jnp.float32
BF16 = jnp.bfloat16
VMEM_LIMIT = 56 * 1024 * 1024
AXES = ("pair", "core", "half", "quad", "side", "rest")
HEAD_GROUPS = 4
ROW_BLOCKS = (272, 256, 192, 128, 96, 80, 64, 48)


def call(body, out_shapes, grid=None, in_specs=None, out_specs=None, scratch=(), flops=0, moved=0):
    extra = {} if grid is None else dict(grid=grid, in_specs=in_specs, out_specs=out_specs)
    return pl.pallas_call(
        body,
        out_shape=out_shapes,
        scratch_shapes=scratch,
        compiler_params=pltpu.CompilerParams(vmem_limit_bytes=VMEM_LIMIT),
        cost_estimate=pl.CostEstimate(flops=flops, bytes_accessed=moved, transcendentals=0),
        **extra,
    )


def dot(left, right):
    return jnp.dot(left, right, preferred_element_type=F32)


def dot_t(left, right):
    return lax.dot_general(left, right, (((1,), (1,)), ((), ())), preferred_element_type=F32)


def t_dot(left, right):
    return lax.dot_general(left, right, (((0,), (0,)), ((), ())), preferred_element_type=F32)


def norm_parts(values):
    center = values - jnp.mean(values, axis=-1, keepdims=True)
    inverse = lax.rsqrt(jnp.mean(center * center, axis=-1, keepdims=True) + norm_eps)
    return center * inverse, inverse


def norm_back(upstream, scaled, inverse, gain_row):
    weighted = upstream * gain_row
    return inverse * (
        weighted
        - jnp.mean(weighted, axis=-1, keepdims=True)
        - scaled * jnp.mean(weighted * scaled, axis=-1, keepdims=True)
    )


def qkv_body(x_ref, gain_ref, shift_ref, w_ref, bias_ref, out_ref, normed_ref):
    scaled, _ = norm_parts(x_ref[...].astype(F32))
    normed = (scaled * gain_ref[...] + shift_ref[...]).astype(BF16)
    normed_ref[...] = normed
    span = out_ref.shape[2] // 3
    width = x_ref.shape[1]
    for part in range(3):
        cols = slice(part * width, (part + 1) * width)
        piece = (dot(normed, w_ref[:, cols]) + bias_ref[:, cols]).astype(BF16)
        for g in range(HEAD_GROUPS):
            out_ref[g, :, part * span : (part + 1) * span] = piece[:, g * span : (g + 1) * span]


def qkv_forward(x, gain, shift, joined, bias):
    rows, width = x.shape
    span = width // HEAD_GROUPS
    return call(
        qkv_body,
        (
            jax.ShapeDtypeStruct((HEAD_GROUPS, rows, 3 * span), BF16),
            jax.ShapeDtypeStruct((rows, width), BF16),
        ),
        grid=(1,),
        in_specs=[
            whole((rows, width)),
            whole((1, width)),
            whole((1, width)),
            whole((width, 3 * width)),
            whole((1, 3 * width)),
        ],
        out_specs=(whole((HEAD_GROUPS, rows, 3 * span)), whole((rows, width))),
        flops=2 * rows * width * 3 * width,
        moved=6 * width * width + 10 * x.size,
    )(x, gain, shift, joined, bias)


def key_chunks(own_ref, other_ref):
    place = 0
    for ref in (own_ref, other_ref):
        total = ref.shape[1]
        step = 256 if total % 256 == 0 else total
        for start in range(0, total, step):
            yield ref, start, place, step
            place += step


def attend_body(q_ref, own_ref, other_ref, out_ref, log_ref, score_ref, *, head):
    span = q_ref.shape[2] // 3
    queries = q_ref.shape[1]
    scale = 1.0 / math.sqrt(head)
    for h in range(span // head):
        q = q_ref[0, :, h * head : (h + 1) * head] * scale
        top = jnp.full((1, queries), -jnp.inf, F32)
        for ref, start, place, step in key_chunks(own_ref, other_ref):
            k = ref[0, start : start + step, span + h * head : span + (h + 1) * head]
            scores = dot_t(k, q)
            score_ref[place : place + step, :] = scores
            top = jnp.maximum(top, jnp.max(scores, axis=0, keepdims=True))
        total = jnp.zeros((1, queries), F32)
        acc = jnp.zeros((head, queries), F32)
        for ref, start, place, step in key_chunks(own_ref, other_ref):
            v = ref[0, start : start + step, 2 * span + h * head : 2 * span + (h + 1) * head]
            e = jnp.exp(score_ref[place : place + step, :] - top)
            total = total + jnp.sum(e, axis=0, keepdims=True)
            acc = acc + t_dot(v, e.astype(BF16))
        out_ref[0, :, h * head : (h + 1) * head] = jnp.transpose(acc / total).astype(BF16)
        log_ref[0, h : h + 1, :] = top + jnp.log(total)


def query_block(queries):
    return 256 if queries % 256 == 0 else queries


def attend_forward(own, other, head):
    clips, queries, wide = own.shape
    span = wide // 3
    keys = queries + other.shape[1]
    block = query_block(queries)

    def body(*refs):
        attend_body(*refs, head=head)

    return call(
        body,
        (
            jax.ShapeDtypeStruct((clips, queries, span), BF16),
            jax.ShapeDtypeStruct((clips, span // head, queries), F32),
        ),
        grid=(clips, queries // block),
        in_specs=[
            pl.BlockSpec((1, block, wide), lambda m, i: (m, i, 0)),
            pl.BlockSpec((1, queries, wide), lambda m, i: (m, 0, 0)),
            pl.BlockSpec((1, other.shape[1], wide), lambda m, i: (m, 0, 0)),
        ],
        out_specs=(
            pl.BlockSpec((1, block, span), lambda m, i: (m, i, 0)),
            pl.BlockSpec((1, span // head, block), lambda m, i: (m, 0, i)),
        ),
        scratch=[pltpu.VMEM((keys, block), F32)],
        flops=16 * clips * queries * keys * span,
        moved=4 * (own.size + other.size),
    )(own, own, other)


def attend_back_body(
    q_ref,
    own_ref,
    other_ref,
    grad_ref,
    log_ref,
    dq_ref,
    dkv_own_ref,
    dkv_other_ref,
    p_ref,
    dp_ref,
    dk_acc,
    dv_acc,
    *,
    head,
):
    span = q_ref.shape[2] // 3
    queries = q_ref.shape[1]
    heads = span // head
    scale = 1.0 / math.sqrt(head)

    @pl.when(pl.program_id(1) == 0)
    def _():
        dk_acc[...] = jnp.zeros_like(dk_acc)
        dv_acc[...] = jnp.zeros_like(dv_acc)

    for h in range(heads):
        q = q_ref[0, :, h * head : (h + 1) * head] * scale
        d_out = grad_ref[0, :, h * head : (h + 1) * head]
        log_total = log_ref[0, h : h + 1, :]
        row_term = jnp.zeros((1, queries), F32)
        for ref, start, place, step in key_chunks(own_ref, other_ref):
            k = ref[0, start : start + step, span + h * head : span + (h + 1) * head]
            v = ref[0, start : start + step, 2 * span + h * head : 2 * span + (h + 1) * head]
            probs = jnp.exp(dot_t(k, q) - log_total)
            d_probs = dot_t(v, d_out)
            p_ref[place : place + step, :] = probs
            dp_ref[place : place + step, :] = d_probs
            row_term = row_term + jnp.sum(probs * d_probs, axis=0, keepdims=True)
            dv_acc[h, place : place + step, :] += dot(probs.astype(BF16), d_out)
        dq = jnp.zeros((head, queries), F32)
        for ref, start, place, step in key_chunks(own_ref, other_ref):
            k = ref[0, start : start + step, span + h * head : span + (h + 1) * head]
            d_scores = (
                p_ref[place : place + step, :] * (dp_ref[place : place + step, :] - row_term)
            ).astype(BF16)
            dk_acc[h, place : place + step, :] += dot(d_scores, q)
            dq = dq + t_dot(k, d_scores)
        dq_ref[0, :, h * head : (h + 1) * head] = jnp.transpose(dq * scale).astype(BF16)

    @pl.when(pl.program_id(1) == pl.num_programs(1) - 1)
    def _():
        place = 0
        for ref in (dkv_own_ref, dkv_other_ref):
            rows = ref.shape[1]
            for h in range(heads):
                ref[0, :, h * head : (h + 1) * head] = dk_acc[h, place : place + rows, :].astype(
                    ref.dtype
                )
                ref[0, :, span + h * head : span + (h + 1) * head] = dv_acc[
                    h, place : place + rows, :
                ].astype(ref.dtype)
            place += rows


def attend_backward(own, other, grad, log_total, head, after=()):
    clips, queries, wide = own.shape
    span = wide // 3
    others = other.shape[1]
    keys = queries + others
    block = query_block(queries)
    heads = span // head

    def body(*refs):
        attend_back_body(*refs[:5], *refs[5 + len(after) :], head=head)

    return call(
        body,
        (
            jax.ShapeDtypeStruct((clips, queries, span), BF16),
            jax.ShapeDtypeStruct((clips, queries, 2 * span), F32),
            jax.ShapeDtypeStruct((clips, others, 2 * span), BF16),
        ),
        grid=(clips, queries // block),
        in_specs=[
            pl.BlockSpec((1, block, wide), lambda m, i: (m, i, 0)),
            pl.BlockSpec((1, queries, wide), lambda m, i: (m, 0, 0)),
            pl.BlockSpec((1, others, wide), lambda m, i: (m, 0, 0)),
            pl.BlockSpec((1, block, span), lambda m, i: (m, i, 0)),
            pl.BlockSpec((1, heads, block), lambda m, i: (m, 0, i)),
        ]
        + [pl.BlockSpec(memory_space=pl.ANY)] * len(after),
        out_specs=(
            pl.BlockSpec((1, block, span), lambda m, i: (m, i, 0)),
            pl.BlockSpec((1, queries, 2 * span), lambda m, i: (m, 0, 0)),
            pl.BlockSpec((1, others, 2 * span), lambda m, i: (m, 0, 0)),
        ),
        scratch=[
            pltpu.VMEM((keys, block), F32),
            pltpu.VMEM((keys, block), F32),
            pltpu.VMEM((heads, keys, head), F32),
            pltpu.VMEM((heads, keys, head), F32),
        ],
        flops=40 * clips * queries * keys * span,
        moved=8 * (own.size + other.size),
    )(own, own, other, grad, log_total, *after)


def feed_body(
    x_ref,
    att_ref,
    w_out_ref,
    b_out_ref,
    gain_ref,
    shift_ref,
    w_up_ref,
    b_up_ref,
    w_down_ref,
    b_down_ref,
    y_ref,
    *rest,
):
    if len(rest) > 2:
        x1_ref, normed_ref, slope_ref, lifted_ref, flat_ref, acc = rest
    else:
        normed_ref, acc = rest
    span = att_ref.shape[2]

    @pl.when(pl.program_id(0) == 0)
    def _():
        middle = x_ref[...].astype(F32) + b_out_ref[...]
        for g in range(HEAD_GROUPS):
            middle = middle + dot(att_ref[g], w_out_ref[g * span : (g + 1) * span, :])
            if len(rest) > 2:
                flat_ref[:, g * span : (g + 1) * span] = att_ref[g]
        if len(rest) > 2:
            x1_ref[...] = middle
        scaled, _ = norm_parts(middle)
        normed_ref[...] = (scaled * gain_ref[...] + shift_ref[...]).astype(BF16)
        acc[...] = middle + b_down_ref[...]

    upper = dot(normed_ref[...], w_up_ref[...]) + b_up_ref[...]
    phi = 0.5 * (1.0 + lax.erf(upper * math.sqrt(0.5)))
    lifted = (upper * phi).astype(BF16)
    if len(rest) > 2:
        density = jnp.exp(-0.5 * upper * upper) * (1.0 / math.sqrt(2.0 * math.pi))
        slope_ref[...] = phi + upper * density
        lifted_ref[...] = lifted
    acc[...] += dot(lifted, w_down_ref[...])

    @pl.when(pl.program_id(0) == pl.num_programs(0) - 1)
    def _():
        y_ref[...] = acc[...].astype(BF16)


def whole(shape):
    return pl.BlockSpec(shape, lambda i: (0,) * len(shape))


def feed_forward(x, att, joined, b_out, gain, shift, b_up, w_down, b_down, keep):
    rows, width = x.shape
    hidden = w_down.shape[0]
    row = whole((1, width))
    full = whole((rows, width))
    part = pl.BlockSpec((rows, width), lambda i: (0, i))
    shapes = [jax.ShapeDtypeStruct((rows, width), BF16)]
    specs = [full]
    scratch = [pltpu.VMEM((rows, width), F32)]
    if keep:
        shapes += [
            jax.ShapeDtypeStruct((rows, width), F32),
            jax.ShapeDtypeStruct((rows, width), BF16),
            jax.ShapeDtypeStruct((rows, hidden), F32),
            jax.ShapeDtypeStruct((rows, hidden), BF16),
            jax.ShapeDtypeStruct((rows, width), BF16),
        ]
        specs += [full, full, part, part, full]
    else:
        scratch = [pltpu.VMEM((rows, width), BF16)] + scratch
    return call(
        feed_body,
        tuple(shapes),
        grid=(hidden // width,),
        in_specs=[
            full,
            whole(att.shape),
            pl.BlockSpec((width, width), lambda i: (0, 3)),
            row,
            row,
            row,
            pl.BlockSpec((width, width), lambda i: (0, 4 + i)),
            pl.BlockSpec((1, width), lambda i: (0, i)),
            pl.BlockSpec((width, width), lambda i: (i, 0)),
            row,
        ],
        out_specs=tuple(specs),
        scratch=scratch,
        flops=2 * rows * width * (2 * hidden + width),
        moved=4 * w_down.size + 2 * width * width + 10 * rows * hidden,
    )(x, att, joined, b_out, gain, shift, joined, b_up, w_down, b_down)


def feed_back_body(
    g_ref,
    slope_ref,
    w_down_ref,
    w_up_ref,
    w_out_ref,
    x1_ref,
    gain_ref,
    d_upper_ref,
    dx1_ref,
    branch_ref,
    datt_ref,
    sums_ref,
    up_sum_ref,
    acc,
):
    @pl.when(pl.program_id(0) == 0)
    def _():
        acc[...] = jnp.zeros_like(acc)

    d_upper = (dot_t(g_ref[...], w_down_ref[...]) * slope_ref[...]).astype(BF16)
    d_upper_ref[...] = d_upper
    up_sum_ref[...] = jnp.sum(d_upper.astype(F32), axis=0, keepdims=True)
    acc[...] += dot_t(d_upper, w_up_ref[...])

    @pl.when(pl.program_id(0) == pl.num_programs(0) - 1)
    def _():
        d_normed = acc[...]
        upstream = g_ref[...].astype(F32)
        scaled, inverse = norm_parts(x1_ref[...])
        d_middle = upstream + norm_back(d_normed, scaled, inverse, gain_ref[...])
        dx1_ref[...] = d_middle
        branch = d_middle.astype(BF16)
        branch_ref[...] = branch
        span = datt_ref.shape[2]
        for g in range(HEAD_GROUPS):
            datt_ref[g] = dot_t(branch, w_out_ref[g * span : (g + 1) * span, :]).astype(BF16)
        sums_ref[0:1, :] = jnp.sum(d_normed * scaled, axis=0, keepdims=True)
        sums_ref[1:2, :] = jnp.sum(d_normed, axis=0, keepdims=True)
        sums_ref[2:3, :] = jnp.sum(branch.astype(F32), axis=0, keepdims=True)
        sums_ref[3:4, :] = jnp.sum(upstream, axis=0, keepdims=True)


def feed_backward(g, slope, w_down, joined, x1, gain):
    rows, width = g.shape
    hidden = w_down.shape[0]
    chunk = width
    full = whole((rows, width))
    return call(
        feed_back_body,
        (
            jax.ShapeDtypeStruct((rows, hidden), BF16),
            jax.ShapeDtypeStruct((rows, width), F32),
            jax.ShapeDtypeStruct((rows, width), BF16),
            jax.ShapeDtypeStruct((HEAD_GROUPS, rows, width // HEAD_GROUPS), BF16),
            jax.ShapeDtypeStruct((4, width), F32),
            jax.ShapeDtypeStruct((1, hidden), F32),
        ),
        grid=(hidden // chunk,),
        in_specs=[
            full,
            pl.BlockSpec((rows, chunk), lambda i: (0, i)),
            pl.BlockSpec((chunk, width), lambda i: (i, 0)),
            pl.BlockSpec((width, chunk), lambda i: (0, 4 + i)),
            pl.BlockSpec((width, width), lambda i: (0, 3)),
            full,
            whole((1, width)),
        ],
        out_specs=(
            pl.BlockSpec((rows, chunk), lambda i: (0, i)),
            full,
            full,
            whole((HEAD_GROUPS, rows, width // HEAD_GROUPS)),
            whole((4, width)),
            pl.BlockSpec((1, chunk), lambda i: (0, i)),
        ),
        scratch=[pltpu.VMEM((rows, width), F32)],
        flops=2 * rows * width * (2 * hidden + width),
        moved=4 * w_down.size + 2 * width * width + 6 * rows * hidden,
    )(g, slope, w_down, joined, joined, x1, gain)


def qkv_back_body(grads_ref, w_ref, x_ref, dx1_ref, gain_ref, dx_ref, flat_ref, sums_ref):
    width = x_ref.shape[1]
    span = grads_ref.shape[2] // 3
    for g in range(HEAD_GROUPS):
        for part in range(3):
            flat_ref[:, part * width + g * span : part * width + (g + 1) * span] = grads_ref[
                g, :, part * span : (part + 1) * span
            ]
    d_normed = dot_t(flat_ref[...], w_ref[...])
    scaled, inverse = norm_parts(x_ref[...].astype(F32))
    dx = dx1_ref[...] + norm_back(d_normed, scaled, inverse, gain_ref[...])
    dx_ref[...] = dx.astype(BF16)
    sums_ref[0:1, :] = jnp.sum(d_normed * scaled, axis=0, keepdims=True)
    sums_ref[1:2, :] = jnp.sum(d_normed, axis=0, keepdims=True)
    sums_ref[2:3, :] = jnp.sum(flat_ref[:, :width].astype(F32), axis=0, keepdims=True)
    sums_ref[3:4, :] = jnp.sum(flat_ref[:, 2 * width :].astype(F32), axis=0, keepdims=True)


def qkv_backward(grads, joined, x, dx1, gain, after=()):
    rows, width = x.shape

    def body(*refs):
        qkv_back_body(*refs[:5], *refs[5 + len(after) :])

    return call(
        body,
        (
            jax.ShapeDtypeStruct((rows, width), BF16),
            jax.ShapeDtypeStruct((rows, 3 * width), BF16),
            jax.ShapeDtypeStruct((4, width), F32),
        ),
        grid=(1,),
        in_specs=[
            whole(grads.shape),
            whole((width, 3 * width)),
            whole((rows, width)),
            whole((rows, width)),
            whole((1, width)),
        ]
        + [pl.BlockSpec(memory_space=pl.ANY)] * len(after),
        out_specs=(whole((rows, width)), whole((rows, 3 * width)), whole((4, width))),
        flops=2 * rows * width * 3 * width,
        moved=6 * width * width + 20 * x.size,
    )(grads, joined, x, dx1, gain, *after)


def add_body(one_ref, two_ref, *rest):
    rest[-1][...] = (one_ref[...].astype(F32) + two_ref[...].astype(F32)).astype(BF16)


def add_after(one, two, after):
    rows, wide = one.shape
    block = next((n for n in ROW_BLOCKS if rows % n == 0), rows)
    spec = pl.BlockSpec((block, wide), lambda i: (i, 0))
    return call(
        add_body,
        jax.ShapeDtypeStruct((rows, wide), BF16),
        grid=(rows // block,),
        in_specs=[spec, spec] + [pl.BlockSpec(memory_space=pl.ANY)] * len(after),
        out_specs=spec,
        flops=one.size,
        moved=6 * one.size,
    )(one, two, *after)


def copy_body(one_ref, *rest):
    rest[-1][...] = one_ref[...]


def copy_after(one, after):
    spec = pl.BlockSpec(one.shape, lambda i: (0, 0))
    return call(
        copy_body,
        jax.ShapeDtypeStruct(one.shape, one.dtype),
        grid=(1,),
        in_specs=[spec] + [pl.BlockSpec(memory_space=pl.ANY)] * len(after),
        out_specs=spec,
        flops=one.size,
        moved=4 * one.size,
    )(one, *after)


def join_body(dq_ref, kept_ref, back_ref, *rest):
    out_ref = rest[-1]
    span = dq_ref.shape[2]
    out_ref[:, :, :span] = dq_ref[...]
    out_ref[:, :, span:] = (kept_ref[...] + back_ref[...].astype(F32)).astype(BF16)


def join_grads(dq, kept, back, after):
    clips, rows, span = dq.shape

    def spec(wide):
        return pl.BlockSpec((1, rows, wide), lambda i: (i, 0, 0))

    return call(
        join_body,
        jax.ShapeDtypeStruct((clips, rows, 3 * span), BF16),
        grid=(clips,),
        in_specs=[spec(span), spec(2 * span), spec(2 * span)]
        + [pl.BlockSpec(memory_space=pl.ANY)] * len(after),
        out_specs=spec(3 * span),
        flops=kept.size,
        moved=8 * kept.size,
    )(dq, kept, back, *after)


def swap(block, axis):
    return lax.ppermute(block, axis, [(0, 1), (1, 0)])


def shift(block, distance):
    count = lax.axis_size("rest")
    return lax.ppermute(block, "rest", [(i, (i + distance) % count) for i in range(count)])


def spread(block):
    return lax.all_to_all(block, ("quad", "side"), 0, 0, tiled=True)


def to_clips(block, clips):
    groups, rows, wide = block.shape
    if clips == 1:
        return block.reshape(1, groups * rows, wide)
    block = block.reshape(groups, clips, rows // clips, wide)
    return jnp.swapaxes(block, 0, 1).reshape(clips, groups * (rows // clips), wide)


def to_tokens(block):
    clips, rows, wide = block.shape
    if clips == 1:
        return block.reshape(HEAD_GROUPS, rows // HEAD_GROUPS, wide)
    block = block.reshape(clips, HEAD_GROUPS, rows // HEAD_GROUPS, wide)
    return jnp.swapaxes(block, 0, 1).reshape(HEAD_GROUPS, -1, wide)


def other_keys(grouped, own, clips):
    if lax.axis_size("rest") == 1:
        return to_clips(swap(grouped, "core"), clips)
    near = [shift(own, k) for k in range(1, lax.axis_size("rest"))]
    far = swap(jnp.concatenate([own] + near, axis=1), "core")
    return jnp.concatenate(near + [far], axis=1)


def return_keys(kept, sent):
    queries = kept.shape[1]
    count = lax.axis_size("rest")
    near = (count - 1) * queries
    back = swap(sent[:, near:], "core")
    total = kept
    for k in range(1, count):
        part = sent[:, (k - 1) * queries : k * queries].astype(F32)
        part = part + back[:, k * queries : (k + 1) * queries].astype(F32)
        total = total + shift(part.astype(BF16), -k).astype(F32)
    return total, back[:, :queries]


def pick(flag, one, two):
    return jnp.where(flag, one, two)


def gather_weight(*blocks):
    core = lax.axis_index("core")
    quads = lax.axis_size("quad")
    part = blocks[0].shape[0] // (2 * quads)
    quad = lax.axis_index("quad")

    def cut(which):
        start = (which * quads + quad) * part
        return jnp.concatenate(
            [lax.dynamic_slice_in_dim(block, start, part, 0) for block in blocks], axis=1
        )

    own = cut(core)
    came = swap(cut(1 - core), "core")
    first = pick(core == 0, own, came)
    second = pick(core == 0, came, own)
    return [
        lax.all_gather(item, ("side", "rest", "core", "quad"), axis=0, tiled=True)
        for item in (first, second)
    ]


def in_order(second, mine, other):
    return pick(second, other, mine), pick(second, mine, other)


def start_downs(block):
    if lax.axis_size("rest") > 1 or lax.axis_size("quad") != 2:
        first, second = gather_weight(block)
        return None, first, second
    core, quad = lax.axis_index("core"), lax.axis_index("quad")
    part = block.shape[0] // 4
    mine, other = in_order(core == 1, block, swap(block, "core"))
    line = lax.dynamic_slice_in_dim(other, (core * 2 + quad) * part, part, 0)
    second = lax.all_gather(line, ("side", "rest", "core", "quad"), axis=0, tiled=True)
    near = lax.dynamic_slice_in_dim(mine, core * 2 * part, 2 * part, 0)
    return swap(near, "side"), mine, second


def finish_down(near, mine):
    if near is None:
        return mine
    core, side = lax.axis_index("core"), lax.axis_index("side")
    other = jnp.concatenate(in_order(core == 1, near, swap(near, "core")), axis=0)
    return jnp.concatenate(in_order(side == 1, mine, other), axis=0)


def add(one, two):
    return (one.astype(F32) + two.astype(F32)).astype(one.dtype)


def cut_columns(left, which):
    shards = lax.axis_size("side") * lax.axis_size("rest")
    part = left.shape[1] // (2 * shards)
    return jnp.concatenate(
        [
            lax.dynamic_slice_in_dim(left, (2 * s + which) * part, part, 1)
            for s in range(shards)
        ],
        axis=1,
    )


def weight_halves(left, right):
    core = lax.axis_index("core")
    return [
        t_dot(cut_columns(left, which), right).astype(BF16) for which in (1 - core, core)
    ]


def parts_body(side_ref, *refs):
    far_one, far_two, near_one, near_two = refs[:4]
    sent_ref, kept_ref = refs[-2:]
    sent_ref[...] = (far_one[...].astype(F32) + far_two[...].astype(F32)).astype(BF16)
    kept_ref[...] = (near_one[...].astype(F32) + near_two[...].astype(F32)).astype(BF16)


def side_parts(sent, kept, *after):
    came = swap(sent, "core")
    rows, wide = kept.shape
    half = rows // 2
    block = next((n for n in ROW_BLOCKS if half % n == 0), half)
    steps = half // block
    far = pl.BlockSpec((block, wide), lambda i, side: ((1 - side[0]) * steps + i, 0))
    near = pl.BlockSpec((block, wide), lambda i, side: (side[0] * steps + i, 0))
    out = pl.BlockSpec((block, wide), lambda i, side: (i, 0))
    return pl.pallas_call(
        parts_body,
        out_shape=(jax.ShapeDtypeStruct((half, wide), BF16),) * 2,
        grid_spec=pltpu.PrefetchScalarGridSpec(
            num_scalar_prefetch=1,
            grid=(steps,),
            in_specs=[far, far, near, near]
            + [pl.BlockSpec(memory_space=pl.ANY)] * len(after),
            out_specs=(out, out),
        ),
        compiler_params=pltpu.CompilerParams(vmem_limit_bytes=VMEM_LIMIT),
        cost_estimate=pl.CostEstimate(
            flops=kept.size, bytes_accessed=6 * kept.size, transcendentals=0
        ),
    )(lax.axis_index("side").astype(jnp.int32).reshape(1), kept, came, kept, came, *after)


def side_sum(sent, kept, *after):
    total = add_after(kept, swap(sent, "side"), after)
    if lax.axis_size("rest") > 1:
        total = lax.psum_scatter(total, "rest", scatter_dimension=0, tiled=True)
    return total


def line_sum(*items):
    return lax.psum(items, ("half", "quad"))


def line_hop(block, pairs):
    return lax.ppermute(block, ("half", "quad"), pairs)


def line_sums(sides, ties):
    inward, across, outward = [(0, 1), (3, 2)], [(1, 2), (2, 1)], [(1, 0), (2, 3)]
    inner = lax.axis_index("half") != lax.axis_index("quad")
    count = len(sides)
    totals, mark = [None] * count, ()
    results = []
    for turn in range(count + 2):
        mark = (*mark, *ties.get(turn, ()))
        if turn < count:
            totals[turn] = sides[turn](*mark)
            mark = (totals[turn],)
        for hops, at in ((inward, turn - 1), (across, turn - 2)):
            if 0 <= at < count:
                totals[at] = add_after(totals[at], line_hop(totals[at], hops), mark)
                mark = (totals[at],)
                if hops is across:
                    results.append(pick(inner, totals[at], line_hop(totals[at], outward)))
    return results


def join_cores(first, second):
    core = lax.axis_index("core")
    came = swap(pick(core == 0, second, first), "core")
    mine = pick(core == 0, first, second)
    return jnp.concatenate([pick(core == 0, mine, came), pick(core == 0, came, mine)], axis=0)


def swap_in(block):
    core, half = lax.axis_index("core"), lax.axis_index("half")
    micro, rows, wide = block.shape
    block = block.reshape(2, (micro // 2) * rows, wide)
    own = lax.dynamic_index_in_dim(block, half, 0, keepdims=False)
    other = lax.dynamic_index_in_dim(block, 1 - half, 0, keepdims=False)
    came = lax.ppermute(other, ("core", "half"), [(1, 2), (2, 1)])
    return pick(core == half, own, came)


def start_out(first, second):
    second_core, second_half = lax.axis_index("core") == 1, lax.axis_index("half") == 1
    mine, sent = in_order(second_core, first, second)
    parts = in_order(second_core, mine, swap(sent, "core"))
    mine, sent = in_order(second_half, *parts)
    return mine, swap(sent, "half")


def finish_out(mine, came, micro):
    rows, wide = mine.shape
    clips = in_order(lax.axis_index("half") == 1, mine, came)
    return jnp.stack(clips).reshape(micro, 2 * rows // micro, wide)


def forward_layer(x, weights, clips, head, keep):
    joined, w_down, gains, shifts, b_qkv, b_out, b_down, b_up = weights
    grouped, normed_one = qkv_forward(x, gains[0:1], shifts[0:1], joined, b_qkv)
    grouped = spread(grouped)
    own = to_clips(grouped, clips)
    other = other_keys(grouped, own, clips)
    att, log_total = attend_forward(own, other, head)
    if callable(w_down):
        w_down = w_down()
        weights = (joined, w_down, *weights[2:])
    att = spread(to_tokens(att))
    y, *kept = feed_forward(
        x, att, joined, b_out, gains[1:2], shifts[1:2], b_up, w_down, b_down, keep
    )
    return y, (x, normed_one, own, other, log_total, *kept), weights


def attention_grads(kept, d_att, clips, head, after):
    return heads_back(kept, to_clips(spread(d_att), clips), head, after)


def heads_back(kept, d_heads, head, after):
    own, other, log_total = kept[2:5]
    dq, kept_kv, sent_kv = attend_backward(own, other, d_heads, log_total, head, after)
    return (dq, *return_keys(kept_kv, sent_kv))


def spread_grads(grads, after=()):
    return spread(to_tokens(join_grads(*grads, after)))


def backward_lean(kept, g, weights, clips, head, *after):
    x, _, _, _, _, x1, _, slope, _, _ = kept
    joined, w_down, gains = weights[:3]
    _, dx1, _, d_att, _, _ = feed_backward(g, slope, w_down, joined, x1, gains[1:2])
    d_tokens = spread_grads(attention_grads(kept, d_att, clips, head, after))
    return qkv_backward(d_tokens, joined, x, dx1, gains[0:1])[0]


def small_rows(sums_one, sums_two, up_sum, shards, wide):
    rows = jnp.concatenate(
        [
            sums_one[0:1],
            sums_two[0:1],
            sums_one[1:2],
            sums_two[1:2],
            sums_one[2:4],
            sums_two[2:4],
        ]
    )
    rows = jnp.swapaxes(rows.reshape(8, shards, -1), 0, 1).reshape(shards, -1)
    packed = jnp.concatenate([rows, up_sum.reshape(shards, -1)], axis=1).astype(BF16)
    packed = packed.reshape(shards, 2, -1)
    lines = -(-packed.shape[2] // wide)
    room = 16 * (-(-lines // 16)) * wide
    packed = jnp.pad(packed, ((0, 0), (0, 0), (0, room - packed.shape[2])))
    return packed.reshape(shards, 2, -1, wide)


def beside(weight, *rows):
    shards, _, wide = rows[0].shape
    return jnp.concatenate([weight.reshape(shards, -1, wide), *rows], axis=1).reshape(-1, wide)


def rest_halves(normed_one, flat, out, sums_one, sums_two, up_sum, shards):
    core = lax.axis_index("core")
    wide = flat.shape[1]
    rows = small_rows(sums_one, sums_two, up_sum, shards, wide)
    return [
        beside(
            item,
            lax.dynamic_index_in_dim(rows, which, 1, keepdims=False),
            outs.reshape(shards, -1, wide),
        )
        for item, outs, which in zip(weight_halves(normed_one, flat), out, (1 - core, core))
    ]


def backward_all(kept_first, kept_second, g, layers, clips, head, shards):
    x, normed_one, _, _, _, x1, normed_two, slope, lifted, att = kept_second
    joined, w_down, gains = layers[1][:3]
    d_upper, dx1, branch, d_att, sums_two, up_sum = feed_backward(
        g, slope, w_down, joined, x1, gains[1:2]
    )
    down = weight_halves(lifted, g)
    up = weight_halves(normed_two, d_upper)
    grads = attention_grads(kept_second, d_att, clips, head, (*down, *up))
    d_tokens = spread_grads(grads)
    out = weight_halves(att, branch)
    down = side_parts(*down, d_tokens)
    d_second, flat, sums_one = qkv_backward(
        d_tokens, joined, x, dx1, gains[0:1], (*down, *out)
    )
    rest = rest_halves(normed_one, flat, out, sums_one, sums_two, up_sum, shards)

    x, normed_one, _, _, _, x1, normed_two, slope, lifted, att = kept_first
    joined, w_down, gains = layers[0][:3]
    d_upper, dx1, branch, d_att, sums_two, up_sum = feed_backward(
        d_second, slope, w_down, joined, x1, gains[1:2]
    )
    down_one = weight_halves(lifted, d_second)
    up_one = weight_halves(normed_two, d_upper)
    d_heads = to_clips(spread(d_att), clips)
    up = side_parts(*up, d_heads)
    down_two = side_sum(*down)
    grads = heads_back(
        kept_first, d_heads, head, (down_two, *up, *rest, *down_one, *up_one)
    )
    rest = side_parts(*rest, grads[0])
    up_two = side_sum(*up, grads[0])
    d_tokens = spread_grads(grads, (up_two, *rest))
    down_one, up_one = side_parts(*down_one), side_parts(*up_one)
    out_one = weight_halves(att, branch)
    d_first, flat, sums_one = qkv_backward(
        d_tokens, joined, x, dx1, gains[0:1], (*down_one, *up_one, *out_one)
    )
    placed = start_out(d_first, d_second)
    halves = rest_halves(normed_one, flat, out_one, sums_one, sums_two, up_sum, shards)
    rest_one = side_parts(*halves)
    blocks = (
        (rest, halves[0]),
        (down_one, rest_one[0]),
        (up_one, rest_one[0]),
        (rest_one, placed[1]),
    )
    sides = [
        lambda *after, item=item, mark=mark: side_sum(*item, *after, mark)
        for item, mark in blocks
    ]
    up_two, down_two = line_sum(up_two, down_two)
    if lax.axis_size("quad") == 2:
        sums = line_sums(sides, {1: (up_two, down_two)})
    else:
        sums = line_sum(*(item() for item in sides))
    rest_two, down_one, up_one, rest_one = sums
    firsts = (rest_one, up_one, down_one)
    seconds = (rest_two, up_two, down_two)
    return placed, [join_cores(a, b) for a, b in zip(firsts, seconds)]


def gather_small(block):
    core, side = lax.axis_index("core"), lax.axis_index("side")
    if lax.axis_size("rest") > 1:
        whole_block = lax.all_gather(block, ("core", "side", "rest"), axis=0, tiled=False)
        return whole_block.reshape(2, -1, block.shape[0])
    came = swap(block, "side")
    layer = jnp.stack([pick(side == 0, block, came), pick(side == 0, came, block)])
    came = swap(layer, "core")
    return jnp.stack([pick(core == 0, layer, came), pick(core == 0, came, layer)])


def per_device(
    frames, out_grad, norm_gain, norm_bias, w_qkv, w_out, w_up, w_down, proj_bias, up_bias
):
    pairs = lax.axis_size("pair")
    pair = lax.axis_index("pair")
    shards = lax.axis_size("side") * lax.axis_size("rest")
    micro, _, width = frames.shape
    clips = micro // 2
    head = width // HEADS
    part = width // shards

    joined = gather_weight(w_qkv[0], w_out[0], w_up[0])
    near, mine, second_down = start_downs(w_down[0])
    downs = [lambda: finish_down(near, mine), lambda: second_down]
    small = jnp.concatenate(
        [norm_gain.reshape(-1), norm_bias.reshape(-1), proj_bias.reshape(-1), up_bias.reshape(-1)]
    )
    small = gather_small(small).astype(F32)
    rows = jnp.swapaxes(small[:, :, : 8 * part].reshape(2, shards, 8, part), 1, 2)
    rows = rows.reshape(2, 8, width)
    ups = small[:, :, 8 * part :].reshape(2, 1, -1)
    x_start = swap_in(frames)
    layers = []
    for layer in range(2):
        r = rows[layer]
        b_qkv = jnp.concatenate([r[4:5], jnp.zeros_like(r[4:5]), r[5:6]], axis=1)
        layers.append(
            (joined[layer], downs[layer], r[0:2], r[2:4], b_qkv, r[6:7], r[7:8], ups[layer])
        )

    x = x_start if near is None else copy_after(x_start, (near,))
    for phase in range(pairs):
        if phase > 0:
            came = lax.ppermute(second, "pair", [(i, i + 1) for i in range(pairs - 1)])
            x = pick(pair == 0, x_start, came)
        keep = phase == pairs - 1
        first, kept_first, layers[0] = forward_layer(x, layers[0], clips, head, keep)
        second, kept_second, layers[1] = forward_layer(first, layers[1], clips, head, keep)
    hidden = finish_out(*start_out(first, second), micro)

    g_start = swap_in(out_grad)
    g = g_start
    for phase in range(pairs - 1):
        d_second = backward_lean(kept_second, g, layers[1], clips, head, hidden)
        d_first = backward_lean(kept_first, d_second, layers[0], clips, head)
        came = lax.ppermute(d_first, "pair", [(i + 1, i) for i in range(pairs - 1)])
        g = pick(pair == pairs - 1, g_start, came)
    placed, (rest, up, down) = backward_all(
        kept_first, kept_second, g, layers, clips, head, shards
    )
    input_grads = finish_out(*placed, micro)

    own_rows = part // 2
    rest = rest.reshape(2, -1, 3 * width)
    out_rows = own_rows // 3
    qkv = rest[:, :own_rows].reshape(-1, 3 * width)
    out = rest[:, rest.shape[1] - out_rows :].reshape(-1, width)
    packed = rest[:, own_rows : rest.shape[1] - out_rows].astype(F32)
    packed = packed.reshape(2, -1)[:, : (8 * part + up_bias.shape[1]) // 2].reshape(-1)
    heads = packed[: 8 * part].reshape(8, part)
    return (
        hidden[None],
        input_grads[None],
        heads[0:2][None],
        heads[2:4][None],
        qkv.astype(F32)[None],
        out.astype(F32)[None],
        up.astype(F32)[None],
        down.astype(F32)[None],
        heads[4:8][None],
        packed[8 * part :][None],
    )


def solution(mesh):
    sections, groups, shards = (mesh.shape[name] for name in ("section", "seq", "shard"))
    cut = Mesh(
        mesh.devices.reshape(sections // 2, 2, 2, groups // 2, 2, shards // 2),
        AXES,
    )
    section, seq, shard = ("pair", "core"), ("half", "quad"), ("side", "rest")
    rows = seq + shard
    return jax.shard_map(
        per_device,
        mesh=cut,
        in_specs=(
            P(None, rows, None),
            P(None, rows, None),
            P(section, None, shard),
            P(section, None, shard),
            P(section, shard, None),
            P(section, shard, None),
            P(section, shard, None),
            P(section, shard, None),
            P(section, None, shard),
            P(section, shard),
        ),
        out_specs=(
            P(section, None, rows, None),
            P(section, None, rows, None),
            P(section, None, shard),
            P(section, None, shard),
            P(section, shard, None),
            P(section, shard, None),
            P(section, shard, None),
            P(section, shard, None),
            P(section, None, shard),
            P(section, shard),
        ),
        check_vma=False,
    )
```

```python
import math

import jax
import jax.numpy as jnp
from jax import lax
from jax.experimental import pallas as pl
from jax.experimental.pallas import tpu as pltpu
from jax.sharding import Mesh
from jax.sharding import PartitionSpec as P

HEADS = 12
norm_eps = 1e-05
F32 = jnp.float32
BF16 = jnp.bfloat16
VMEM_LIMIT = 56 * 1024 * 1024
AXES = ("pair", "core", "half", "quad", "side", "rest")
HEAD_GROUPS = 4
INWARD, ACROSS, OUTWARD = [(0, 1), (3, 2)], [(1, 2), (2, 1)], [(1, 0), (2, 3)]
ROW_BLOCKS = (272, 256, 192, 128, 96, 80, 64, 48)


def call(body, out_shapes, grid=None, in_specs=None, out_specs=None, scratch=(), flops=0, moved=0):
    extra = {} if grid is None else dict(grid=grid, in_specs=in_specs, out_specs=out_specs)
    return pl.pallas_call(
        body,
        out_shape=out_shapes,
        scratch_shapes=scratch,
        compiler_params=pltpu.CompilerParams(vmem_limit_bytes=VMEM_LIMIT),
        cost_estimate=pl.CostEstimate(flops=flops, bytes_accessed=moved, transcendentals=0),
        **extra,
    )


def dot(left, right):
    return jnp.dot(left, right, preferred_element_type=F32)


def dot_t(left, right):
    return lax.dot_general(left, right, (((1,), (1,)), ((), ())), preferred_element_type=F32)


def t_dot(left, right):
    return lax.dot_general(left, right, (((0,), (0,)), ((), ())), preferred_element_type=F32)


def norm_parts(values):
    center = values - jnp.mean(values, axis=-1, keepdims=True)
    inverse = lax.rsqrt(jnp.mean(center * center, axis=-1, keepdims=True) + norm_eps)
    return center * inverse, inverse


def norm_back(upstream, scaled, inverse, gain_row):
    weighted = upstream * gain_row
    return inverse * (
        weighted
        - jnp.mean(weighted, axis=-1, keepdims=True)
        - scaled * jnp.mean(weighted * scaled, axis=-1, keepdims=True)
    )


def qkv_body(x_ref, gain_ref, shift_ref, w_ref, bias_ref, out_ref, normed_ref):
    scaled, _ = norm_parts(x_ref[...].astype(F32))
    normed = (scaled * gain_ref[...] + shift_ref[...]).astype(BF16)
    normed_ref[...] = normed
    span = out_ref.shape[2] // 3
    width = x_ref.shape[1]
    for part in range(3):
        cols = slice(part * width, (part + 1) * width)
        piece = (dot(normed, w_ref[:, cols]) + bias_ref[:, cols]).astype(BF16)
        for g in range(HEAD_GROUPS):
            out_ref[g, :, part * span : (part + 1) * span] = piece[:, g * span : (g + 1) * span]


def qkv_forward(x, gain, shift, joined, bias):
    rows, width = x.shape
    span = width // HEAD_GROUPS
    return call(
        qkv_body,
        (
            jax.ShapeDtypeStruct((HEAD_GROUPS, rows, 3 * span), BF16),
            jax.ShapeDtypeStruct((rows, width), BF16),
        ),
        grid=(1,),
        in_specs=[
            whole((rows, width)),
            whole((1, width)),
            whole((1, width)),
            whole((width, 3 * width)),
            whole((1, 3 * width)),
        ],
        out_specs=(whole((HEAD_GROUPS, rows, 3 * span)), whole((rows, width))),
        flops=2 * rows * width * 3 * width,
        moved=6 * width * width + 10 * x.size,
    )(x, gain, shift, joined, bias)


def key_chunks(own_ref, other_ref):
    place = 0
    for ref in (own_ref, other_ref):
        total = ref.shape[1]
        step = 256 if total % 256 == 0 else total
        for start in range(0, total, step):
            yield ref, start, place, step
            place += step


def attend_body(q_ref, own_ref, other_ref, out_ref, log_ref, score_ref, *, head):
    span = q_ref.shape[2] // 3
    queries = q_ref.shape[1]
    scale = 1.0 / math.sqrt(head)
    for h in range(span // head):
        q = q_ref[0, :, h * head : (h + 1) * head] * scale
        top = jnp.full((1, queries), -jnp.inf, F32)
        for ref, start, place, step in key_chunks(own_ref, other_ref):
            k = ref[0, start : start + step, span + h * head : span + (h + 1) * head]
            scores = dot_t(k, q)
            score_ref[place : place + step, :] = scores
            top = jnp.maximum(top, jnp.max(scores, axis=0, keepdims=True))
        total = jnp.zeros((1, queries), F32)
        acc = jnp.zeros((head, queries), F32)
        for ref, start, place, step in key_chunks(own_ref, other_ref):
            v = ref[0, start : start + step, 2 * span + h * head : 2 * span + (h + 1) * head]
            e = jnp.exp(score_ref[place : place + step, :] - top)
            total = total + jnp.sum(e, axis=0, keepdims=True)
            acc = acc + t_dot(v, e.astype(BF16))
        out_ref[0, :, h * head : (h + 1) * head] = jnp.transpose(acc / total).astype(BF16)
        log_ref[0, h : h + 1, :] = top + jnp.log(total)


def query_block(queries):
    return 256 if queries % 256 == 0 else queries


def attend_forward(own, other, head):
    clips, queries, wide = own.shape
    span = wide // 3
    keys = queries + other.shape[1]
    block = query_block(queries)

    def body(*refs):
        attend_body(*refs, head=head)

    return call(
        body,
        (
            jax.ShapeDtypeStruct((clips, queries, span), BF16),
            jax.ShapeDtypeStruct((clips, span // head, queries), F32),
        ),
        grid=(clips, queries // block),
        in_specs=[
            pl.BlockSpec((1, block, wide), lambda m, i: (m, i, 0)),
            pl.BlockSpec((1, queries, wide), lambda m, i: (m, 0, 0)),
            pl.BlockSpec((1, other.shape[1], wide), lambda m, i: (m, 0, 0)),
        ],
        out_specs=(
            pl.BlockSpec((1, block, span), lambda m, i: (m, i, 0)),
            pl.BlockSpec((1, span // head, block), lambda m, i: (m, 0, i)),
        ),
        scratch=[pltpu.VMEM((keys, block), F32)],
        flops=16 * clips * queries * keys * span,
        moved=4 * (own.size + other.size),
    )(own, own, other)


def attend_back_body(
    q_ref,
    own_ref,
    other_ref,
    grad_ref,
    log_ref,
    dq_ref,
    dkv_own_ref,
    dkv_other_ref,
    p_ref,
    dp_ref,
    dk_acc,
    dv_acc,
    *,
    head,
):
    span = q_ref.shape[2] // 3
    queries = q_ref.shape[1]
    heads = span // head
    scale = 1.0 / math.sqrt(head)

    @pl.when(pl.program_id(1) == 0)
    def _():
        dk_acc[...] = jnp.zeros_like(dk_acc)
        dv_acc[...] = jnp.zeros_like(dv_acc)

    for h in range(heads):
        q = q_ref[0, :, h * head : (h + 1) * head] * scale
        d_out = grad_ref[0, :, h * head : (h + 1) * head]
        log_total = log_ref[0, h : h + 1, :]
        row_term = jnp.zeros((1, queries), F32)
        for ref, start, place, step in key_chunks(own_ref, other_ref):
            k = ref[0, start : start + step, span + h * head : span + (h + 1) * head]
            v = ref[0, start : start + step, 2 * span + h * head : 2 * span + (h + 1) * head]
            probs = jnp.exp(dot_t(k, q) - log_total)
            d_probs = dot_t(v, d_out)
            p_ref[place : place + step, :] = probs
            dp_ref[place : place + step, :] = d_probs
            row_term = row_term + jnp.sum(probs * d_probs, axis=0, keepdims=True)
            dv_acc[h, place : place + step, :] += dot(probs.astype(BF16), d_out)
        dq = jnp.zeros((head, queries), F32)
        for ref, start, place, step in key_chunks(own_ref, other_ref):
            k = ref[0, start : start + step, span + h * head : span + (h + 1) * head]
            d_scores = (
                p_ref[place : place + step, :] * (dp_ref[place : place + step, :] - row_term)
            ).astype(BF16)
            dk_acc[h, place : place + step, :] += dot(d_scores, q)
            dq = dq + t_dot(k, d_scores)
        dq_ref[0, :, h * head : (h + 1) * head] = jnp.transpose(dq * scale).astype(BF16)

    @pl.when(pl.program_id(1) == pl.num_programs(1) - 1)
    def _():
        place = 0
        for ref in (dkv_own_ref, dkv_other_ref):
            rows = ref.shape[1]
            for h in range(heads):
                ref[0, :, h * head : (h + 1) * head] = dk_acc[h, place : place + rows, :].astype(
                    ref.dtype
                )
                ref[0, :, span + h * head : span + (h + 1) * head] = dv_acc[
                    h, place : place + rows, :
                ].astype(ref.dtype)
            place += rows


def attend_backward(own, other, grad, log_total, head, after=()):
    clips, queries, wide = own.shape
    span = wide // 3
    others = other.shape[1]
    keys = queries + others
    block = query_block(queries)
    heads = span // head

    def body(*refs):
        attend_back_body(*refs[:5], *refs[5 + len(after) :], head=head)

    return call(
        body,
        (
            jax.ShapeDtypeStruct((clips, queries, span), BF16),
            jax.ShapeDtypeStruct((clips, queries, 2 * span), F32),
            jax.ShapeDtypeStruct((clips, others, 2 * span), BF16),
        ),
        grid=(clips, queries // block),
        in_specs=[
            pl.BlockSpec((1, block, wide), lambda m, i: (m, i, 0)),
            pl.BlockSpec((1, queries, wide), lambda m, i: (m, 0, 0)),
            pl.BlockSpec((1, others, wide), lambda m, i: (m, 0, 0)),
            pl.BlockSpec((1, block, span), lambda m, i: (m, i, 0)),
            pl.BlockSpec((1, heads, block), lambda m, i: (m, 0, i)),
        ]
        + [pl.BlockSpec(memory_space=pl.ANY)] * len(after),
        out_specs=(
            pl.BlockSpec((1, block, span), lambda m, i: (m, i, 0)),
            pl.BlockSpec((1, queries, 2 * span), lambda m, i: (m, 0, 0)),
            pl.BlockSpec((1, others, 2 * span), lambda m, i: (m, 0, 0)),
        ),
        scratch=[
            pltpu.VMEM((keys, block), F32),
            pltpu.VMEM((keys, block), F32),
            pltpu.VMEM((heads, keys, head), F32),
            pltpu.VMEM((heads, keys, head), F32),
        ],
        flops=40 * clips * queries * keys * span,
        moved=8 * (own.size + other.size),
    )(own, own, other, grad, log_total, *after)


def feed_body(
    x_ref,
    att_ref,
    w_out_ref,
    b_out_ref,
    gain_ref,
    shift_ref,
    w_up_ref,
    b_up_ref,
    w_down_ref,
    b_down_ref,
    y_ref,
    *rest,
):
    if len(rest) > 2:
        x1_ref, normed_ref, slope_ref, lifted_ref, flat_ref, acc = rest
    else:
        normed_ref, acc = rest
    span = att_ref.shape[2]

    @pl.when(pl.program_id(0) == 0)
    def _():
        middle = x_ref[...].astype(F32) + b_out_ref[...]
        for g in range(HEAD_GROUPS):
            middle = middle + dot(att_ref[g], w_out_ref[g * span : (g + 1) * span, :])
            if len(rest) > 2:
                flat_ref[:, g * span : (g + 1) * span] = att_ref[g]
        if len(rest) > 2:
            x1_ref[...] = middle
        scaled, _ = norm_parts(middle)
        normed_ref[...] = (scaled * gain_ref[...] + shift_ref[...]).astype(BF16)
        acc[...] = middle + b_down_ref[...]

    upper = dot(normed_ref[...], w_up_ref[...]) + b_up_ref[...]
    phi = 0.5 * (1.0 + lax.erf(upper * math.sqrt(0.5)))
    lifted = (upper * phi).astype(BF16)
    if len(rest) > 2:
        density = jnp.exp(-0.5 * upper * upper) * (1.0 / math.sqrt(2.0 * math.pi))
        slope_ref[...] = phi + upper * density
        lifted_ref[...] = lifted
    acc[...] += dot(lifted, w_down_ref[...])

    @pl.when(pl.program_id(0) == pl.num_programs(0) - 1)
    def _():
        y_ref[...] = acc[...].astype(BF16)


def whole(shape):
    return pl.BlockSpec(shape, lambda i: (0,) * len(shape))


def feed_forward(x, att, joined, b_out, gain, shift, b_up, w_down, b_down, keep):
    rows, width = x.shape
    hidden = w_down.shape[0]
    row = whole((1, width))
    full = whole((rows, width))
    part = pl.BlockSpec((rows, width), lambda i: (0, i))
    shapes = [jax.ShapeDtypeStruct((rows, width), BF16)]
    specs = [full]
    scratch = [pltpu.VMEM((rows, width), F32)]
    if keep:
        shapes += [
            jax.ShapeDtypeStruct((rows, width), F32),
            jax.ShapeDtypeStruct((rows, width), BF16),
            jax.ShapeDtypeStruct((rows, hidden), F32),
            jax.ShapeDtypeStruct((rows, hidden), BF16),
            jax.ShapeDtypeStruct((rows, width), BF16),
        ]
        specs += [full, full, part, part, full]
    else:
        scratch = [pltpu.VMEM((rows, width), BF16)] + scratch
    return call(
        feed_body,
        tuple(shapes),
        grid=(hidden // width,),
        in_specs=[
            full,
            whole(att.shape),
            pl.BlockSpec((width, width), lambda i: (0, 3)),
            row,
            row,
            row,
            pl.BlockSpec((width, width), lambda i: (0, 4 + i)),
            pl.BlockSpec((1, width), lambda i: (0, i)),
            pl.BlockSpec((width, width), lambda i: (i, 0)),
            row,
        ],
        out_specs=tuple(specs),
        scratch=scratch,
        flops=2 * rows * width * (2 * hidden + width),
        moved=4 * w_down.size + 2 * width * width + 10 * rows * hidden,
    )(x, att, joined, b_out, gain, shift, joined, b_up, w_down, b_down)


def feed_back_body(
    g_ref,
    slope_ref,
    w_down_ref,
    w_up_ref,
    w_out_ref,
    x1_ref,
    gain_ref,
    d_upper_ref,
    dx1_ref,
    branch_ref,
    datt_ref,
    sums_ref,
    up_sum_ref,
    acc,
):
    @pl.when(pl.program_id(0) == 0)
    def _():
        acc[...] = jnp.zeros_like(acc)

    d_upper = (dot_t(g_ref[...], w_down_ref[...]) * slope_ref[...]).astype(BF16)
    d_upper_ref[...] = d_upper
    up_sum_ref[...] = jnp.sum(d_upper.astype(F32), axis=0, keepdims=True)
    acc[...] += dot_t(d_upper, w_up_ref[...])

    @pl.when(pl.program_id(0) == pl.num_programs(0) - 1)
    def _():
        d_normed = acc[...]
        upstream = g_ref[...].astype(F32)
        scaled, inverse = norm_parts(x1_ref[...])
        d_middle = upstream + norm_back(d_normed, scaled, inverse, gain_ref[...])
        dx1_ref[...] = d_middle
        branch = d_middle.astype(BF16)
        branch_ref[...] = branch
        span = datt_ref.shape[2]
        for g in range(HEAD_GROUPS):
            datt_ref[g] = dot_t(branch, w_out_ref[g * span : (g + 1) * span, :]).astype(BF16)
        sums_ref[0:1, :] = jnp.sum(d_normed * scaled, axis=0, keepdims=True)
        sums_ref[1:2, :] = jnp.sum(d_normed, axis=0, keepdims=True)
        sums_ref[2:3, :] = jnp.sum(branch.astype(F32), axis=0, keepdims=True)
        sums_ref[3:4, :] = jnp.sum(upstream, axis=0, keepdims=True)


def feed_backward(g, slope, w_down, joined, x1, gain):
    rows, width = g.shape
    hidden = w_down.shape[0]
    chunk = width
    full = whole((rows, width))
    return call(
        feed_back_body,
        (
            jax.ShapeDtypeStruct((rows, hidden), BF16),
            jax.ShapeDtypeStruct((rows, width), F32),
            jax.ShapeDtypeStruct((rows, width), BF16),
            jax.ShapeDtypeStruct((HEAD_GROUPS, rows, width // HEAD_GROUPS), BF16),
            jax.ShapeDtypeStruct((4, width), F32),
            jax.ShapeDtypeStruct((1, hidden), F32),
        ),
        grid=(hidden // chunk,),
        in_specs=[
            full,
            pl.BlockSpec((rows, chunk), lambda i: (0, i)),
            pl.BlockSpec((chunk, width), lambda i: (i, 0)),
            pl.BlockSpec((width, chunk), lambda i: (0, 4 + i)),
            pl.BlockSpec((width, width), lambda i: (0, 3)),
            full,
            whole((1, width)),
        ],
        out_specs=(
            pl.BlockSpec((rows, chunk), lambda i: (0, i)),
            full,
            full,
            whole((HEAD_GROUPS, rows, width // HEAD_GROUPS)),
            whole((4, width)),
            pl.BlockSpec((1, chunk), lambda i: (0, i)),
        ),
        scratch=[pltpu.VMEM((rows, width), F32)],
        flops=2 * rows * width * (2 * hidden + width),
        moved=4 * w_down.size + 2 * width * width + 6 * rows * hidden,
    )(g, slope, w_down, joined, joined, x1, gain)


def qkv_back_body(grads_ref, w_ref, x_ref, dx1_ref, gain_ref, dx_ref, flat_ref, sums_ref):
    width = x_ref.shape[1]
    span = grads_ref.shape[2] // 3
    for g in range(HEAD_GROUPS):
        for part in range(3):
            flat_ref[:, part * width + g * span : part * width + (g + 1) * span] = grads_ref[
                g, :, part * span : (part + 1) * span
            ]
    d_normed = dot_t(flat_ref[...], w_ref[...])
    scaled, inverse = norm_parts(x_ref[...].astype(F32))
    dx = dx1_ref[...] + norm_back(d_normed, scaled, inverse, gain_ref[...])
    dx_ref[...] = dx.astype(BF16)
    sums_ref[0:1, :] = jnp.sum(d_normed * scaled, axis=0, keepdims=True)
    sums_ref[1:2, :] = jnp.sum(d_normed, axis=0, keepdims=True)
    sums_ref[2:3, :] = jnp.sum(flat_ref[:, :width].astype(F32), axis=0, keepdims=True)
    sums_ref[3:4, :] = jnp.sum(flat_ref[:, 2 * width :].astype(F32), axis=0, keepdims=True)


def qkv_backward(grads, joined, x, dx1, gain, after=()):
    rows, width = x.shape

    def body(*refs):
        qkv_back_body(*refs[:5], *refs[5 + len(after) :])

    return call(
        body,
        (
            jax.ShapeDtypeStruct((rows, width), BF16),
            jax.ShapeDtypeStruct((rows, 3 * width), BF16),
            jax.ShapeDtypeStruct((4, width), F32),
        ),
        grid=(1,),
        in_specs=[
            whole(grads.shape),
            whole((width, 3 * width)),
            whole((rows, width)),
            whole((rows, width)),
            whole((1, width)),
        ]
        + [pl.BlockSpec(memory_space=pl.ANY)] * len(after),
        out_specs=(whole((rows, width)), whole((rows, 3 * width)), whole((4, width))),
        flops=2 * rows * width * 3 * width,
        moved=6 * width * width + 20 * x.size,
    )(grads, joined, x, dx1, gain, *after)


def add_body(one_ref, two_ref, *rest):
    rest[-1][...] = (one_ref[...].astype(F32) + two_ref[...].astype(F32)).astype(BF16)


def add_after(one, two, after):
    rows, wide = one.shape
    block = next((n for n in ROW_BLOCKS if rows % n == 0), rows)
    spec = pl.BlockSpec((block, wide), lambda i: (i, 0))
    return call(
        add_body,
        jax.ShapeDtypeStruct((rows, wide), BF16),
        grid=(rows // block,),
        in_specs=[spec, spec] + [pl.BlockSpec(memory_space=pl.ANY)] * len(after),
        out_specs=spec,
        flops=one.size,
        moved=6 * one.size,
    )(one, two, *after)


def copy_body(one_ref, *rest):
    rest[-1][...] = one_ref[...]


def copy_after(one, after):
    spec = pl.BlockSpec(one.shape, lambda i: (0, 0))
    return call(
        copy_body,
        jax.ShapeDtypeStruct(one.shape, one.dtype),
        grid=(1,),
        in_specs=[spec] + [pl.BlockSpec(memory_space=pl.ANY)] * len(after),
        out_specs=spec,
        flops=one.size,
        moved=4 * one.size,
    )(one, *after)


def join_body(dq_ref, kept_ref, back_ref, *rest):
    out_ref = rest[-1]
    span = dq_ref.shape[2]
    out_ref[:, :, :span] = dq_ref[...]
    out_ref[:, :, span:] = (kept_ref[...] + back_ref[...].astype(F32)).astype(BF16)


def join_grads(dq, kept, back, after):
    clips, rows, span = dq.shape

    def spec(wide):
        return pl.BlockSpec((1, rows, wide), lambda i: (i, 0, 0))

    return call(
        join_body,
        jax.ShapeDtypeStruct((clips, rows, 3 * span), BF16),
        grid=(clips,),
        in_specs=[spec(span), spec(2 * span), spec(2 * span)]
        + [pl.BlockSpec(memory_space=pl.ANY)] * len(after),
        out_specs=spec(3 * span),
        flops=kept.size,
        moved=8 * kept.size,
    )(dq, kept, back, *after)


def swap(block, axis):
    return lax.ppermute(block, axis, [(0, 1), (1, 0)])


def shift(block, distance):
    count = lax.axis_size("rest")
    return lax.ppermute(block, "rest", [(i, (i + distance) % count) for i in range(count)])


def spread(block):
    return lax.all_to_all(block, ("quad", "side"), 0, 0, tiled=True)


def to_clips(block, clips):
    groups, rows, wide = block.shape
    if clips == 1:
        return block.reshape(1, groups * rows, wide)
    block = block.reshape(groups, clips, rows // clips, wide)
    return jnp.swapaxes(block, 0, 1).reshape(clips, groups * (rows // clips), wide)


def to_tokens(block):
    clips, rows, wide = block.shape
    if clips == 1:
        return block.reshape(HEAD_GROUPS, rows // HEAD_GROUPS, wide)
    block = block.reshape(clips, HEAD_GROUPS, rows // HEAD_GROUPS, wide)
    return jnp.swapaxes(block, 0, 1).reshape(HEAD_GROUPS, -1, wide)


def other_keys(grouped, own, clips):
    if lax.axis_size("rest") == 1:
        return to_clips(swap(grouped, "core"), clips)
    near = [shift(own, k) for k in range(1, lax.axis_size("rest"))]
    far = swap(jnp.concatenate([own] + near, axis=1), "core")
    return jnp.concatenate(near + [far], axis=1)


def return_keys(kept, sent):
    queries = kept.shape[1]
    count = lax.axis_size("rest")
    near = (count - 1) * queries
    back = swap(sent[:, near:], "core")
    total = kept
    for k in range(1, count):
        part = sent[:, (k - 1) * queries : k * queries].astype(F32)
        part = part + back[:, k * queries : (k + 1) * queries].astype(F32)
        total = total + shift(part.astype(BF16), -k).astype(F32)
    return total, back[:, :queries]


def pick(flag, one, two):
    return jnp.where(flag, one, two)


def gather_weight(*blocks):
    core = lax.axis_index("core")
    quads = lax.axis_size("quad")
    part = blocks[0].shape[0] // (2 * quads)
    quad = lax.axis_index("quad")

    def cut(which):
        start = (which * quads + quad) * part
        return jnp.concatenate(
            [lax.dynamic_slice_in_dim(block, start, part, 0) for block in blocks], axis=1
        )

    own = cut(core)
    came = swap(cut(1 - core), "core")
    first = pick(core == 0, own, came)
    second = pick(core == 0, came, own)
    return [
        lax.all_gather(item, ("side", "rest", "core", "quad"), axis=0, tiled=True)
        for item in (first, second)
    ]


def in_order(second, mine, other):
    return pick(second, other, mine), pick(second, mine, other)


def start_downs(block):
    if lax.axis_size("rest") > 1 or lax.axis_size("quad") != 2:
        first, second = gather_weight(block)
        return None, first, second
    core, quad = lax.axis_index("core"), lax.axis_index("quad")
    part = block.shape[0] // 4
    mine, other = in_order(core == 1, block, swap(block, "core"))
    line = lax.dynamic_slice_in_dim(other, (core * 2 + quad) * part, part, 0)
    second = lax.all_gather(line, ("side", "rest", "core", "quad"), axis=0, tiled=True)
    near = lax.dynamic_slice_in_dim(mine, core * 2 * part, 2 * part, 0)
    return swap(near, "side"), mine, second


def finish_down(near, mine):
    if near is None:
        return mine
    core, side = lax.axis_index("core"), lax.axis_index("side")
    other = jnp.concatenate(in_order(core == 1, near, swap(near, "core")), axis=0)
    return jnp.concatenate(in_order(side == 1, mine, other), axis=0)


def add(one, two):
    return (one.astype(F32) + two.astype(F32)).astype(one.dtype)


def cut_columns(left, which):
    shards = lax.axis_size("side") * lax.axis_size("rest")
    part = left.shape[1] // (2 * shards)
    return jnp.concatenate(
        [
            lax.dynamic_slice_in_dim(left, (2 * s + which) * part, part, 1)
            for s in range(shards)
        ],
        axis=1,
    )


def weight_halves(left, right):
    core = lax.axis_index("core")
    return [
        t_dot(cut_columns(left, which), right).astype(BF16) for which in (1 - core, core)
    ]


def parts_body(side_ref, *refs):
    far_one, far_two, near_one, near_two = refs[:4]
    sent_ref, kept_ref = refs[-2:]
    sent_ref[...] = (far_one[...].astype(F32) + far_two[...].astype(F32)).astype(BF16)
    kept_ref[...] = (near_one[...].astype(F32) + near_two[...].astype(F32)).astype(BF16)


def side_parts(sent, kept, *after):
    came = swap(sent, "core")
    rows, wide = kept.shape
    half = rows // 2
    block = next((n for n in ROW_BLOCKS if half % n == 0), half)
    steps = half // block
    far = pl.BlockSpec((block, wide), lambda i, side: ((1 - side[0]) * steps + i, 0))
    near = pl.BlockSpec((block, wide), lambda i, side: (side[0] * steps + i, 0))
    out = pl.BlockSpec((block, wide), lambda i, side: (i, 0))
    return pl.pallas_call(
        parts_body,
        out_shape=(jax.ShapeDtypeStruct((half, wide), BF16),) * 2,
        grid_spec=pltpu.PrefetchScalarGridSpec(
            num_scalar_prefetch=1,
            grid=(steps,),
            in_specs=[far, far, near, near]
            + [pl.BlockSpec(memory_space=pl.ANY)] * len(after),
            out_specs=(out, out),
        ),
        compiler_params=pltpu.CompilerParams(vmem_limit_bytes=VMEM_LIMIT),
        cost_estimate=pl.CostEstimate(
            flops=kept.size, bytes_accessed=6 * kept.size, transcendentals=0
        ),
    )(lax.axis_index("side").astype(jnp.int32).reshape(1), kept, came, kept, came, *after)


def side_sum(sent, kept, *after):
    total = add_after(kept, swap(sent, "side"), after)
    if lax.axis_size("rest") > 1:
        total = lax.psum_scatter(total, "rest", scatter_dimension=0, tiled=True)
    return total


def line_sum(*items):
    return lax.psum(items, ("half", "quad"))


def line_hop(block, pairs):
    return lax.ppermute(block, ("half", "quad"), pairs)


def line_sums(begun, sides, ties):
    inner = lax.axis_index("half") != lax.axis_index("quad")
    count = len(begun) + len(sides)
    totals, mark = [*begun, *sides], ()
    results = []
    for turn in range(2, count + 2):
        mark = (*mark, *ties.get(turn, ()))
        if turn < count:
            totals[turn] = totals[turn](*mark)
            mark = (totals[turn],)
        for hops, at in ((INWARD, turn - 1), (ACROSS, turn - 2)):
            if 0 <= at < count:
                if hops is ACROSS:
                    mark = (*mark, *results[-1:])
                totals[at] = add_after(totals[at], line_hop(totals[at], hops), mark)
                mark = (totals[at],)
                if hops is ACROSS:
                    results.append(pick(inner, totals[at], line_hop(totals[at], OUTWARD)))
    return results


def join_cores(first, second):
    core = lax.axis_index("core")
    came = swap(pick(core == 0, second, first), "core")
    mine = pick(core == 0, first, second)
    return jnp.concatenate([pick(core == 0, mine, came), pick(core == 0, came, mine)], axis=0)


def swap_in(block):
    core, half = lax.axis_index("core"), lax.axis_index("half")
    micro, rows, wide = block.shape
    block = block.reshape(2, (micro // 2) * rows, wide)
    own = lax.dynamic_index_in_dim(block, half, 0, keepdims=False)
    other = lax.dynamic_index_in_dim(block, 1 - half, 0, keepdims=False)
    came = lax.ppermute(other, ("core", "half"), [(1, 2), (2, 1)])
    return pick(core == half, own, came)


def start_out(first, second):
    second_core, second_half = lax.axis_index("core") == 1, lax.axis_index("half") == 1
    mine, sent = in_order(second_core, first, second)
    parts = in_order(second_core, mine, swap(sent, "core"))
    mine, sent = in_order(second_half, *parts)
    return mine, swap(sent, "half")


def finish_out(mine, came, micro):
    rows, wide = mine.shape
    clips = in_order(lax.axis_index("half") == 1, mine, came)
    return jnp.stack(clips).reshape(micro, 2 * rows // micro, wide)


def forward_layer(x, weights, clips, head, keep):
    joined, w_down, gains, shifts, b_qkv, b_out, b_down, b_up = weights
    grouped, normed_one = qkv_forward(x, gains[0:1], shifts[0:1], joined, b_qkv)
    grouped = spread(grouped)
    own = to_clips(grouped, clips)
    other = other_keys(grouped, own, clips)
    att, log_total = attend_forward(own, other, head)
    if callable(w_down):
        w_down = w_down()
        weights = (joined, w_down, *weights[2:])
    att = spread(to_tokens(att))
    y, *kept = feed_forward(
        x, att, joined, b_out, gains[1:2], shifts[1:2], b_up, w_down, b_down, keep
    )
    return y, (x, normed_one, own, other, log_total, *kept), weights


def attention_grads(kept, d_att, clips, head, after):
    return heads_back(kept, to_clips(spread(d_att), clips), head, after)


def heads_back(kept, d_heads, head, after):
    own, other, log_total = kept[2:5]
    dq, kept_kv, sent_kv = attend_backward(own, other, d_heads, log_total, head, after)
    return (dq, *return_keys(kept_kv, sent_kv))


def spread_grads(grads, after=()):
    return spread(to_tokens(join_grads(*grads, after)))


def backward_lean(kept, g, weights, clips, head, *after):
    x, _, _, _, _, x1, _, slope, _, _ = kept
    joined, w_down, gains = weights[:3]
    _, dx1, _, d_att, _, _ = feed_backward(g, slope, w_down, joined, x1, gains[1:2])
    d_tokens = spread_grads(attention_grads(kept, d_att, clips, head, after))
    return qkv_backward(d_tokens, joined, x, dx1, gains[0:1])[0]


def small_rows(sums_one, sums_two, up_sum, shards, wide):
    rows = jnp.concatenate(
        [
            sums_one[0:1],
            sums_two[0:1],
            sums_one[1:2],
            sums_two[1:2],
            sums_one[2:4],
            sums_two[2:4],
        ]
    )
    rows = jnp.swapaxes(rows.reshape(8, shards, -1), 0, 1).reshape(shards, -1)
    packed = jnp.concatenate([rows, up_sum.reshape(shards, -1)], axis=1).astype(BF16)
    packed = packed.reshape(shards, 2, -1)
    lines = -(-packed.shape[2] // wide)
    room = 16 * (-(-lines // 16)) * wide
    packed = jnp.pad(packed, ((0, 0), (0, 0), (0, room - packed.shape[2])))
    return packed.reshape(shards, 2, -1, wide)


def beside(weight, *rows):
    shards, _, wide = rows[0].shape
    return jnp.concatenate([weight.reshape(shards, -1, wide), *rows], axis=1).reshape(-1, wide)


def rest_halves(normed_one, flat, out, sums_one, sums_two, up_sum, shards):
    core = lax.axis_index("core")
    wide = flat.shape[1]
    rows = small_rows(sums_one, sums_two, up_sum, shards, wide)
    return [
        beside(
            item,
            lax.dynamic_index_in_dim(rows, which, 1, keepdims=False),
            outs.reshape(shards, -1, wide),
        )
        for item, outs, which in zip(weight_halves(normed_one, flat), out, (1 - core, core))
    ]


def backward_all(kept_first, kept_second, g, layers, clips, head, shards):
    x, normed_one, _, _, _, x1, normed_two, slope, lifted, att = kept_second
    joined, w_down, gains = layers[1][:3]
    d_upper, dx1, branch, d_att, sums_two, up_sum = feed_backward(
        g, slope, w_down, joined, x1, gains[1:2]
    )
    down = weight_halves(lifted, g)
    up = weight_halves(normed_two, d_upper)
    grads = attention_grads(kept_second, d_att, clips, head, (*down, *up))
    d_tokens = spread_grads(grads)
    out = weight_halves(att, branch)
    down = side_parts(*down, d_tokens)
    d_second, flat, sums_one = qkv_backward(
        d_tokens, joined, x, dx1, gains[0:1], (*down, *out)
    )
    rest = rest_halves(normed_one, flat, out, sums_one, sums_two, up_sum, shards)

    x, normed_one, _, _, _, x1, normed_two, slope, lifted, att = kept_first
    joined, w_down, gains = layers[0][:3]
    d_upper, dx1, branch, d_att, sums_two, up_sum = feed_backward(
        d_second, slope, w_down, joined, x1, gains[1:2]
    )
    down_one = weight_halves(lifted, d_second)
    up_one = weight_halves(normed_two, d_upper)
    d_heads = to_clips(spread(d_att), clips)
    up = side_parts(*up, d_heads)
    down_two = side_sum(*down)
    grads = heads_back(
        kept_first, d_heads, head, (down_two, *up, *rest, *down_one, *up_one)
    )
    rest = side_parts(*rest, grads[0])
    up_two = side_sum(*up, grads[0])
    line = lax.axis_size("quad") == 2
    if line:
        down_two = add_after(down_two, line_hop(down_two, INWARD), (grads[0],))
    d_tokens = spread_grads(grads, (down_two, up_two, *rest))
    down_one, up_one = side_parts(*down_one), side_parts(*up_one)
    out_one = weight_halves(att, branch)
    d_first, flat, sums_one = qkv_backward(
        d_tokens, joined, x, dx1, gains[0:1], (*down_one, *up_one, *out_one)
    )
    placed = start_out(d_first, d_second)
    halves = rest_halves(normed_one, flat, out_one, sums_one, sums_two, up_sum, shards)
    rest_one = side_parts(*halves)
    blocks = (
        (rest, halves[0]),
        (down_one, rest_one[0]),
        (up_one, rest_one[0]),
        (rest_one, rest_one[0]),
    )
    sides = [
        lambda *after, item=item, mark=mark: side_sum(*item, *after, mark)
        for item, mark in blocks
    ]
    if line:
        sums = line_sums((down_two, up_two), sides, {3: placed[1:]})
    else:
        sums = line_sum(down_two, up_two, *(item() for item in sides))
    down_two, up_two, rest_two, down_one, up_one, rest_one = sums
    firsts = (rest_one, up_one, down_one)
    seconds = (rest_two, up_two, down_two)
    return placed, [join_cores(a, b) for a, b in zip(firsts, seconds)]


def gather_small(block):
    core, side = lax.axis_index("core"), lax.axis_index("side")
    if lax.axis_size("rest") > 1:
        whole_block = lax.all_gather(block, ("core", "side", "rest"), axis=0, tiled=False)
        return whole_block.reshape(2, -1, block.shape[0])
    came = swap(block, "side")
    layer = jnp.stack([pick(side == 0, block, came), pick(side == 0, came, block)])
    came = swap(layer, "core")
    return jnp.stack([pick(core == 0, layer, came), pick(core == 0, came, layer)])


def per_device(
    frames, out_grad, norm_gain, norm_bias, w_qkv, w_out, w_up, w_down, proj_bias, up_bias
):
    pairs = lax.axis_size("pair")
    pair = lax.axis_index("pair")
    shards = lax.axis_size("side") * lax.axis_size("rest")
    micro, _, width = frames.shape
    clips = micro // 2
    head = width // HEADS
    part = width // shards

    joined = gather_weight(w_qkv[0], w_out[0], w_up[0])
    near, mine, second_down = start_downs(w_down[0])
    downs = [lambda: finish_down(near, mine), lambda: second_down]
    small = jnp.concatenate(
        [norm_gain.reshape(-1), norm_bias.reshape(-1), proj_bias.reshape(-1), up_bias.reshape(-1)]
    )
    small = gather_small(small).astype(F32)
    rows = jnp.swapaxes(small[:, :, : 8 * part].reshape(2, shards, 8, part), 1, 2)
    rows = rows.reshape(2, 8, width)
    ups = small[:, :, 8 * part :].reshape(2, 1, -1)
    x_start = swap_in(frames)
    layers = []
    for layer in range(2):
        r = rows[layer]
        b_qkv = jnp.concatenate([r[4:5], jnp.zeros_like(r[4:5]), r[5:6]], axis=1)
        layers.append(
            (joined[layer], downs[layer], r[0:2], r[2:4], b_qkv, r[6:7], r[7:8], ups[layer])
        )

    x = x_start if near is None else copy_after(x_start, (near,))
    for phase in range(pairs):
        if phase > 0:
            came = lax.ppermute(second, "pair", [(i, i + 1) for i in range(pairs - 1)])
            x = pick(pair == 0, x_start, came)
        keep = phase == pairs - 1
        first, kept_first, layers[0] = forward_layer(x, layers[0], clips, head, keep)
        second, kept_second, layers[1] = forward_layer(first, layers[1], clips, head, keep)
    hidden = finish_out(*start_out(first, second), micro)

    g_start = swap_in(out_grad)
    g = g_start
    for phase in range(pairs - 1):
        d_second = backward_lean(kept_second, g, layers[1], clips, head, hidden)
        d_first = backward_lean(kept_first, d_second, layers[0], clips, head)
        came = lax.ppermute(d_first, "pair", [(i + 1, i) for i in range(pairs - 1)])
        g = pick(pair == pairs - 1, g_start, came)
    placed, (rest, up, down) = backward_all(
        kept_first, kept_second, g, layers, clips, head, shards
    )
    input_grads = finish_out(*placed, micro)

    own_rows = part // 2
    rest = rest.reshape(2, -1, 3 * width)
    out_rows = own_rows // 3
    qkv = rest[:, :own_rows].reshape(-1, 3 * width)
    out = rest[:, rest.shape[1] - out_rows :].reshape(-1, width)
    packed = rest[:, own_rows : rest.shape[1] - out_rows].astype(F32)
    packed = packed.reshape(2, -1)[:, : (8 * part + up_bias.shape[1]) // 2].reshape(-1)
    heads = packed[: 8 * part].reshape(8, part)
    return (
        hidden[None],
        input_grads[None],
        heads[0:2][None],
        heads[2:4][None],
        qkv.astype(F32)[None],
        out.astype(F32)[None],
        up.astype(F32)[None],
        down.astype(F32)[None],
        heads[4:8][None],
        packed[8 * part :][None],
    )


def solution(mesh):
    sections, groups, shards = (mesh.shape[name] for name in ("section", "seq", "shard"))
    cut = Mesh(
        mesh.devices.reshape(sections // 2, 2, 2, groups // 2, 2, shards // 2),
        AXES,
    )
    section, seq, shard = ("pair", "core"), ("half", "quad"), ("side", "rest")
    rows = seq + shard
    return jax.shard_map(
        per_device,
        mesh=cut,
        in_specs=(
            P(None, rows, None),
            P(None, rows, None),
            P(section, None, shard),
            P(section, None, shard),
            P(section, shard, None),
            P(section, shard, None),
            P(section, shard, None),
            P(section, shard, None),
            P(section, None, shard),
            P(section, shard),
        ),
        out_specs=(
            P(section, None, rows, None),
            P(section, None, rows, None),
            P(section, None, shard),
            P(section, None, shard),
            P(section, shard, None),
            P(section, shard, None),
            P(section, shard, None),
            P(section, shard, None),
            P(section, None, shard),
            P(section, shard),
        ),
        check_vma=False,
    )
```

```python
import math

import jax
import jax.numpy as jnp
from jax import lax
from jax.experimental import pallas as pl
from jax.experimental.pallas import tpu as pltpu
from jax.sharding import Mesh
from jax.sharding import PartitionSpec as P

HEADS = 12
norm_eps = 1e-05
F32 = jnp.float32
BF16 = jnp.bfloat16
VMEM_LIMIT = 56 * 1024 * 1024
AXES = ("pair", "core", "half", "quad", "side", "rest")
HEAD_GROUPS = 4
INWARD, ACROSS, OUTWARD = [(0, 1), (3, 2)], [(1, 2), (2, 1)], [(1, 0), (2, 3)]
ROW_BLOCKS = (272, 256, 192, 128, 96, 80, 64, 48)


def call(body, out_shapes, grid=None, in_specs=None, out_specs=None, scratch=(), flops=0, moved=0):
    extra = {} if grid is None else dict(grid=grid, in_specs=in_specs, out_specs=out_specs)
    return pl.pallas_call(
        body,
        out_shape=out_shapes,
        scratch_shapes=scratch,
        compiler_params=pltpu.CompilerParams(vmem_limit_bytes=VMEM_LIMIT),
        cost_estimate=pl.CostEstimate(flops=flops, bytes_accessed=moved, transcendentals=0),
        **extra,
    )


def dot(left, right):
    return jnp.dot(left, right, preferred_element_type=F32)


def dot_t(left, right):
    return lax.dot_general(left, right, (((1,), (1,)), ((), ())), preferred_element_type=F32)


def t_dot(left, right):
    return lax.dot_general(left, right, (((0,), (0,)), ((), ())), preferred_element_type=F32)


def norm_parts(values):
    center = values - jnp.mean(values, axis=-1, keepdims=True)
    inverse = lax.rsqrt(jnp.mean(center * center, axis=-1, keepdims=True) + norm_eps)
    return center * inverse, inverse


def norm_back(upstream, scaled, inverse, gain_row):
    weighted = upstream * gain_row
    return inverse * (
        weighted
        - jnp.mean(weighted, axis=-1, keepdims=True)
        - scaled * jnp.mean(weighted * scaled, axis=-1, keepdims=True)
    )


def qkv_body(x_ref, gain_ref, shift_ref, w_ref, bias_ref, out_ref, normed_ref):
    scaled, _ = norm_parts(x_ref[...].astype(F32))
    normed = (scaled * gain_ref[...] + shift_ref[...]).astype(BF16)
    normed_ref[...] = normed
    span = out_ref.shape[2] // 3
    width = x_ref.shape[1]
    for part in range(3):
        cols = slice(part * width, (part + 1) * width)
        piece = (dot(normed, w_ref[:, cols]) + bias_ref[:, cols]).astype(BF16)
        for g in range(HEAD_GROUPS):
            out_ref[g, :, part * span : (part + 1) * span] = piece[:, g * span : (g + 1) * span]


def qkv_forward(x, gain, shift, joined, bias):
    rows, width = x.shape
    span = width // HEAD_GROUPS
    return call(
        qkv_body,
        (
            jax.ShapeDtypeStruct((HEAD_GROUPS, rows, 3 * span), BF16),
            jax.ShapeDtypeStruct((rows, width), BF16),
        ),
        grid=(1,),
        in_specs=[
            whole((rows, width)),
            whole((1, width)),
            whole((1, width)),
            whole((width, 3 * width)),
            whole((1, 3 * width)),
        ],
        out_specs=(whole((HEAD_GROUPS, rows, 3 * span)), whole((rows, width))),
        flops=2 * rows * width * 3 * width,
        moved=6 * width * width + 10 * x.size,
    )(x, gain, shift, joined, bias)


def key_chunks(own_ref, other_ref):
    place = 0
    for ref in (own_ref, other_ref):
        total = ref.shape[1]
        step = 256 if total % 256 == 0 else total
        for start in range(0, total, step):
            yield ref, start, place, step
            place += step


def attend_body(q_ref, own_ref, other_ref, out_ref, log_ref, score_ref, *, head):
    span = q_ref.shape[2] // 3
    queries = q_ref.shape[1]
    scale = 1.0 / math.sqrt(head)
    for h in range(span // head):
        q = q_ref[0, :, h * head : (h + 1) * head] * scale
        top = jnp.full((1, queries), -jnp.inf, F32)
        for ref, start, place, step in key_chunks(own_ref, other_ref):
            k = ref[0, start : start + step, span + h * head : span + (h + 1) * head]
            scores = dot_t(k, q)
            score_ref[place : place + step, :] = scores
            top = jnp.maximum(top, jnp.max(scores, axis=0, keepdims=True))
        total = jnp.zeros((1, queries), F32)
        acc = jnp.zeros((head, queries), F32)
        for ref, start, place, step in key_chunks(own_ref, other_ref):
            v = ref[0, start : start + step, 2 * span + h * head : 2 * span + (h + 1) * head]
            e = jnp.exp(score_ref[place : place + step, :] - top)
            total = total + jnp.sum(e, axis=0, keepdims=True)
            acc = acc + t_dot(v, e.astype(BF16))
        out_ref[0, :, h * head : (h + 1) * head] = jnp.transpose(acc / total).astype(BF16)
        log_ref[0, h : h + 1, :] = top + jnp.log(total)


def query_block(queries):
    return 256 if queries % 256 == 0 else queries


def attend_forward(own, other, head):
    clips, queries, wide = own.shape
    span = wide // 3
    keys = queries + other.shape[1]
    block = query_block(queries)

    def body(*refs):
        attend_body(*refs, head=head)

    return call(
        body,
        (
            jax.ShapeDtypeStruct((clips, queries, span), BF16),
            jax.ShapeDtypeStruct((clips, span // head, queries), F32),
        ),
        grid=(clips, queries // block),
        in_specs=[
            pl.BlockSpec((1, block, wide), lambda m, i: (m, i, 0)),
            pl.BlockSpec((1, queries, wide), lambda m, i: (m, 0, 0)),
            pl.BlockSpec((1, other.shape[1], wide), lambda m, i: (m, 0, 0)),
        ],
        out_specs=(
            pl.BlockSpec((1, block, span), lambda m, i: (m, i, 0)),
            pl.BlockSpec((1, span // head, block), lambda m, i: (m, 0, i)),
        ),
        scratch=[pltpu.VMEM((keys, block), F32)],
        flops=16 * clips * queries * keys * span,
        moved=4 * (own.size + other.size),
    )(own, own, other)


def attend_back_body(
    q_ref,
    own_ref,
    other_ref,
    grad_ref,
    log_ref,
    dq_ref,
    dkv_own_ref,
    dkv_other_ref,
    p_ref,
    dp_ref,
    dk_acc,
    dv_acc,
    *,
    head,
):
    span = q_ref.shape[2] // 3
    queries = q_ref.shape[1]
    heads = span // head
    scale = 1.0 / math.sqrt(head)

    @pl.when(pl.program_id(1) == 0)
    def _():
        dk_acc[...] = jnp.zeros_like(dk_acc)
        dv_acc[...] = jnp.zeros_like(dv_acc)

    for h in range(heads):
        q = q_ref[0, :, h * head : (h + 1) * head] * scale
        d_out = grad_ref[0, :, h * head : (h + 1) * head]
        log_total = log_ref[0, h : h + 1, :]
        row_term = jnp.zeros((1, queries), F32)
        for ref, start, place, step in key_chunks(own_ref, other_ref):
            k = ref[0, start : start + step, span + h * head : span + (h + 1) * head]
            v = ref[0, start : start + step, 2 * span + h * head : 2 * span + (h + 1) * head]
            probs = jnp.exp(dot_t(k, q) - log_total)
            d_probs = dot_t(v, d_out)
            p_ref[place : place + step, :] = probs
            dp_ref[place : place + step, :] = d_probs
            row_term = row_term + jnp.sum(probs * d_probs, axis=0, keepdims=True)
            dv_acc[h, place : place + step, :] += dot(probs.astype(BF16), d_out)
        dq = jnp.zeros((head, queries), F32)
        for ref, start, place, step in key_chunks(own_ref, other_ref):
            k = ref[0, start : start + step, span + h * head : span + (h + 1) * head]
            d_scores = (
                p_ref[place : place + step, :] * (dp_ref[place : place + step, :] - row_term)
            ).astype(BF16)
            dk_acc[h, place : place + step, :] += dot(d_scores, q)
            dq = dq + t_dot(k, d_scores)
        dq_ref[0, :, h * head : (h + 1) * head] = jnp.transpose(dq * scale).astype(BF16)

    @pl.when(pl.program_id(1) == pl.num_programs(1) - 1)
    def _():
        place = 0
        for ref in (dkv_own_ref, dkv_other_ref):
            rows = ref.shape[1]
            for h in range(heads):
                ref[0, :, h * head : (h + 1) * head] = dk_acc[h, place : place + rows, :].astype(
                    ref.dtype
                )
                ref[0, :, span + h * head : span + (h + 1) * head] = dv_acc[
                    h, place : place + rows, :
                ].astype(ref.dtype)
            place += rows


def attend_backward(own, other, grad, log_total, head, after=()):
    clips, queries, wide = own.shape
    span = wide // 3
    others = other.shape[1]
    keys = queries + others
    block = query_block(queries)
    heads = span // head

    def body(*refs):
        attend_back_body(*refs[:5], *refs[5 + len(after) :], head=head)

    return call(
        body,
        (
            jax.ShapeDtypeStruct((clips, queries, span), BF16),
            jax.ShapeDtypeStruct((clips, queries, 2 * span), F32),
            jax.ShapeDtypeStruct((clips, others, 2 * span), BF16),
        ),
        grid=(clips, queries // block),
        in_specs=[
            pl.BlockSpec((1, block, wide), lambda m, i: (m, i, 0)),
            pl.BlockSpec((1, queries, wide), lambda m, i: (m, 0, 0)),
            pl.BlockSpec((1, others, wide), lambda m, i: (m, 0, 0)),
            pl.BlockSpec((1, block, span), lambda m, i: (m, i, 0)),
            pl.BlockSpec((1, heads, block), lambda m, i: (m, 0, i)),
        ]
        + [pl.BlockSpec(memory_space=pl.ANY)] * len(after),
        out_specs=(
            pl.BlockSpec((1, block, span), lambda m, i: (m, i, 0)),
            pl.BlockSpec((1, queries, 2 * span), lambda m, i: (m, 0, 0)),
            pl.BlockSpec((1, others, 2 * span), lambda m, i: (m, 0, 0)),
        ),
        scratch=[
            pltpu.VMEM((keys, block), F32),
            pltpu.VMEM((keys, block), F32),
            pltpu.VMEM((heads, keys, head), F32),
            pltpu.VMEM((heads, keys, head), F32),
        ],
        flops=40 * clips * queries * keys * span,
        moved=8 * (own.size + other.size),
    )(own, own, other, grad, log_total, *after)


def feed_body(
    x_ref,
    att_ref,
    w_out_ref,
    b_out_ref,
    gain_ref,
    shift_ref,
    w_up_ref,
    b_up_ref,
    w_down_ref,
    b_down_ref,
    y_ref,
    *rest,
):
    if len(rest) > 2:
        x1_ref, normed_ref, slope_ref, lifted_ref, flat_ref, acc = rest
    else:
        normed_ref, acc = rest
    span = att_ref.shape[2]

    @pl.when(pl.program_id(0) == 0)
    def _():
        middle = x_ref[...].astype(F32) + b_out_ref[...]
        for g in range(HEAD_GROUPS):
            middle = middle + dot(att_ref[g], w_out_ref[g * span : (g + 1) * span, :])
            if len(rest) > 2:
                flat_ref[:, g * span : (g + 1) * span] = att_ref[g]
        if len(rest) > 2:
            x1_ref[...] = middle
        scaled, _ = norm_parts(middle)
        normed_ref[...] = (scaled * gain_ref[...] + shift_ref[...]).astype(BF16)
        acc[...] = middle + b_down_ref[...]

    upper = dot(normed_ref[...], w_up_ref[...]) + b_up_ref[...]
    phi = 0.5 * (1.0 + lax.erf(upper * math.sqrt(0.5)))
    lifted = (upper * phi).astype(BF16)
    if len(rest) > 2:
        density = jnp.exp(-0.5 * upper * upper) * (1.0 / math.sqrt(2.0 * math.pi))
        slope_ref[...] = phi + upper * density
        lifted_ref[...] = lifted
    acc[...] += dot(lifted, w_down_ref[...])

    @pl.when(pl.program_id(0) == pl.num_programs(0) - 1)
    def _():
        y_ref[...] = acc[...].astype(BF16)


def whole(shape):
    return pl.BlockSpec(shape, lambda i: (0,) * len(shape))


def feed_forward(x, att, joined, b_out, gain, shift, b_up, w_down, b_down, keep):
    rows, width = x.shape
    hidden = w_down.shape[0]
    row = whole((1, width))
    full = whole((rows, width))
    part = pl.BlockSpec((rows, width), lambda i: (0, i))
    shapes = [jax.ShapeDtypeStruct((rows, width), BF16)]
    specs = [full]
    scratch = [pltpu.VMEM((rows, width), F32)]
    if keep:
        shapes += [
            jax.ShapeDtypeStruct((rows, width), F32),
            jax.ShapeDtypeStruct((rows, width), BF16),
            jax.ShapeDtypeStruct((rows, hidden), F32),
            jax.ShapeDtypeStruct((rows, hidden), BF16),
            jax.ShapeDtypeStruct((rows, width), BF16),
        ]
        specs += [full, full, part, part, full]
    else:
        scratch = [pltpu.VMEM((rows, width), BF16)] + scratch
    return call(
        feed_body,
        tuple(shapes),
        grid=(hidden // width,),
        in_specs=[
            full,
            whole(att.shape),
            pl.BlockSpec((width, width), lambda i: (0, 3)),
            row,
            row,
            row,
            pl.BlockSpec((width, width), lambda i: (0, 4 + i)),
            pl.BlockSpec((1, width), lambda i: (0, i)),
            pl.BlockSpec((width, width), lambda i: (i, 0)),
            row,
        ],
        out_specs=tuple(specs),
        scratch=scratch,
        flops=2 * rows * width * (2 * hidden + width),
        moved=4 * w_down.size + 2 * width * width + 10 * rows * hidden,
    )(x, att, joined, b_out, gain, shift, joined, b_up, w_down, b_down)


def feed_back_body(
    g_ref,
    slope_ref,
    w_down_ref,
    w_up_ref,
    w_out_ref,
    x1_ref,
    gain_ref,
    d_upper_ref,
    dx1_ref,
    branch_ref,
    datt_ref,
    sums_ref,
    up_sum_ref,
    acc,
):
    @pl.when(pl.program_id(0) == 0)
    def _():
        acc[...] = jnp.zeros_like(acc)

    d_upper = (dot_t(g_ref[...], w_down_ref[...]) * slope_ref[...]).astype(BF16)
    d_upper_ref[...] = d_upper
    up_sum_ref[...] = jnp.sum(d_upper.astype(F32), axis=0, keepdims=True)
    acc[...] += dot_t(d_upper, w_up_ref[...])

    @pl.when(pl.program_id(0) == pl.num_programs(0) - 1)
    def _():
        d_normed = acc[...]
        upstream = g_ref[...].astype(F32)
        scaled, inverse = norm_parts(x1_ref[...])
        d_middle = upstream + norm_back(d_normed, scaled, inverse, gain_ref[...])
        dx1_ref[...] = d_middle
        branch = d_middle.astype(BF16)
        branch_ref[...] = branch
        span = datt_ref.shape[2]
        for g in range(HEAD_GROUPS):
            datt_ref[g] = dot_t(branch, w_out_ref[g * span : (g + 1) * span, :]).astype(BF16)
        sums_ref[0:1, :] = jnp.sum(d_normed * scaled, axis=0, keepdims=True)
        sums_ref[1:2, :] = jnp.sum(d_normed, axis=0, keepdims=True)
        sums_ref[2:3, :] = jnp.sum(branch.astype(F32), axis=0, keepdims=True)
        sums_ref[3:4, :] = jnp.sum(upstream, axis=0, keepdims=True)


def feed_backward(g, slope, w_down, joined, x1, gain):
    rows, width = g.shape
    hidden = w_down.shape[0]
    chunk = width
    full = whole((rows, width))
    return call(
        feed_back_body,
        (
            jax.ShapeDtypeStruct((rows, hidden), BF16),
            jax.ShapeDtypeStruct((rows, width), F32),
            jax.ShapeDtypeStruct((rows, width), BF16),
            jax.ShapeDtypeStruct((HEAD_GROUPS, rows, width // HEAD_GROUPS), BF16),
            jax.ShapeDtypeStruct((4, width), F32),
            jax.ShapeDtypeStruct((1, hidden), F32),
        ),
        grid=(hidden // chunk,),
        in_specs=[
            full,
            pl.BlockSpec((rows, chunk), lambda i: (0, i)),
            pl.BlockSpec((chunk, width), lambda i: (i, 0)),
            pl.BlockSpec((width, chunk), lambda i: (0, 4 + i)),
            pl.BlockSpec((width, width), lambda i: (0, 3)),
            full,
            whole((1, width)),
        ],
        out_specs=(
            pl.BlockSpec((rows, chunk), lambda i: (0, i)),
            full,
            full,
            whole((HEAD_GROUPS, rows, width // HEAD_GROUPS)),
            whole((4, width)),
            pl.BlockSpec((1, chunk), lambda i: (0, i)),
        ),
        scratch=[pltpu.VMEM((rows, width), F32)],
        flops=2 * rows * width * (2 * hidden + width),
        moved=4 * w_down.size + 2 * width * width + 6 * rows * hidden,
    )(g, slope, w_down, joined, joined, x1, gain)


def qkv_back_body(grads_ref, w_ref, x_ref, dx1_ref, gain_ref, dx_ref, flat_ref, sums_ref):
    width = x_ref.shape[1]
    span = grads_ref.shape[2] // 3
    for g in range(HEAD_GROUPS):
        for part in range(3):
            flat_ref[:, part * width + g * span : part * width + (g + 1) * span] = grads_ref[
                g, :, part * span : (part + 1) * span
            ]
    d_normed = dot_t(flat_ref[...], w_ref[...])
    scaled, inverse = norm_parts(x_ref[...].astype(F32))
    dx = dx1_ref[...] + norm_back(d_normed, scaled, inverse, gain_ref[...])
    dx_ref[...] = dx.astype(BF16)
    sums_ref[0:1, :] = jnp.sum(d_normed * scaled, axis=0, keepdims=True)
    sums_ref[1:2, :] = jnp.sum(d_normed, axis=0, keepdims=True)
    sums_ref[2:3, :] = jnp.sum(flat_ref[:, :width].astype(F32), axis=0, keepdims=True)
    sums_ref[3:4, :] = jnp.sum(flat_ref[:, 2 * width :].astype(F32), axis=0, keepdims=True)


def qkv_backward(grads, joined, x, dx1, gain, after=()):
    rows, width = x.shape

    def body(*refs):
        qkv_back_body(*refs[:5], *refs[5 + len(after) :])

    return call(
        body,
        (
            jax.ShapeDtypeStruct((rows, width), BF16),
            jax.ShapeDtypeStruct((rows, 3 * width), BF16),
            jax.ShapeDtypeStruct((4, width), F32),
        ),
        grid=(1,),
        in_specs=[
            whole(grads.shape),
            whole((width, 3 * width)),
            whole((rows, width)),
            whole((rows, width)),
            whole((1, width)),
        ]
        + [pl.BlockSpec(memory_space=pl.ANY)] * len(after),
        out_specs=(whole((rows, width)), whole((rows, 3 * width)), whole((4, width))),
        flops=2 * rows * width * 3 * width,
        moved=6 * width * width + 20 * x.size,
    )(grads, joined, x, dx1, gain, *after)


def add_body(one_ref, two_ref, *rest):
    rest[-1][...] = (one_ref[...].astype(F32) + two_ref[...].astype(F32)).astype(BF16)


def add_after(one, two, after):
    rows, wide = one.shape
    block = next((n for n in ROW_BLOCKS if rows % n == 0), rows)
    spec = pl.BlockSpec((block, wide), lambda i: (i, 0))
    return call(
        add_body,
        jax.ShapeDtypeStruct((rows, wide), BF16),
        grid=(rows // block,),
        in_specs=[spec, spec] + [pl.BlockSpec(memory_space=pl.ANY)] * len(after),
        out_specs=spec,
        flops=one.size,
        moved=6 * one.size,
    )(one, two, *after)


def copy_body(one_ref, *rest):
    rest[-1][...] = one_ref[...]


def copy_after(one, after):
    spec = pl.BlockSpec(one.shape, lambda i: (0, 0))
    return call(
        copy_body,
        jax.ShapeDtypeStruct(one.shape, one.dtype),
        grid=(1,),
        in_specs=[spec] + [pl.BlockSpec(memory_space=pl.ANY)] * len(after),
        out_specs=spec,
        flops=one.size,
        moved=4 * one.size,
    )(one, *after)


def join_body(dq_ref, kept_ref, back_ref, *rest):
    out_ref = rest[-1]
    span = dq_ref.shape[2]
    out_ref[:, :, :span] = dq_ref[...]
    out_ref[:, :, span:] = (kept_ref[...] + back_ref[...].astype(F32)).astype(BF16)


def join_grads(dq, kept, back, after):
    clips, rows, span = dq.shape

    def spec(wide):
        return pl.BlockSpec((1, rows, wide), lambda i: (i, 0, 0))

    return call(
        join_body,
        jax.ShapeDtypeStruct((clips, rows, 3 * span), BF16),
        grid=(clips,),
        in_specs=[spec(span), spec(2 * span), spec(2 * span)]
        + [pl.BlockSpec(memory_space=pl.ANY)] * len(after),
        out_specs=spec(3 * span),
        flops=kept.size,
        moved=8 * kept.size,
    )(dq, kept, back, *after)


def swap(block, axis):
    return lax.ppermute(block, axis, [(0, 1), (1, 0)])


def shift(block, distance):
    count = lax.axis_size("rest")
    return lax.ppermute(block, "rest", [(i, (i + distance) % count) for i in range(count)])


def spread(block):
    return lax.all_to_all(block, ("quad", "side"), 0, 0, tiled=True)


def to_clips(block, clips):
    groups, rows, wide = block.shape
    if clips == 1:
        return block.reshape(1, groups * rows, wide)
    block = block.reshape(groups, clips, rows // clips, wide)
    return jnp.swapaxes(block, 0, 1).reshape(clips, groups * (rows // clips), wide)


def to_tokens(block):
    clips, rows, wide = block.shape
    if clips == 1:
        return block.reshape(HEAD_GROUPS, rows // HEAD_GROUPS, wide)
    block = block.reshape(clips, HEAD_GROUPS, rows // HEAD_GROUPS, wide)
    return jnp.swapaxes(block, 0, 1).reshape(HEAD_GROUPS, -1, wide)


def other_keys(grouped, own, clips):
    if lax.axis_size("rest") == 1:
        return to_clips(swap(grouped, "core"), clips)
    near = [shift(own, k) for k in range(1, lax.axis_size("rest"))]
    far = swap(jnp.concatenate([own] + near, axis=1), "core")
    return jnp.concatenate(near + [far], axis=1)


def return_keys(kept, sent):
    queries = kept.shape[1]
    count = lax.axis_size("rest")
    near = (count - 1) * queries
    back = swap(sent[:, near:], "core")
    total = kept
    for k in range(1, count):
        part = sent[:, (k - 1) * queries : k * queries].astype(F32)
        part = part + back[:, k * queries : (k + 1) * queries].astype(F32)
        total = total + shift(part.astype(BF16), -k).astype(F32)
    return total, back[:, :queries]


def pick(flag, one, two):
    return jnp.where(flag, one, two)


def gather_weight(*blocks):
    core = lax.axis_index("core")
    quads = lax.axis_size("quad")
    part = blocks[0].shape[0] // (2 * quads)
    quad = lax.axis_index("quad")

    def cut(which):
        start = (which * quads + quad) * part
        return jnp.concatenate(
            [lax.dynamic_slice_in_dim(block, start, part, 0) for block in blocks], axis=1
        )

    own = cut(core)
    came = swap(cut(1 - core), "core")
    first = pick(core == 0, own, came)
    second = pick(core == 0, came, own)
    return [
        lax.all_gather(item, ("side", "rest", "core", "quad"), axis=0, tiled=True)
        for item in (first, second)
    ]


def in_order(second, mine, other):
    return pick(second, other, mine), pick(second, mine, other)


def start_downs(block):
    if lax.axis_size("rest") > 1 or lax.axis_size("quad") != 2:
        first, second = gather_weight(block)
        return None, first, second
    core, quad = lax.axis_index("core"), lax.axis_index("quad")
    part = block.shape[0] // 4
    mine, other = in_order(core == 1, block, swap(block, "core"))
    line = lax.dynamic_slice_in_dim(other, (core * 2 + quad) * part, part, 0)
    second = lax.all_gather(line, ("side", "rest", "core", "quad"), axis=0, tiled=True)
    near = lax.dynamic_slice_in_dim(mine, core * 2 * part, 2 * part, 0)
    return swap(near, "side"), mine, second


def finish_down(near, mine):
    if near is None:
        return mine
    core, side = lax.axis_index("core"), lax.axis_index("side")
    other = jnp.concatenate(in_order(core == 1, near, swap(near, "core")), axis=0)
    return jnp.concatenate(in_order(side == 1, mine, other), axis=0)


def add(one, two):
    return (one.astype(F32) + two.astype(F32)).astype(one.dtype)


def cut_columns(left, which):
    shards = lax.axis_size("side") * lax.axis_size("rest")
    part = left.shape[1] // (2 * shards)
    return jnp.concatenate(
        [
            lax.dynamic_slice_in_dim(left, (2 * s + which) * part, part, 1)
            for s in range(shards)
        ],
        axis=1,
    )


def weight_halves(left, right):
    core = lax.axis_index("core")
    return [
        t_dot(cut_columns(left, which), right).astype(BF16) for which in (1 - core, core)
    ]


def parts_body(side_ref, *refs):
    far_one, far_two, near_one, near_two = refs[:4]
    sent_ref, kept_ref = refs[-2:]
    sent_ref[...] = (far_one[...].astype(F32) + far_two[...].astype(F32)).astype(BF16)
    kept_ref[...] = (near_one[...].astype(F32) + near_two[...].astype(F32)).astype(BF16)


def side_parts(sent, kept, *after):
    came = swap(sent, "core")
    rows, wide = kept.shape
    half = rows // 2
    block = next((n for n in ROW_BLOCKS if half % n == 0), half)
    steps = half // block
    far = pl.BlockSpec((block, wide), lambda i, side: ((1 - side[0]) * steps + i, 0))
    near = pl.BlockSpec((block, wide), lambda i, side: (side[0] * steps + i, 0))
    out = pl.BlockSpec((block, wide), lambda i, side: (i, 0))
    return pl.pallas_call(
        parts_body,
        out_shape=(jax.ShapeDtypeStruct((half, wide), BF16),) * 2,
        grid_spec=pltpu.PrefetchScalarGridSpec(
            num_scalar_prefetch=1,
            grid=(steps,),
            in_specs=[far, far, near, near]
            + [pl.BlockSpec(memory_space=pl.ANY)] * len(after),
            out_specs=(out, out),
        ),
        compiler_params=pltpu.CompilerParams(vmem_limit_bytes=VMEM_LIMIT),
        cost_estimate=pl.CostEstimate(
            flops=kept.size, bytes_accessed=6 * kept.size, transcendentals=0
        ),
    )(lax.axis_index("side").astype(jnp.int32).reshape(1), kept, came, kept, came, *after)


def side_sum(sent, kept, *after):
    total = add_after(kept, swap(sent, "side"), after)
    if lax.axis_size("rest") > 1:
        total = lax.psum_scatter(total, "rest", scatter_dimension=0, tiled=True)
    return total


def line_sum(*items):
    return lax.psum(items, ("half", "quad"))


def line_hop(block, pairs):
    return lax.ppermute(block, ("half", "quad"), pairs)


def line_sums(begun, sides, ties):
    inner = lax.axis_index("half") != lax.axis_index("quad")
    count = len(begun) + len(sides)
    totals, mark = [*begun, *sides], ()
    results = []
    for turn in range(2, count + 2):
        mark = (*mark, *ties.get(turn, ()))
        if turn < count:
            totals[turn] = totals[turn](*mark)
            mark = (totals[turn],)
        for hops, at in ((INWARD, turn - 1), (ACROSS, turn - 2)):
            if 0 <= at < count:
                if hops is ACROSS:
                    mark = (*mark, *results[-1:])
                totals[at] = add_after(totals[at], line_hop(totals[at], hops), mark)
                mark = (totals[at],)
                if hops is ACROSS:
                    results.append(pick(inner, totals[at], line_hop(totals[at], OUTWARD)))
    return results


def join_cores(first, second):
    core = lax.axis_index("core")
    came = swap(pick(core == 0, second, first), "core")
    mine = pick(core == 0, first, second)
    return jnp.concatenate([pick(core == 0, mine, came), pick(core == 0, came, mine)], axis=0)


def swap_in(block):
    core, half = lax.axis_index("core"), lax.axis_index("half")
    micro, rows, wide = block.shape
    block = block.reshape(2, (micro // 2) * rows, wide)
    own = lax.dynamic_index_in_dim(block, half, 0, keepdims=False)
    other = lax.dynamic_index_in_dim(block, 1 - half, 0, keepdims=False)
    came = lax.ppermute(other, ("core", "half"), [(1, 2), (2, 1)])
    return pick(core == half, own, came)


def start_out(first, second):
    second_core, second_half = lax.axis_index("core") == 1, lax.axis_index("half") == 1
    mine, sent = in_order(second_core, first, second)
    parts = in_order(second_core, mine, swap(sent, "core"))
    mine, sent = in_order(second_half, *parts)
    return mine, swap(sent, "half")


def finish_out(mine, came, micro):
    rows, wide = mine.shape
    clips = in_order(lax.axis_index("half") == 1, mine, came)
    return jnp.stack(clips).reshape(micro, 2 * rows // micro, wide)


def forward_layer(x, weights, clips, head, keep):
    joined, w_down, gains, shifts, b_qkv, b_out, b_down, b_up = weights
    grouped, normed_one = qkv_forward(x, gains[0:1], shifts[0:1], joined, b_qkv)
    grouped = spread(grouped)
    own = to_clips(grouped, clips)
    other = other_keys(grouped, own, clips)
    att, log_total = attend_forward(own, other, head)
    if callable(w_down):
        w_down = w_down()
        weights = (joined, w_down, *weights[2:])
    att = spread(to_tokens(att))
    y, *kept = feed_forward(
        x, att, joined, b_out, gains[1:2], shifts[1:2], b_up, w_down, b_down, keep
    )
    return y, (x, normed_one, own, other, log_total, *kept), weights


def attention_grads(kept, d_att, clips, head, after):
    return heads_back(kept, to_clips(spread(d_att), clips), head, after)


def heads_back(kept, d_heads, head, after):
    own, other, log_total = kept[2:5]
    dq, kept_kv, sent_kv = attend_backward(own, other, d_heads, log_total, head, after)
    return (dq, *return_keys(kept_kv, sent_kv))


def spread_grads(grads, after=()):
    return spread(to_tokens(join_grads(*grads, after)))


def backward_lean(kept, g, weights, clips, head, *after):
    x, _, _, _, _, x1, _, slope, _, _ = kept
    joined, w_down, gains = weights[:3]
    _, dx1, _, d_att, _, _ = feed_backward(g, slope, w_down, joined, x1, gains[1:2])
    d_tokens = spread_grads(attention_grads(kept, d_att, clips, head, after))
    return qkv_backward(d_tokens, joined, x, dx1, gains[0:1])[0]


def small_rows(sums_one, sums_two, up_sum, shards, wide):
    rows = jnp.concatenate(
        [
            sums_one[0:1],
            sums_two[0:1],
            sums_one[1:2],
            sums_two[1:2],
            sums_one[2:4],
            sums_two[2:4],
        ]
    )
    rows = jnp.swapaxes(rows.reshape(8, shards, -1), 0, 1).reshape(shards, -1)
    packed = jnp.concatenate([rows, up_sum.reshape(shards, -1)], axis=1).astype(BF16)
    packed = packed.reshape(shards, 2, -1)
    lines = -(-packed.shape[2] // wide)
    room = 16 * (-(-lines // 16)) * wide
    packed = jnp.pad(packed, ((0, 0), (0, 0), (0, room - packed.shape[2])))
    return packed.reshape(shards, 2, -1, wide)


def beside(weight, *rows):
    shards, _, wide = rows[0].shape
    return jnp.concatenate([weight.reshape(shards, -1, wide), *rows], axis=1).reshape(-1, wide)


def rest_halves(normed_one, flat, out, sums_one, sums_two, up_sum, shards):
    core = lax.axis_index("core")
    wide = flat.shape[1]
    rows = small_rows(sums_one, sums_two, up_sum, shards, wide)
    return [
        beside(
            item,
            lax.dynamic_index_in_dim(rows, which, 1, keepdims=False),
            outs.reshape(shards, -1, wide),
        )
        for item, outs, which in zip(weight_halves(normed_one, flat), out, (1 - core, core))
    ]


def backward_all(kept_first, kept_second, g, layers, clips, head, shards):
    x, normed_one, _, _, _, x1, normed_two, slope, lifted, att = kept_second
    joined, w_down, gains = layers[1][:3]
    d_upper, dx1, branch, d_att, sums_two, up_sum = feed_backward(
        g, slope, w_down, joined, x1, gains[1:2]
    )
    down = weight_halves(lifted, g)
    up = weight_halves(normed_two, d_upper)
    grads = attention_grads(kept_second, d_att, clips, head, (*down, *up))
    d_tokens = spread_grads(grads)
    out = weight_halves(att, branch)
    down = side_parts(*down, d_tokens)
    d_second, flat, sums_one = qkv_backward(
        d_tokens, joined, x, dx1, gains[0:1], (*down, *out)
    )
    rest = rest_halves(normed_one, flat, out, sums_one, sums_two, up_sum, shards)

    x, normed_one, _, _, _, x1, normed_two, slope, lifted, att = kept_first
    joined, w_down, gains = layers[0][:3]
    d_upper, dx1, branch, d_att, sums_two, up_sum = feed_backward(
        d_second, slope, w_down, joined, x1, gains[1:2]
    )
    down_one = weight_halves(lifted, d_second)
    up_one = weight_halves(normed_two, d_upper)
    d_heads = to_clips(spread(d_att), clips)
    up = side_parts(*up, d_heads)
    down_two = side_sum(*down)
    grads = heads_back(
        kept_first, d_heads, head, (down_two, *up, *rest, *down_one, *up_one)
    )
    rest = side_parts(*rest, grads[0])
    up_two = side_sum(*up, grads[0])
    line = lax.axis_size("quad") == 2
    if line:
        down_two = add_after(down_two, line_hop(down_two, INWARD), (grads[0],))
    d_tokens = spread_grads(grads, (down_two, up_two, *rest))
    down_one, up_one = side_parts(*down_one), side_parts(*up_one)
    out_one = weight_halves(att, branch)
    d_first, flat, sums_one = qkv_backward(
        d_tokens, joined, x, dx1, gains[0:1], (*down_one, *up_one, *out_one)
    )
    placed = start_out(d_first, d_second)
    halves = rest_halves(normed_one, flat, out_one, sums_one, sums_two, up_sum, shards)
    rest_one = side_parts(*halves)
    blocks = (
        (rest, halves[0]),
        (down_one, rest_one[0]),
        (up_one, rest_one[0]),
        (rest_one, rest_one[0]),
    )
    sides = [
        lambda *after, item=item, mark=mark: side_sum(*item, *after, mark)
        for item, mark in blocks
    ]
    if line:
        sums = line_sums((down_two, up_two), sides, {4: placed[1:]})
    else:
        sums = line_sum(down_two, up_two, *(item() for item in sides))
    down_two, up_two, rest_two, down_one, up_one, rest_one = sums
    firsts = (rest_one, up_one, down_one)
    seconds = (rest_two, up_two, down_two)
    return placed, [join_cores(a, b) for a, b in zip(firsts, seconds)]


def gather_small(block):
    core, side = lax.axis_index("core"), lax.axis_index("side")
    if lax.axis_size("rest") > 1:
        whole_block = lax.all_gather(block, ("core", "side", "rest"), axis=0, tiled=False)
        return whole_block.reshape(2, -1, block.shape[0])
    came = swap(block, "side")
    layer = jnp.stack([pick(side == 0, block, came), pick(side == 0, came, block)])
    came = swap(layer, "core")
    return jnp.stack([pick(core == 0, layer, came), pick(core == 0, came, layer)])


def per_device(
    frames, out_grad, norm_gain, norm_bias, w_qkv, w_out, w_up, w_down, proj_bias, up_bias
):
    pairs = lax.axis_size("pair")
    pair = lax.axis_index("pair")
    shards = lax.axis_size("side") * lax.axis_size("rest")
    micro, _, width = frames.shape
    clips = micro // 2
    head = width // HEADS
    part = width // shards

    joined = gather_weight(w_qkv[0], w_out[0], w_up[0])
    near, mine, second_down = start_downs(w_down[0])
    downs = [lambda: finish_down(near, mine), lambda: second_down]
    small = jnp.concatenate(
        [norm_gain.reshape(-1), norm_bias.reshape(-1), proj_bias.reshape(-1), up_bias.reshape(-1)]
    )
    small = gather_small(small).astype(F32)
    rows = jnp.swapaxes(small[:, :, : 8 * part].reshape(2, shards, 8, part), 1, 2)
    rows = rows.reshape(2, 8, width)
    ups = small[:, :, 8 * part :].reshape(2, 1, -1)
    x_start = swap_in(frames)
    layers = []
    for layer in range(2):
        r = rows[layer]
        b_qkv = jnp.concatenate([r[4:5], jnp.zeros_like(r[4:5]), r[5:6]], axis=1)
        layers.append(
            (joined[layer], downs[layer], r[0:2], r[2:4], b_qkv, r[6:7], r[7:8], ups[layer])
        )

    x = x_start if near is None else copy_after(x_start, (near,))
    for phase in range(pairs):
        if phase > 0:
            came = lax.ppermute(second, "pair", [(i, i + 1) for i in range(pairs - 1)])
            x = pick(pair == 0, x_start, came)
        keep = phase == pairs - 1
        first, kept_first, layers[0] = forward_layer(x, layers[0], clips, head, keep)
        second, kept_second, layers[1] = forward_layer(first, layers[1], clips, head, keep)
    hidden = finish_out(*start_out(first, second), micro)

    g_start = swap_in(out_grad)
    g = g_start
    for phase in range(pairs - 1):
        d_second = backward_lean(kept_second, g, layers[1], clips, head, hidden)
        d_first = backward_lean(kept_first, d_second, layers[0], clips, head)
        came = lax.ppermute(d_first, "pair", [(i + 1, i) for i in range(pairs - 1)])
        g = pick(pair == pairs - 1, g_start, came)
    placed, (rest, up, down) = backward_all(
        kept_first, kept_second, g, layers, clips, head, shards
    )
    input_grads = finish_out(*placed, micro)

    own_rows = part // 2
    rest = rest.reshape(2, -1, 3 * width)
    out_rows = own_rows // 3
    qkv = rest[:, :own_rows].reshape(-1, 3 * width)
    out = rest[:, rest.shape[1] - out_rows :].reshape(-1, width)
    packed = rest[:, own_rows : rest.shape[1] - out_rows].astype(F32)
    packed = packed.reshape(2, -1)[:, : (8 * part + up_bias.shape[1]) // 2].reshape(-1)
    heads = packed[: 8 * part].reshape(8, part)
    return (
        hidden[None],
        input_grads[None],
        heads[0:2][None],
        heads[2:4][None],
        qkv.astype(F32)[None],
        out.astype(F32)[None],
        up.astype(F32)[None],
        down.astype(F32)[None],
        heads[4:8][None],
        packed[8 * part :][None],
    )


def solution(mesh):
    sections, groups, shards = (mesh.shape[name] for name in ("section", "seq", "shard"))
    cut = Mesh(
        mesh.devices.reshape(sections // 2, 2, 2, groups // 2, 2, shards // 2),
        AXES,
    )
    section, seq, shard = ("pair", "core"), ("half", "quad"), ("side", "rest")
    rows = seq + shard
    return jax.shard_map(
        per_device,
        mesh=cut,
        in_specs=(
            P(None, rows, None),
            P(None, rows, None),
            P(section, None, shard),
            P(section, None, shard),
            P(section, shard, None),
            P(section, shard, None),
            P(section, shard, None),
            P(section, shard, None),
            P(section, None, shard),
            P(section, shard),
        ),
        out_specs=(
            P(section, None, rows, None),
            P(section, None, rows, None),
            P(section, None, shard),
            P(section, None, shard),
            P(section, shard, None),
            P(section, shard, None),
            P(section, shard, None),
            P(section, shard, None),
            P(section, None, shard),
            P(section, shard),
        ),
        check_vma=False,
    )
```

```python
import math

import jax
import jax.numpy as jnp
from jax import lax
from jax.experimental import pallas as pl
from jax.experimental.pallas import tpu as pltpu
from jax.sharding import Mesh
from jax.sharding import PartitionSpec as P

HEADS = 12
norm_eps = 1e-05
F32 = jnp.float32
BF16 = jnp.bfloat16
VMEM_LIMIT = 56 * 1024 * 1024
AXES = ("pair", "core", "half", "quad", "side", "rest")
HEAD_GROUPS = 4
INWARD, ACROSS, OUTWARD = [(0, 1), (3, 2)], [(1, 2), (2, 1)], [(1, 0), (2, 3)]
ROW_BLOCKS = (272, 256, 192, 128, 96, 80, 64, 48)


def call(body, out_shapes, grid=None, in_specs=None, out_specs=None, scratch=(), flops=0, moved=0):
    extra = {} if grid is None else dict(grid=grid, in_specs=in_specs, out_specs=out_specs)
    return pl.pallas_call(
        body,
        out_shape=out_shapes,
        scratch_shapes=scratch,
        compiler_params=pltpu.CompilerParams(vmem_limit_bytes=VMEM_LIMIT),
        cost_estimate=pl.CostEstimate(flops=flops, bytes_accessed=moved, transcendentals=0),
        **extra,
    )


def dot(left, right):
    return jnp.dot(left, right, preferred_element_type=F32)


def dot_t(left, right):
    return lax.dot_general(left, right, (((1,), (1,)), ((), ())), preferred_element_type=F32)


def t_dot(left, right):
    return lax.dot_general(left, right, (((0,), (0,)), ((), ())), preferred_element_type=F32)


def norm_parts(values):
    center = values - jnp.mean(values, axis=-1, keepdims=True)
    inverse = lax.rsqrt(jnp.mean(center * center, axis=-1, keepdims=True) + norm_eps)
    return center * inverse, inverse


def norm_back(upstream, scaled, inverse, gain_row):
    weighted = upstream * gain_row
    return inverse * (
        weighted
        - jnp.mean(weighted, axis=-1, keepdims=True)
        - scaled * jnp.mean(weighted * scaled, axis=-1, keepdims=True)
    )


def qkv_body(x_ref, gain_ref, shift_ref, w_ref, bias_ref, out_ref, normed_ref):
    scaled, _ = norm_parts(x_ref[...].astype(F32))
    normed = (scaled * gain_ref[...] + shift_ref[...]).astype(BF16)
    normed_ref[...] = normed
    span = out_ref.shape[2] // 3
    width = x_ref.shape[1]
    for part in range(3):
        cols = slice(part * width, (part + 1) * width)
        piece = (dot(normed, w_ref[:, cols]) + bias_ref[:, cols]).astype(BF16)
        for g in range(HEAD_GROUPS):
            out_ref[g, :, part * span : (part + 1) * span] = piece[:, g * span : (g + 1) * span]


def qkv_forward(x, gain, shift, joined, bias):
    rows, width = x.shape
    span = width // HEAD_GROUPS
    return call(
        qkv_body,
        (
            jax.ShapeDtypeStruct((HEAD_GROUPS, rows, 3 * span), BF16),
            jax.ShapeDtypeStruct((rows, width), BF16),
        ),
        grid=(1,),
        in_specs=[
            whole((rows, width)),
            whole((1, width)),
            whole((1, width)),
            whole((width, 3 * width)),
            whole((1, 3 * width)),
        ],
        out_specs=(whole((HEAD_GROUPS, rows, 3 * span)), whole((rows, width))),
        flops=2 * rows * width * 3 * width,
        moved=6 * width * width + 10 * x.size,
    )(x, gain, shift, joined, bias)


def key_chunks(own_ref, other_ref):
    place = 0
    for ref in (own_ref, other_ref):
        total = ref.shape[1]
        step = 256 if total % 256 == 0 else total
        for start in range(0, total, step):
            yield ref, start, place, step
            place += step


def attend_body(q_ref, own_ref, other_ref, out_ref, log_ref, score_ref, *, head):
    span = q_ref.shape[2] // 3
    queries = q_ref.shape[1]
    scale = 1.0 / math.sqrt(head)
    for h in range(span // head):
        q = q_ref[0, :, h * head : (h + 1) * head] * scale
        top = jnp.full((1, queries), -jnp.inf, F32)
        for ref, start, place, step in key_chunks(own_ref, other_ref):
            k = ref[0, start : start + step, span + h * head : span + (h + 1) * head]
            scores = dot_t(k, q)
            score_ref[place : place + step, :] = scores
            top = jnp.maximum(top, jnp.max(scores, axis=0, keepdims=True))
        total = jnp.zeros((1, queries), F32)
        acc = jnp.zeros((head, queries), F32)
        for ref, start, place, step in key_chunks(own_ref, other_ref):
            v = ref[0, start : start + step, 2 * span + h * head : 2 * span + (h + 1) * head]
            e = jnp.exp(score_ref[place : place + step, :] - top)
            total = total + jnp.sum(e, axis=0, keepdims=True)
            acc = acc + t_dot(v, e.astype(BF16))
        out_ref[0, :, h * head : (h + 1) * head] = jnp.transpose(acc / total).astype(BF16)
        log_ref[0, h : h + 1, :] = top + jnp.log(total)


def query_block(queries):
    return 256 if queries % 256 == 0 else queries


def attend_forward(own, other, head):
    clips, queries, wide = own.shape
    span = wide // 3
    keys = queries + other.shape[1]
    block = query_block(queries)

    def body(*refs):
        attend_body(*refs, head=head)

    return call(
        body,
        (
            jax.ShapeDtypeStruct((clips, queries, span), BF16),
            jax.ShapeDtypeStruct((clips, span // head, queries), F32),
        ),
        grid=(clips, queries // block),
        in_specs=[
            pl.BlockSpec((1, block, wide), lambda m, i: (m, i, 0)),
            pl.BlockSpec((1, queries, wide), lambda m, i: (m, 0, 0)),
            pl.BlockSpec((1, other.shape[1], wide), lambda m, i: (m, 0, 0)),
        ],
        out_specs=(
            pl.BlockSpec((1, block, span), lambda m, i: (m, i, 0)),
            pl.BlockSpec((1, span // head, block), lambda m, i: (m, 0, i)),
        ),
        scratch=[pltpu.VMEM((keys, block), F32)],
        flops=16 * clips * queries * keys * span,
        moved=4 * (own.size + other.size),
    )(own, own, other)


def attend_back_body(
    q_ref,
    own_ref,
    other_ref,
    grad_ref,
    log_ref,
    dq_ref,
    dkv_own_ref,
    dkv_other_ref,
    p_ref,
    dp_ref,
    dk_acc,
    dv_acc,
    *,
    head,
):
    span = q_ref.shape[2] // 3
    queries = q_ref.shape[1]
    heads = span // head
    scale = 1.0 / math.sqrt(head)

    @pl.when(pl.program_id(1) == 0)
    def _():
        dk_acc[...] = jnp.zeros_like(dk_acc)
        dv_acc[...] = jnp.zeros_like(dv_acc)

    for h in range(heads):
        q = q_ref[0, :, h * head : (h + 1) * head] * scale
        d_out = grad_ref[0, :, h * head : (h + 1) * head]
        log_total = log_ref[0, h : h + 1, :]
        row_term = jnp.zeros((1, queries), F32)
        for ref, start, place, step in key_chunks(own_ref, other_ref):
            k = ref[0, start : start + step, span + h * head : span + (h + 1) * head]
            v = ref[0, start : start + step, 2 * span + h * head : 2 * span + (h + 1) * head]
            probs = jnp.exp(dot_t(k, q) - log_total)
            d_probs = dot_t(v, d_out)
            p_ref[place : place + step, :] = probs
            dp_ref[place : place + step, :] = d_probs
            row_term = row_term + jnp.sum(probs * d_probs, axis=0, keepdims=True)
            dv_acc[h, place : place + step, :] += dot(probs.astype(BF16), d_out)
        dq = jnp.zeros((head, queries), F32)
        for ref, start, place, step in key_chunks(own_ref, other_ref):
            k = ref[0, start : start + step, span + h * head : span + (h + 1) * head]
            d_scores = (
                p_ref[place : place + step, :] * (dp_ref[place : place + step, :] - row_term)
            ).astype(BF16)
            dk_acc[h, place : place + step, :] += dot(d_scores, q)
            dq = dq + t_dot(k, d_scores)
        dq_ref[0, :, h * head : (h + 1) * head] = jnp.transpose(dq * scale).astype(BF16)

    @pl.when(pl.program_id(1) == pl.num_programs(1) - 1)
    def _():
        place = 0
        for ref in (dkv_own_ref, dkv_other_ref):
            rows = ref.shape[1]
            for h in range(heads):
                ref[0, :, h * head : (h + 1) * head] = dk_acc[h, place : place + rows, :].astype(
                    ref.dtype
                )
                ref[0, :, span + h * head : span + (h + 1) * head] = dv_acc[
                    h, place : place + rows, :
                ].astype(ref.dtype)
            place += rows


def attend_backward(own, other, grad, log_total, head, after=()):
    clips, queries, wide = own.shape
    span = wide // 3
    others = other.shape[1]
    keys = queries + others
    block = query_block(queries)
    heads = span // head

    def body(*refs):
        attend_back_body(*refs[:5], *refs[5 + len(after) :], head=head)

    return call(
        body,
        (
            jax.ShapeDtypeStruct((clips, queries, span), BF16),
            jax.ShapeDtypeStruct((clips, queries, 2 * span), F32),
            jax.ShapeDtypeStruct((clips, others, 2 * span), BF16),
        ),
        grid=(clips, queries // block),
        in_specs=[
            pl.BlockSpec((1, block, wide), lambda m, i: (m, i, 0)),
            pl.BlockSpec((1, queries, wide), lambda m, i: (m, 0, 0)),
            pl.BlockSpec((1, others, wide), lambda m, i: (m, 0, 0)),
            pl.BlockSpec((1, block, span), lambda m, i: (m, i, 0)),
            pl.BlockSpec((1, heads, block), lambda m, i: (m, 0, i)),
        ]
        + [pl.BlockSpec(memory_space=pl.ANY)] * len(after),
        out_specs=(
            pl.BlockSpec((1, block, span), lambda m, i: (m, i, 0)),
            pl.BlockSpec((1, queries, 2 * span), lambda m, i: (m, 0, 0)),
            pl.BlockSpec((1, others, 2 * span), lambda m, i: (m, 0, 0)),
        ),
        scratch=[
            pltpu.VMEM((keys, block), F32),
            pltpu.VMEM((keys, block), F32),
            pltpu.VMEM((heads, keys, head), F32),
            pltpu.VMEM((heads, keys, head), F32),
        ],
        flops=40 * clips * queries * keys * span,
        moved=8 * (own.size + other.size),
    )(own, own, other, grad, log_total, *after)


def feed_body(
    x_ref,
    att_ref,
    w_out_ref,
    b_out_ref,
    gain_ref,
    shift_ref,
    w_up_ref,
    b_up_ref,
    w_down_ref,
    b_down_ref,
    y_ref,
    *rest,
):
    if len(rest) > 2:
        x1_ref, normed_ref, slope_ref, lifted_ref, flat_ref, acc = rest
    else:
        normed_ref, acc = rest
    span = att_ref.shape[2]

    @pl.when(pl.program_id(0) == 0)
    def _():
        middle = x_ref[...].astype(F32) + b_out_ref[...]
        for g in range(HEAD_GROUPS):
            middle = middle + dot(att_ref[g], w_out_ref[g * span : (g + 1) * span, :])
            if len(rest) > 2:
                flat_ref[:, g * span : (g + 1) * span] = att_ref[g]
        if len(rest) > 2:
            x1_ref[...] = middle
        scaled, _ = norm_parts(middle)
        normed_ref[...] = (scaled * gain_ref[...] + shift_ref[...]).astype(BF16)
        acc[...] = middle + b_down_ref[...]

    upper = dot(normed_ref[...], w_up_ref[...]) + b_up_ref[...]
    phi = 0.5 * (1.0 + lax.erf(upper * math.sqrt(0.5)))
    lifted = (upper * phi).astype(BF16)
    if len(rest) > 2:
        density = jnp.exp(-0.5 * upper * upper) * (1.0 / math.sqrt(2.0 * math.pi))
        slope_ref[...] = phi + upper * density
        lifted_ref[...] = lifted
    acc[...] += dot(lifted, w_down_ref[...])

    @pl.when(pl.program_id(0) == pl.num_programs(0) - 1)
    def _():
        y_ref[...] = acc[...].astype(BF16)


def whole(shape):
    return pl.BlockSpec(shape, lambda i: (0,) * len(shape))


def feed_forward(x, att, joined, b_out, gain, shift, b_up, w_down, b_down, keep):
    rows, width = x.shape
    hidden = w_down.shape[0]
    row = whole((1, width))
    full = whole((rows, width))
    part = pl.BlockSpec((rows, width), lambda i: (0, i))
    shapes = [jax.ShapeDtypeStruct((rows, width), BF16)]
    specs = [full]
    scratch = [pltpu.VMEM((rows, width), F32)]
    if keep:
        shapes += [
            jax.ShapeDtypeStruct((rows, width), F32),
            jax.ShapeDtypeStruct((rows, width), BF16),
            jax.ShapeDtypeStruct((rows, hidden), F32),
            jax.ShapeDtypeStruct((rows, hidden), BF16),
            jax.ShapeDtypeStruct((rows, width), BF16),
        ]
        specs += [full, full, part, part, full]
    else:
        scratch = [pltpu.VMEM((rows, width), BF16)] + scratch
    return call(
        feed_body,
        tuple(shapes),
        grid=(hidden // width,),
        in_specs=[
            full,
            whole(att.shape),
            pl.BlockSpec((width, width), lambda i: (0, 3)),
            row,
            row,
            row,
            pl.BlockSpec((width, width), lambda i: (0, 4 + i)),
            pl.BlockSpec((1, width), lambda i: (0, i)),
            pl.BlockSpec((width, width), lambda i: (i, 0)),
            row,
        ],
        out_specs=tuple(specs),
        scratch=scratch,
        flops=2 * rows * width * (2 * hidden + width),
        moved=4 * w_down.size + 2 * width * width + 10 * rows * hidden,
    )(x, att, joined, b_out, gain, shift, joined, b_up, w_down, b_down)


def feed_back_body(
    g_ref,
    slope_ref,
    w_down_ref,
    w_up_ref,
    w_out_ref,
    x1_ref,
    gain_ref,
    d_upper_ref,
    dx1_ref,
    branch_ref,
    datt_ref,
    sums_ref,
    up_sum_ref,
    acc,
):
    @pl.when(pl.program_id(0) == 0)
    def _():
        acc[...] = jnp.zeros_like(acc)

    d_upper = (dot_t(g_ref[...], w_down_ref[...]) * slope_ref[...]).astype(BF16)
    d_upper_ref[...] = d_upper
    up_sum_ref[...] = jnp.sum(d_upper.astype(F32), axis=0, keepdims=True)
    acc[...] += dot_t(d_upper, w_up_ref[...])

    @pl.when(pl.program_id(0) == pl.num_programs(0) - 1)
    def _():
        d_normed = acc[...]
        upstream = g_ref[...].astype(F32)
        scaled, inverse = norm_parts(x1_ref[...])
        d_middle = upstream + norm_back(d_normed, scaled, inverse, gain_ref[...])
        dx1_ref[...] = d_middle
        branch = d_middle.astype(BF16)
        branch_ref[...] = branch
        span = datt_ref.shape[2]
        for g in range(HEAD_GROUPS):
            datt_ref[g] = dot_t(branch, w_out_ref[g * span : (g + 1) * span, :]).astype(BF16)
        sums_ref[0:1, :] = jnp.sum(d_normed * scaled, axis=0, keepdims=True)
        sums_ref[1:2, :] = jnp.sum(d_normed, axis=0, keepdims=True)
        sums_ref[2:3, :] = jnp.sum(branch.astype(F32), axis=0, keepdims=True)
        sums_ref[3:4, :] = jnp.sum(upstream, axis=0, keepdims=True)


def feed_backward(g, slope, w_down, joined, x1, gain):
    rows, width = g.shape
    hidden = w_down.shape[0]
    chunk = width
    full = whole((rows, width))
    return call(
        feed_back_body,
        (
            jax.ShapeDtypeStruct((rows, hidden), BF16),
            jax.ShapeDtypeStruct((rows, width), F32),
            jax.ShapeDtypeStruct((rows, width), BF16),
            jax.ShapeDtypeStruct((HEAD_GROUPS, rows, width // HEAD_GROUPS), BF16),
            jax.ShapeDtypeStruct((4, width), F32),
            jax.ShapeDtypeStruct((1, hidden), F32),
        ),
        grid=(hidden // chunk,),
        in_specs=[
            full,
            pl.BlockSpec((rows, chunk), lambda i: (0, i)),
            pl.BlockSpec((chunk, width), lambda i: (i, 0)),
            pl.BlockSpec((width, chunk), lambda i: (0, 4 + i)),
            pl.BlockSpec((width, width), lambda i: (0, 3)),
            full,
            whole((1, width)),
        ],
        out_specs=(
            pl.BlockSpec((rows, chunk), lambda i: (0, i)),
            full,
            full,
            whole((HEAD_GROUPS, rows, width // HEAD_GROUPS)),
            whole((4, width)),
            pl.BlockSpec((1, chunk), lambda i: (0, i)),
        ),
        scratch=[pltpu.VMEM((rows, width), F32)],
        flops=2 * rows * width * (2 * hidden + width),
        moved=4 * w_down.size + 2 * width * width + 6 * rows * hidden,
    )(g, slope, w_down, joined, joined, x1, gain)


def qkv_back_body(grads_ref, w_ref, x_ref, dx1_ref, gain_ref, dx_ref, flat_ref, sums_ref):
    width = x_ref.shape[1]
    span = grads_ref.shape[2] // 3
    for g in range(HEAD_GROUPS):
        for part in range(3):
            flat_ref[:, part * width + g * span : part * width + (g + 1) * span] = grads_ref[
                g, :, part * span : (part + 1) * span
            ]
    d_normed = dot_t(flat_ref[...], w_ref[...])
    scaled, inverse = norm_parts(x_ref[...].astype(F32))
    dx = dx1_ref[...] + norm_back(d_normed, scaled, inverse, gain_ref[...])
    dx_ref[...] = dx.astype(BF16)
    sums_ref[0:1, :] = jnp.sum(d_normed * scaled, axis=0, keepdims=True)
    sums_ref[1:2, :] = jnp.sum(d_normed, axis=0, keepdims=True)
    sums_ref[2:3, :] = jnp.sum(flat_ref[:, :width].astype(F32), axis=0, keepdims=True)
    sums_ref[3:4, :] = jnp.sum(flat_ref[:, 2 * width :].astype(F32), axis=0, keepdims=True)


def qkv_backward(grads, joined, x, dx1, gain, after=()):
    rows, width = x.shape

    def body(*refs):
        qkv_back_body(*refs[:5], *refs[5 + len(after) :])

    return call(
        body,
        (
            jax.ShapeDtypeStruct((rows, width), BF16),
            jax.ShapeDtypeStruct((rows, 3 * width), BF16),
            jax.ShapeDtypeStruct((4, width), F32),
        ),
        grid=(1,),
        in_specs=[
            whole(grads.shape),
            whole((width, 3 * width)),
            whole((rows, width)),
            whole((rows, width)),
            whole((1, width)),
        ]
        + [pl.BlockSpec(memory_space=pl.ANY)] * len(after),
        out_specs=(whole((rows, width)), whole((rows, 3 * width)), whole((4, width))),
        flops=2 * rows * width * 3 * width,
        moved=6 * width * width + 20 * x.size,
    )(grads, joined, x, dx1, gain, *after)


def add_body(one_ref, two_ref, *rest):
    rest[-1][...] = (one_ref[...].astype(F32) + two_ref[...].astype(F32)).astype(BF16)


def add_after(one, two, after):
    rows, wide = one.shape
    block = next((n for n in ROW_BLOCKS if rows % n == 0), rows)
    spec = pl.BlockSpec((block, wide), lambda i: (i, 0))
    return call(
        add_body,
        jax.ShapeDtypeStruct((rows, wide), BF16),
        grid=(rows // block,),
        in_specs=[spec, spec] + [pl.BlockSpec(memory_space=pl.ANY)] * len(after),
        out_specs=spec,
        flops=one.size,
        moved=6 * one.size,
    )(one, two, *after)


def copy_body(one_ref, *rest):
    rest[-1][...] = one_ref[...]


def copy_after(one, after):
    spec = pl.BlockSpec(one.shape, lambda i: (0, 0))
    return call(
        copy_body,
        jax.ShapeDtypeStruct(one.shape, one.dtype),
        grid=(1,),
        in_specs=[spec] + [pl.BlockSpec(memory_space=pl.ANY)] * len(after),
        out_specs=spec,
        flops=one.size,
        moved=4 * one.size,
    )(one, *after)


def join_body(dq_ref, kept_ref, back_ref, *rest):
    out_ref = rest[-1]
    span = dq_ref.shape[2]
    out_ref[:, :, :span] = dq_ref[...]
    out_ref[:, :, span:] = (kept_ref[...] + back_ref[...].astype(F32)).astype(BF16)


def join_grads(dq, kept, back, after):
    clips, rows, span = dq.shape

    def spec(wide):
        return pl.BlockSpec((1, rows, wide), lambda i: (i, 0, 0))

    return call(
        join_body,
        jax.ShapeDtypeStruct((clips, rows, 3 * span), BF16),
        grid=(clips,),
        in_specs=[spec(span), spec(2 * span), spec(2 * span)]
        + [pl.BlockSpec(memory_space=pl.ANY)] * len(after),
        out_specs=spec(3 * span),
        flops=kept.size,
        moved=8 * kept.size,
    )(dq, kept, back, *after)


def swap(block, axis):
    return lax.ppermute(block, axis, [(0, 1), (1, 0)])


def shift(block, distance):
    count = lax.axis_size("rest")
    return lax.ppermute(block, "rest", [(i, (i + distance) % count) for i in range(count)])


def spread(block):
    return lax.all_to_all(block, ("quad", "side"), 0, 0, tiled=True)


def to_clips(block, clips):
    groups, rows, wide = block.shape
    if clips == 1:
        return block.reshape(1, groups * rows, wide)
    block = block.reshape(groups, clips, rows // clips, wide)
    return jnp.swapaxes(block, 0, 1).reshape(clips, groups * (rows // clips), wide)


def to_tokens(block):
    clips, rows, wide = block.shape
    if clips == 1:
        return block.reshape(HEAD_GROUPS, rows // HEAD_GROUPS, wide)
    block = block.reshape(clips, HEAD_GROUPS, rows // HEAD_GROUPS, wide)
    return jnp.swapaxes(block, 0, 1).reshape(HEAD_GROUPS, -1, wide)


def other_keys(grouped, own, clips):
    if lax.axis_size("rest") == 1:
        return to_clips(swap(grouped, "core"), clips)
    near = [shift(own, k) for k in range(1, lax.axis_size("rest"))]
    far = swap(jnp.concatenate([own] + near, axis=1), "core")
    return jnp.concatenate(near + [far], axis=1)


def return_keys(kept, sent):
    queries = kept.shape[1]
    count = lax.axis_size("rest")
    near = (count - 1) * queries
    back = swap(sent[:, near:], "core")
    total = kept
    for k in range(1, count):
        part = sent[:, (k - 1) * queries : k * queries].astype(F32)
        part = part + back[:, k * queries : (k + 1) * queries].astype(F32)
        total = total + shift(part.astype(BF16), -k).astype(F32)
    return total, back[:, :queries]


def pick(flag, one, two):
    return jnp.where(flag, one, two)


def gather_weight(*blocks):
    core = lax.axis_index("core")
    quads = lax.axis_size("quad")
    part = blocks[0].shape[0] // (2 * quads)
    quad = lax.axis_index("quad")

    def cut(which):
        start = (which * quads + quad) * part
        return jnp.concatenate(
            [lax.dynamic_slice_in_dim(block, start, part, 0) for block in blocks], axis=1
        )

    own = cut(core)
    came = swap(cut(1 - core), "core")
    first = pick(core == 0, own, came)
    second = pick(core == 0, came, own)
    return [
        lax.all_gather(item, ("side", "rest", "core", "quad"), axis=0, tiled=True)
        for item in (first, second)
    ]


def in_order(second, mine, other):
    return pick(second, other, mine), pick(second, mine, other)


def start_downs(block):
    if lax.axis_size("rest") > 1 or lax.axis_size("quad") != 2:
        first, second = gather_weight(block)
        return None, first, second
    core, quad = lax.axis_index("core"), lax.axis_index("quad")
    part = block.shape[0] // 4
    mine, other = in_order(core == 1, block, swap(block, "core"))
    line = lax.dynamic_slice_in_dim(other, (core * 2 + quad) * part, part, 0)
    second = lax.all_gather(line, ("side", "rest", "core", "quad"), axis=0, tiled=True)
    near = lax.dynamic_slice_in_dim(mine, core * 2 * part, 2 * part, 0)
    return swap(near, "side"), mine, second


def finish_down(near, mine):
    if near is None:
        return mine
    core, side = lax.axis_index("core"), lax.axis_index("side")
    other = jnp.concatenate(in_order(core == 1, near, swap(near, "core")), axis=0)
    return jnp.concatenate(in_order(side == 1, mine, other), axis=0)


def add(one, two):
    return (one.astype(F32) + two.astype(F32)).astype(one.dtype)


def cut_columns(left, which):
    shards = lax.axis_size("side") * lax.axis_size("rest")
    part = left.shape[1] // (2 * shards)
    return jnp.concatenate(
        [
            lax.dynamic_slice_in_dim(left, (2 * s + which) * part, part, 1)
            for s in range(shards)
        ],
        axis=1,
    )


def weight_halves(left, right):
    core = lax.axis_index("core")
    return [
        t_dot(cut_columns(left, which), right).astype(BF16) for which in (1 - core, core)
    ]


def parts_body(side_ref, *refs):
    far_one, far_two, near_one, near_two = refs[:4]
    sent_ref, kept_ref = refs[-2:]
    sent_ref[...] = (far_one[...].astype(F32) + far_two[...].astype(F32)).astype(BF16)
    kept_ref[...] = (near_one[...].astype(F32) + near_two[...].astype(F32)).astype(BF16)


def side_parts(sent, kept, *after):
    came = swap(sent, "core")
    rows, wide = kept.shape
    half = rows // 2
    block = next((n for n in ROW_BLOCKS if half % n == 0), half)
    steps = half // block
    far = pl.BlockSpec((block, wide), lambda i, side: ((1 - side[0]) * steps + i, 0))
    near = pl.BlockSpec((block, wide), lambda i, side: (side[0] * steps + i, 0))
    out = pl.BlockSpec((block, wide), lambda i, side: (i, 0))
    return pl.pallas_call(
        parts_body,
        out_shape=(jax.ShapeDtypeStruct((half, wide), BF16),) * 2,
        grid_spec=pltpu.PrefetchScalarGridSpec(
            num_scalar_prefetch=1,
            grid=(steps,),
            in_specs=[far, far, near, near]
            + [pl.BlockSpec(memory_space=pl.ANY)] * len(after),
            out_specs=(out, out),
        ),
        compiler_params=pltpu.CompilerParams(vmem_limit_bytes=VMEM_LIMIT),
        cost_estimate=pl.CostEstimate(
            flops=kept.size, bytes_accessed=6 * kept.size, transcendentals=0
        ),
    )(lax.axis_index("side").astype(jnp.int32).reshape(1), kept, came, kept, came, *after)


def side_sum(sent, kept, *after):
    total = add_after(kept, swap(sent, "side"), after)
    if lax.axis_size("rest") > 1:
        total = lax.psum_scatter(total, "rest", scatter_dimension=0, tiled=True)
    return total


def line_sum(*items):
    return lax.psum(items, ("half", "quad"))


def line_hop(block, pairs):
    return lax.ppermute(block, ("half", "quad"), pairs)


def line_sums(begun, sides, ties):
    inner = lax.axis_index("half") != lax.axis_index("quad")
    count = len(begun) + len(sides)
    totals, mark = [*begun, *sides], ()
    results = []
    for turn in range(2, count + 2):
        mark = (*mark, *ties.get(turn, ()))
        if turn < count:
            totals[turn] = totals[turn](*mark)
            mark = (totals[turn],)
        for hops, at in ((INWARD, turn - 1), (ACROSS, turn - 2)):
            if 0 <= at < count:
                if hops is ACROSS:
                    mark = (*mark, *results[-1:])
                totals[at] = add_after(totals[at], line_hop(totals[at], hops), mark)
                mark = (totals[at],)
                if hops is ACROSS:
                    results.append(pick(inner, totals[at], line_hop(totals[at], OUTWARD)))
    return results


def join_cores(first, second):
    core = lax.axis_index("core")
    came = swap(pick(core == 0, second, first), "core")
    mine = pick(core == 0, first, second)
    return jnp.concatenate([pick(core == 0, mine, came), pick(core == 0, came, mine)], axis=0)


def swap_in(block):
    core, half = lax.axis_index("core"), lax.axis_index("half")
    micro, rows, wide = block.shape
    block = block.reshape(2, (micro // 2) * rows, wide)
    own = lax.dynamic_index_in_dim(block, half, 0, keepdims=False)
    other = lax.dynamic_index_in_dim(block, 1 - half, 0, keepdims=False)
    came = lax.ppermute(other, ("core", "half"), [(1, 2), (2, 1)])
    return pick(core == half, own, came)


def start_out(first, second):
    second_core, second_half = lax.axis_index("core") == 1, lax.axis_index("half") == 1
    mine, sent = in_order(second_core, first, second)
    parts = in_order(second_core, mine, swap(sent, "core"))
    mine, sent = in_order(second_half, *parts)
    return mine, swap(sent, "half")


def finish_out(mine, came, micro):
    rows, wide = mine.shape
    clips = in_order(lax.axis_index("half") == 1, mine, came)
    return jnp.stack(clips).reshape(micro, 2 * rows // micro, wide)


def forward_layer(x, weights, clips, head, keep):
    joined, w_down, gains, shifts, b_qkv, b_out, b_down, b_up = weights
    grouped, normed_one = qkv_forward(x, gains[0:1], shifts[0:1], joined, b_qkv)
    grouped = spread(grouped)
    own = to_clips(grouped, clips)
    other = other_keys(grouped, own, clips)
    att, log_total = attend_forward(own, other, head)
    if callable(w_down):
        w_down = w_down()
        weights = (joined, w_down, *weights[2:])
    att = spread(to_tokens(att))
    y, *kept = feed_forward(
        x, att, joined, b_out, gains[1:2], shifts[1:2], b_up, w_down, b_down, keep
    )
    return y, (x, normed_one, own, other, log_total, *kept), weights


def attention_grads(kept, d_att, clips, head, after):
    return heads_back(kept, to_clips(spread(d_att), clips), head, after)


def heads_back(kept, d_heads, head, after):
    own, other, log_total = kept[2:5]
    dq, kept_kv, sent_kv = attend_backward(own, other, d_heads, log_total, head, after)
    return (dq, *return_keys(kept_kv, sent_kv))


def spread_grads(grads, after=()):
    return spread(to_tokens(join_grads(*grads, after)))


def backward_lean(kept, g, weights, clips, head, *after):
    x, _, _, _, _, x1, _, slope, _, _ = kept
    joined, w_down, gains = weights[:3]
    _, dx1, _, d_att, _, _ = feed_backward(g, slope, w_down, joined, x1, gains[1:2])
    d_tokens = spread_grads(attention_grads(kept, d_att, clips, head, after))
    return qkv_backward(d_tokens, joined, x, dx1, gains[0:1])[0]


def small_rows(sums_one, sums_two, up_sum, shards, wide):
    rows = jnp.concatenate(
        [
            sums_one[0:1],
            sums_two[0:1],
            sums_one[1:2],
            sums_two[1:2],
            sums_one[2:4],
            sums_two[2:4],
        ]
    )
    rows = jnp.swapaxes(rows.reshape(8, shards, -1), 0, 1).reshape(shards, -1)
    packed = jnp.concatenate([rows, up_sum.reshape(shards, -1)], axis=1).astype(BF16)
    packed = packed.reshape(shards, 2, -1)
    lines = -(-packed.shape[2] // wide)
    room = 16 * (-(-lines // 16)) * wide
    packed = jnp.pad(packed, ((0, 0), (0, 0), (0, room - packed.shape[2])))
    return packed.reshape(shards, 2, -1, wide)


def beside(weight, *rows):
    shards, _, wide = rows[0].shape
    return jnp.concatenate([weight.reshape(shards, -1, wide), *rows], axis=1).reshape(-1, wide)


def rest_halves(normed_one, flat, out, sums_one, sums_two, up_sum, shards):
    core = lax.axis_index("core")
    wide = flat.shape[1]
    rows = small_rows(sums_one, sums_two, up_sum, shards, wide)
    return [
        beside(
            item,
            lax.dynamic_index_in_dim(rows, which, 1, keepdims=False),
            outs.reshape(shards, -1, wide),
        )
        for item, outs, which in zip(weight_halves(normed_one, flat), out, (1 - core, core))
    ]


def backward_all(kept_first, kept_second, g, layers, clips, head, shards):
    x, normed_one, _, _, _, x1, normed_two, slope, lifted, att = kept_second
    joined, w_down, gains = layers[1][:3]
    d_upper, dx1, branch, d_att, sums_two, up_sum = feed_backward(
        g, slope, w_down, joined, x1, gains[1:2]
    )
    down = weight_halves(lifted, g)
    up = weight_halves(normed_two, d_upper)
    grads = attention_grads(kept_second, d_att, clips, head, (*down, *up))
    d_tokens = spread_grads(grads)
    out = weight_halves(att, branch)
    down = side_parts(*down, d_tokens)
    d_second, flat, sums_one = qkv_backward(
        d_tokens, joined, x, dx1, gains[0:1], (*down, *out)
    )
    rest = rest_halves(normed_one, flat, out, sums_one, sums_two, up_sum, shards)

    x, normed_one, _, _, _, x1, normed_two, slope, lifted, att = kept_first
    joined, w_down, gains = layers[0][:3]
    d_upper, dx1, branch, d_att, sums_two, up_sum = feed_backward(
        d_second, slope, w_down, joined, x1, gains[1:2]
    )
    down_one = weight_halves(lifted, d_second)
    up_one = weight_halves(normed_two, d_upper)
    d_heads = to_clips(spread(d_att), clips)
    up = side_parts(*up, d_heads)
    down_two = side_sum(*down)
    grads = heads_back(
        kept_first, d_heads, head, (down_two, *up, *rest, *down_one, *up_one)
    )
    rest = side_parts(*rest, grads[0])
    up_two = side_sum(*up, grads[0])
    line = lax.axis_size("quad") == 2
    if line:
        down_two = add_after(down_two, line_hop(down_two, INWARD), (grads[0],))
    d_tokens = spread_grads(grads, (down_two, up_two, *rest))
    down_one, up_one = side_parts(*down_one), side_parts(*up_one)
    out_one = weight_halves(att, branch)
    d_first, flat, sums_one = qkv_backward(
        d_tokens, joined, x, dx1, gains[0:1], (*down_one, *up_one, *out_one)
    )
    placed = start_out(d_first, d_second)
    halves = rest_halves(normed_one, flat, out_one, sums_one, sums_two, up_sum, shards)
    rest_one = side_parts(*halves)
    blocks = (
        (rest, halves[0]),
        (down_one, rest_one[0]),
        (up_one, rest_one[0]),
        (rest_one, rest_one[0]),
    )
    sides = [
        lambda *after, item=item, mark=mark: side_sum(*item, *after, mark)
        for item, mark in blocks
    ]
    if line:
        sums = line_sums((down_two, up_two), sides, {2: placed[1:]})
    else:
        sums = line_sum(down_two, up_two, *(item() for item in sides))
    down_two, up_two, rest_two, down_one, up_one, rest_one = sums
    firsts = (rest_one, up_one, down_one)
    seconds = (rest_two, up_two, down_two)
    return placed, [join_cores(a, b) for a, b in zip(firsts, seconds)]


def gather_small(block):
    core, side = lax.axis_index("core"), lax.axis_index("side")
    if lax.axis_size("rest") > 1:
        whole_block = lax.all_gather(block, ("core", "side", "rest"), axis=0, tiled=False)
        return whole_block.reshape(2, -1, block.shape[0])
    came = swap(block, "side")
    layer = jnp.stack([pick(side == 0, block, came), pick(side == 0, came, block)])
    came = swap(layer, "core")
    return jnp.stack([pick(core == 0, layer, came), pick(core == 0, came, layer)])


def per_device(
    frames, out_grad, norm_gain, norm_bias, w_qkv, w_out, w_up, w_down, proj_bias, up_bias
):
    pairs = lax.axis_size("pair")
    pair = lax.axis_index("pair")
    shards = lax.axis_size("side") * lax.axis_size("rest")
    micro, _, width = frames.shape
    clips = micro // 2
    head = width // HEADS
    part = width // shards

    joined = gather_weight(w_qkv[0], w_out[0], w_up[0])
    near, mine, second_down = start_downs(w_down[0])
    downs = [lambda: finish_down(near, mine), lambda: second_down]
    small = jnp.concatenate(
        [norm_gain.reshape(-1), norm_bias.reshape(-1), proj_bias.reshape(-1), up_bias.reshape(-1)]
    )
    small = gather_small(small).astype(F32)
    rows = jnp.swapaxes(small[:, :, : 8 * part].reshape(2, shards, 8, part), 1, 2)
    rows = rows.reshape(2, 8, width)
    ups = small[:, :, 8 * part :].reshape(2, 1, -1)
    x_start = swap_in(frames)
    layers = []
    for layer in range(2):
        r = rows[layer]
        b_qkv = jnp.concatenate([r[4:5], jnp.zeros_like(r[4:5]), r[5:6]], axis=1)
        layers.append(
            (joined[layer], downs[layer], r[0:2], r[2:4], b_qkv, r[6:7], r[7:8], ups[layer])
        )

    x = x_start if near is None else copy_after(x_start, (near,))
    for phase in range(pairs):
        if phase > 0:
            came = lax.ppermute(second, "pair", [(i, i + 1) for i in range(pairs - 1)])
            x = pick(pair == 0, x_start, came)
        keep = phase == pairs - 1
        first, kept_first, layers[0] = forward_layer(x, layers[0], clips, head, keep)
        second, kept_second, layers[1] = forward_layer(first, layers[1], clips, head, keep)
    hidden = finish_out(*start_out(first, second), micro)

    g_start = swap_in(out_grad)
    g = g_start
    for phase in range(pairs - 1):
        d_second = backward_lean(kept_second, g, layers[1], clips, head, hidden)
        d_first = backward_lean(kept_first, d_second, layers[0], clips, head)
        came = lax.ppermute(d_first, "pair", [(i + 1, i) for i in range(pairs - 1)])
        g = pick(pair == pairs - 1, g_start, came)
    placed, (rest, up, down) = backward_all(
        kept_first, kept_second, g, layers, clips, head, shards
    )
    input_grads = finish_out(*placed, micro)

    own_rows = part // 2
    rest = rest.reshape(2, -1, 3 * width)
    out_rows = own_rows // 3
    qkv = rest[:, :own_rows].reshape(-1, 3 * width)
    out = rest[:, rest.shape[1] - out_rows :].reshape(-1, width)
    packed = rest[:, own_rows : rest.shape[1] - out_rows].astype(F32)
    packed = packed.reshape(2, -1)[:, : (8 * part + up_bias.shape[1]) // 2].reshape(-1)
    heads = packed[: 8 * part].reshape(8, part)
    return (
        hidden[None],
        input_grads[None],
        heads[0:2][None],
        heads[2:4][None],
        qkv.astype(F32)[None],
        out.astype(F32)[None],
        up.astype(F32)[None],
        down.astype(F32)[None],
        heads[4:8][None],
        packed[8 * part :][None],
    )


def solution(mesh):
    sections, groups, shards = (mesh.shape[name] for name in ("section", "seq", "shard"))
    cut = Mesh(
        mesh.devices.reshape(sections // 2, 2, 2, groups // 2, 2, shards // 2),
        AXES,
    )
    section, seq, shard = ("pair", "core"), ("half", "quad"), ("side", "rest")
    rows = seq + shard
    return jax.shard_map(
        per_device,
        mesh=cut,
        in_specs=(
            P(None, rows, None),
            P(None, rows, None),
            P(section, None, shard),
            P(section, None, shard),
            P(section, shard, None),
            P(section, shard, None),
            P(section, shard, None),
            P(section, shard, None),
            P(section, None, shard),
            P(section, shard),
        ),
        out_specs=(
            P(section, None, rows, None),
            P(section, None, rows, None),
            P(section, None, shard),
            P(section, None, shard),
            P(section, shard, None),
            P(section, shard, None),
            P(section, shard, None),
            P(section, shard, None),
            P(section, None, shard),
            P(section, shard),
        ),
        check_vma=False,
    )
```
